32 devices in a mesh: dp: 8 (over y, x, core), tensor: 4 (over z).
Axes of the slice: x: 2, y: 2, z: 4, core: 2. Of those that a mesh axis runs over, the one named last changes fastest.
Arguments:
- gen_tokens: bfloat16 [24, 5, 256, 512], P('dp', None, 'tensor'), may hold values from -6 to 6
- rec_grad: bfloat16 [24, 5, 256, 512], P('dp', None, 'tensor'), may hold values from -6 to 6
- adv_grad: bfloat16 [24, 5, 256, 512], P('dp', None, 'tensor'), may hold values from -6 to 6
- gen_aspect: int32 [24], P('dp'), may hold values from 0 to 2
- gen_frames: int32 [24], P('dp'), may hold values from 1 to 5, 90 in all
- disc_tokens: bfloat16 [24, 5, 256, 512], P('dp', None, 'tensor'), may hold values from -6 to 6
- disc_aspect: int32 [24], P('dp'), may hold values from 0 to 2
- disc_frames: int32 [24], P('dp'), may hold values from 1 to 5, 90 in all
- disc_labels: int32 [24], P('dp'), may hold values from 0 to 1
- logit_gain: float32 [512], replicated, may hold values from 0.1 to 1.9
- adv_weight: float32 [1], replicated, may hold values from 0.5 to 1.5
- train_step: int32 [1], replicated, may hold values from 1000 to 19999
- ln1_gain: float32 [512], replicated, may hold values from 0.1 to 1.9
- ln1_bias: float32 [512], replicated, may hold values from -1.5 to 1.5
- spatial_qkv: bfloat16 [3, 512, 512], P(None, None, 'tensor'), may hold values from -0.25 to 0.25
- spatial_out: bfloat16 [512, 512], P('tensor'), may hold values from -0.75 to 0.75
- ln2_gain: float32 [512], replicated, may hold values from 0.1 to 1.9
- ln2_bias: float32 [512], replicated, may hold values from -1.5 to 1.5
- temporal_qkv: bfloat16 [3, 512, 512], P(None, None, 'tensor'), may hold values from -0.25 to 0.25
- temporal_out: bfloat16 [512, 512], P('tensor'), may hold values from -0.5 to 0.5
- ln3_gain: float32 [512], replicated, may hold values from 0.1 to 1.9
- ln3_bias: float32 [512], replicated, may hold values from -1.5 to 1.5
- mlp_in: bfloat16 [512, 2048], P(None, 'tensor'), may hold values from -0.25 to 0.25
- mlp_out: bfloat16 [2048, 512], P('tensor'), may hold values from -0.125 to 0.125
Outputs:
- gen_out: bfloat16 [24, 5, 256, 512], P('dp', None, 'tensor')
- gen_in_grad: bfloat16 [24, 5, 256, 512], P('dp', None, 'tensor')
- disc_out: bfloat16 [24, 5, 256, 512], P('dp', None, 'tensor')
- disc_in_grad: bfloat16 [24, 5, 256, 512], P('dp', None, 'tensor')
- ln1_gain_grad: float32 [512], P('dp')
- ln1_bias_grad: float32 [512], P('dp')
- spatial_qkv_grad: float32 [3, 512, 512], P(None, 'dp', 'tensor')
- spatial_out_grad: float32 [512, 512], P('tensor', 'dp')
- ln2_gain_grad: float32 [512], P('dp')
- ln2_bias_grad: float32 [512], P('dp')
- temporal_qkv_grad: float32 [3, 512, 512], P(None, 'dp', 'tensor')
- temporal_out_grad: float32 [512, 512], P('tensor', 'dp')
- ln3_gain_grad: float32 [512], P('dp')
- ln3_bias_grad: float32 [512], P('dp')
- mlp_in_grad: float32 [512, 2048], P('dp', 'tensor')
- mlp_out_grad: float32 [2048, 512], P('tensor', 'dp')
The draws below stay inside these ranges and needn't reach their ends.
Inputs may be any that keep to these rules, and one draw needn't show every extreme that they name: `gen_aspect`: 0 lays a frame's patches on a square grid, 1 on a grid twice as wide, 2 on a grid half as wide; windows are 8 x 8 patches. `disc_aspect`: as gen_aspect. `gen_frames`: frames at or beyond a clip's count are padding; some clip has 5. `disc_frames`: as gen_frames.
All inputs are finite; a program needn't handle non-finite values. No bound on the sum of `gen_frames` or of `disc_frames` on one device may be relied on, other than what follows from the above.
Results may differ from the reference program's by a relative error of at most 0.025.
Values may be sent and summed in bfloat16 or wider, within the bound.
No kernel may reach another device: no remote copies, remote signals or barrier semaphores. Data moves between devices by JAX's collectives and lax.ppermute only.
A program may use at most 320 MiB of HBM per device.

```python
import math
from functools import partial
import jax
import jax.numpy as jnp
import numpy as np
from jax import lax

D = 512
HEADS = 8
HEAD_DIM = 64
FF = 2048
P_SIZE = 256
WIN = 8
FRAMES = 5
HALF = 5000
CLIPS_ALL = 24


def plant(array, rng, smallest, top_value):
    longest = array.shape.index(max(array.shape))
    spots = []
    for shift in (0, 1):
        where = [jax.random.randint(jax.random.fold_in(rng, axis), (), 0, length) for axis, length in enumerate(array.shape)]
        where[longest] = (where[longest] + shift) % array.shape[longest]
        spots.append(tuple(where))
    return array.at[spots[0]].set(smallest).at[spots[1]].set(top_value)


def level_of(stream_key, shape, cuts, smallest, top_value):
    def one(axis_at, parts):
        steps = jax.random.uniform(jax.random.fold_in(jax.random.fold_in(stream_key, 6), axis_at), (parts,), jnp.float32, smallest / len(cuts), top_value / len(cuts))
        return jnp.repeat(jnp.exp(steps), shape[axis_at] // parts).reshape((-1,) + (1,) * (len(shape) - axis_at - 1))

    level = one(*cuts[0])
    for cut in cuts[1:]:
        level = level * one(*cut)
    return level


def split_up(amount, total, bound, slope):
    portions = [(1 << 20) // math.isqrt(grade ** slope) + 1 for grade in range(2, amount + 1)]
    spare, given = total - bound - (amount - 1), [1] * (amount - 1)
    while spare > 0:
        movable = [i for i in range(amount - 1) if given[i] < bound]
        mass, left = sum([portions[i] for i in movable]), spare
        for i in movable:
            extra = min(bound - given[i], max(1, left * portions[i] // mass), spare)
            given[i] = given[i] + extra
            spare = spare - extra
    return np.array([bound] + given)


def uneven_parts(key, number_of, total, limit, slope):
    if number_of == 2:
        one = jax.random.randint(key, (), max(1, total - limit), min(limit, total - 1) + 1)
        return jnp.stack([one, total - one])
    lengths = jnp.asarray(split_up(number_of, total, limit, slope), jnp.int32)
    couples = (number_of - 1) // 2
    giver, taker = lengths[1:1 + 2 * couples:2], lengths[2:2 + 2 * couples:2]
    slack = jnp.minimum(giver - 1, limit - taker)
    passed = jax.random.randint(jax.random.fold_in(key, 1), (couples,), 0, 1 << 20) % (slack + 1)
    lengths = lengths.at[1:1 + 2 * couples:2].set(giver - passed).at[2:2 + 2 * couples:2].set(taker + passed)
    return lengths[jax.random.permutation(jax.random.fold_in(key, 2), number_of)]


def bell_draw(rng, shape, scale, most, shards=(), held_as=jnp.bfloat16):
    values = scale * jax.random.normal(rng, shape, jnp.float32)
    if shards:
        values = values * level_of(rng, shape, shards, -0.22, 0.18)
    return jnp.clip(values, -most, most).astype(held_as)


def setup_inputs(seed: int = 0) -> dict:
    streams_of = jax.random.split(jax.random.key(seed), 25)
    gen_tokens = bell_draw(streams_of[0], (CLIPS_ALL, FRAMES, P_SIZE, D), 1.0, 6.0, ((0, 8), (2, 4)))
    rec_grad = bell_draw(streams_of[1], (CLIPS_ALL, FRAMES, P_SIZE, D), 1.0, 6.0, ((0, 8), (2, 4)))
    adv_grad = bell_draw(streams_of[2], (CLIPS_ALL, FRAMES, P_SIZE, D), 1.0, 6.0, ((0, 8), (2, 4)))
    gen_aspect = plant(jax.random.randint(streams_of[3], (CLIPS_ALL,), 0, 3), jax.random.fold_in(streams_of[3], 1), 0, 2).astype(jnp.int32)
    gen_frames = uneven_parts(streams_of[4], CLIPS_ALL, CLIPS_ALL * FRAMES * 3 // 4, FRAMES, 1).astype(jnp.int32)
    disc_tokens = bell_draw(streams_of[5], (CLIPS_ALL, FRAMES, P_SIZE, D), 1.0, 6.0, ((0, 8), (2, 4)))
    disc_aspect = plant(jax.random.randint(streams_of[6], (CLIPS_ALL,), 0, 3), jax.random.fold_in(streams_of[6], 1), 0, 2).astype(jnp.int32)
    disc_frames = uneven_parts(streams_of[7], CLIPS_ALL, CLIPS_ALL * FRAMES * 3 // 4, FRAMES, 1).astype(jnp.int32)
    disc_labels = plant(jax.random.randint(streams_of[8], (CLIPS_ALL,), 0, 2), jax.random.fold_in(streams_of[8], 1), 0, 1).astype(jnp.int32)
    logit_gain = jnp.clip(1.0 + 0.18 * jax.random.normal(streams_of[9], (D,), jnp.float32), 0.1, 1.9)
    adv_weight = jnp.clip(jax.random.uniform(streams_of[10], (1,), jnp.float32, 0.5, 1.5), 0.5, 1.5)
    train_step = jax.random.randint(streams_of[11], (1,), 1000, 20000).astype(jnp.int32)
    ln1_gain = jnp.clip(1.0 + 0.18 * jax.random.normal(streams_of[12], (D,), jnp.float32), 0.1, 1.9)
    ln1_bias = bell_draw(streams_of[13], (D,), 0.3, 1.5, (), jnp.float32)
    spatial_qkv = bell_draw(streams_of[14], (3, D, D), D ** -0.5, 0.25, ((2, 4),))
    spatial_out = bell_draw(streams_of[15], (D, D), (D // 8) ** -0.5, 0.75, ((0, 4),))
    ln2_gain = jnp.clip(1.0 + 0.18 * jax.random.normal(streams_of[16], (D,), jnp.float32), 0.1, 1.9)
    ln2_bias = bell_draw(streams_of[17], (D,), 0.3, 1.5, (), jnp.float32)
    temporal_qkv = bell_draw(streams_of[18], (3, D, D), D ** -0.5, 0.25, ((2, 4),))
    temporal_out = bell_draw(streams_of[19], (D, D), (D // 4) ** -0.5, 0.5, ((0, 4),))
    ln3_gain = jnp.clip(1.0 + 0.18 * jax.random.normal(streams_of[20], (D,), jnp.float32), 0.1, 1.9)
    ln3_bias = bell_draw(streams_of[21], (D,), 0.3, 1.5, (), jnp.float32)
    mlp_in = bell_draw(streams_of[22], (D, FF), D ** -0.5, 0.25, ((1, 4),))
    mlp_out = bell_draw(streams_of[23], (FF, D), FF ** -0.5, 0.125, ((0, 4),))
    return {"gen_tokens": gen_tokens, "rec_grad": rec_grad, "adv_grad": adv_grad, "gen_aspect": gen_aspect, "gen_frames": gen_frames, "disc_tokens": disc_tokens, "disc_aspect": disc_aspect, "disc_frames": disc_frames, "disc_labels": disc_labels, "logit_gain": logit_gain, "adv_weight": adv_weight, "train_step": train_step, "ln1_gain": ln1_gain, "ln1_bias": ln1_bias, "spatial_qkv": spatial_qkv, "spatial_out": spatial_out, "ln2_gain": ln2_gain, "ln2_bias": ln2_bias, "temporal_qkv": temporal_qkv, "temporal_out": temporal_out, "ln3_gain": ln3_gain, "ln3_bias": ln3_bias, "mlp_in": mlp_in, "mlp_out": mlp_out}


HIGH = lax.Precision.HIGHEST
EPS = 1e-05

@jax.custom_vjp
def low(v):
    return lax.optimization_barrier(v.astype(jnp.bfloat16)).astype(jnp.float32)

@jax.custom_vjp
def low_back(v):
    return v

def low_keep(v):
    return (low(v), None)

def low_pass(kept, grad):
    return (grad,)

def back_keep(v):
    return (v, None)

def back_low(kept, grad):
    return (low(grad),)
low.defvjp(low_keep, low_pass)
low_back.defvjp(back_keep, back_low)

def layer_norm(value, norm_gain, norm_bias):
    average = lax.optimization_barrier(jnp.mean(value, axis=-1, keepdims=True))
    centred = value - average
    variance = lax.optimization_barrier(jnp.mean(centred * centred, axis=-1, keepdims=True))
    return centred * lax.rsqrt(variance + EPS) * norm_gain + norm_bias

def window_maps(aspect, tokens_frame):
    grid_side = math.isqrt(tokens_frame)
    window_area = WIN * WIN
    grid_width = jnp.where(aspect == 1, 2 * grid_side, jnp.where(aspect == 2, grid_side // 2, grid_side)).astype(jnp.int32)[:, None]
    across = grid_width // WIN
    places = jnp.arange(tokens_frame, dtype=jnp.int32)[None, :]
    window = places // window_area
    inside = places % window_area
    grid_row = window // across * WIN + inside // WIN
    grid_col = window % across * WIN + inside % WIN
    forward_order = (grid_row * grid_width + grid_col).astype(jnp.int32)
    raster_row = places // grid_width
    raster_col = places % grid_width
    back_order = ((raster_row // WIN * across + raster_col // WIN) * window_area + raster_row % WIN * WIN + raster_col % WIN).astype(jnp.int32)
    return (forward_order, back_order)

def spatial_groups(win_order, values):
    reordered = jnp.take(values, win_order, axis=1)
    return reordered.reshape(-1, WIN * WIN, HEADS, HEAD_DIM)

def spatial_merge(win_back, frame_count, values):
    flat = values.reshape(frame_count, -1, HEADS * HEAD_DIM)
    return jnp.take(flat, win_back, axis=1)

def temporal_groups(values):
    heads_split = values.reshape(values.shape[0], values.shape[1], HEADS, HEAD_DIM)
    return jnp.transpose(heads_split, (1, 0, 2, 3))

def temporal_merge(values):
    moved = jnp.transpose(values, (1, 0, 2, 3))
    return moved.reshape(moved.shape[0], moved.shape[1], HEADS * HEAD_DIM)

def attention_block(residual, norm_gain, norm_bias, w_qkv, w_out, grouping, merging, allowed):
    normed = low(layer_norm(residual, norm_gain, norm_bias))
    packed = low(low_back(jnp.einsum('fpd,kde->kfpe', normed, w_qkv, precision=HIGH)))
    queries, key_rows, value_rows = (grouping(packed[0]), grouping(packed[1]), grouping(packed[2]))
    scores = low_back(jnp.einsum('bqhd,bkhd->bhqk', queries, key_rows, precision=HIGH) * (1.0 / math.sqrt(HEAD_DIM)))
    if allowed is not None:
        scores = jnp.where(allowed, scores, -1e+30)
    prob_low = low(jax.nn.softmax(scores, axis=-1))
    attended = low(low_back(jnp.einsum('bhqk,bkhd->bqhd', prob_low, value_rows, precision=HIGH)))
    branch = low_back(jnp.einsum('fpe,ed->fpd', merging(attended), w_out, precision=HIGH))
    return residual + branch

def mlp_block(residual, norm_gain, norm_bias, w_in, w_out):
    normed = low(layer_norm(residual, norm_gain, norm_bias))
    hidden = low_back(jnp.einsum('fpd,de->fpe', normed, w_in, precision=HIGH))
    active = low(jax.nn.gelu(hidden, approximate=False))
    return residual + low_back(jnp.einsum('fpe,ed->fpd', active, w_out, precision=HIGH))

def layer(tokens, params, win_order, win_back):
    gain_one, bias_one, space_qkv, space_out, gain_two, bias_two, time_qkv, time_out, gain_three, bias_three, w_in, w_out = params
    frame_count = tokens.shape[0]
    frame_steps = jnp.arange(frame_count, dtype=jnp.int32)
    allowed = (frame_steps[None, :] <= frame_steps[:, None])[None, None]
    after_space = attention_block(tokens, gain_one, bias_one, space_qkv, space_out, partial(spatial_groups, win_order), partial(spatial_merge, win_back, frame_count), None)
    after_time = attention_block(after_space, gain_two, bias_two, time_qkv, time_out, temporal_groups, temporal_merge, allowed)
    return mlp_block(after_time, gain_three, bias_three, w_in, w_out)

def reference(gen_tokens, rec_grad, adv_grad, gen_aspect, gen_frames, disc_tokens, disc_aspect, disc_frames, disc_labels, logit_gain, adv_weight, train_step, ln1_gain, ln1_bias, spatial_qkv, spatial_out, ln2_gain, ln2_bias, temporal_qkv, temporal_out, ln3_gain, ln3_bias, mlp_in, mlp_out):
    params = tuple((weight.astype(jnp.float32) for weight in (ln1_gain, ln1_bias, spatial_qkv, spatial_out, ln2_gain, ln2_bias, temporal_qkv, temporal_out, ln3_gain, ln3_bias, mlp_in, mlp_out)))
    step_value = train_step[0].astype(jnp.float32)
    ramp = adv_weight[0] * step_value / (step_value + HALF)
    frame_ids = jnp.arange(FRAMES, dtype=jnp.int32)
    zero_sums = tuple((jnp.zeros_like(weight) for weight in params))

    def gen_clip(totals, item):
        tokens, aspect, count, recon, advers = item
        win_order, win_back = window_maps(aspect[None], P_SIZE)
        output, pullback = jax.vjp(lambda inputs, weights: layer(inputs, weights, win_order[0], win_back[0]), tokens.astype(jnp.float32), params)
        live = (frame_ids < count).astype(jnp.float32)[:, None, None]
        grad_in, grad_weights = pullback(live * (recon.astype(jnp.float32) + ramp * advers.astype(jnp.float32)))
        return (jax.tree.map(jnp.add, totals, grad_weights), (output.astype(jnp.bfloat16), grad_in.astype(jnp.bfloat16)))

    def disc_clip(totals, item):
        tokens, aspect, count, label = item
        win_order, win_back = window_maps(aspect[None], P_SIZE)
        output, pullback = jax.vjp(lambda inputs, weights: layer(inputs, weights, win_order[0], win_back[0]), tokens.astype(jnp.float32), params)
        live = (frame_ids < count).astype(jnp.float32)[:, None, None]
        signs = (2 * label - 1).astype(jnp.float32)

        def hinge(output_value):
            return jnp.sum(live * jax.nn.softplus(1.0 - signs * logit_gain * output_value))
        grad_in, grad_weights = pullback(jax.grad(hinge)(output))
        return (jax.tree.map(jnp.add, totals, grad_weights), (output.astype(jnp.bfloat16), grad_in.astype(jnp.bfloat16)))
    totals, (gen_out, gen_in_grad) = lax.scan(gen_clip, zero_sums, (gen_tokens, gen_aspect, gen_frames, rec_grad, adv_grad))
    totals, (disc_out, disc_in_grad) = lax.scan(disc_clip, totals, (disc_tokens, disc_aspect, disc_frames, disc_labels))
    return (gen_out, gen_in_grad, disc_out, disc_in_grad, totals[0], totals[1], totals[2], totals[3], totals[4], totals[5], totals[6], totals[7], totals[8], totals[9], totals[10], totals[11])
```

```python
from functools import partial
import math

import jax
import jax.numpy as jnp
from jax import lax
from jax.experimental import pallas as pl
from jax.experimental.pallas import tpu as pltpu
from jax.sharding import PartitionSpec as P

HEAD_DIM = 64
WIN = 8
AREA = WIN * WIN
HALF = 5000
EPS = 1e-05
F32 = jnp.float32
BF16 = jnp.bfloat16
VMEM_LIMIT = 56 * 1024 * 1024

NT = (((1,), (1,)), ((), ()))
TN = (((0,), (0,)), ((), ()))


def dot(lhs, rhs):
    return jnp.dot(lhs, rhs, preferred_element_type=F32)


def dot_nt(lhs, rhs):
    return lax.dot_general(lhs, rhs, NT, preferred_element_type=F32)


def dot_tn(lhs, rhs):
    return lax.dot_general(lhs, rhs, TN, preferred_element_type=F32)


def normalize(value):
    average = jnp.mean(value, axis=-1, keepdims=True)
    centred = value - average
    variance = jnp.mean(centred * centred, axis=-1, keepdims=True)
    scale = lax.rsqrt(variance + EPS)
    return centred * scale, scale


def norm_backward(unit, scale, gain, grad):
    scaled = grad * gain
    inner = scaled - jnp.mean(scaled, axis=-1, keepdims=True)
    return scale * (inner - unit * jnp.mean(scaled * unit, axis=-1, keepdims=True))


def row_sums(values):
    return jnp.sum(values.reshape(-1, 8, values.shape[-1]), axis=0)


def params(cost=None):
    return pltpu.CompilerParams(dimension_semantics=("arbitrary",), vmem_limit_bytes=VMEM_LIMIT)


def whole(shape):
    zeros = (0,) * len(shape)
    return pl.BlockSpec(shape, lambda i: zeros)


def per_clip(shape):
    zeros = (0,) * (len(shape) - 1)
    return pl.BlockSpec((1,) + tuple(shape[1:]), lambda i: (i,) + zeros)


def head_mask(dtype):
    rows = lax.broadcasted_iota(jnp.int32, (256, 256), 0) // HEAD_DIM
    cols = lax.broadcasted_iota(jnp.int32, (256, 256), 1) // HEAD_DIM
    return jnp.where(rows == cols, 1.0, 0.0).astype(dtype)


def spread(values, mask):
    return jnp.concatenate([values] * 4, axis=0) * mask


def pair_product(scores, values, low_lane):
    parts = []
    for c in range(2):
        full = dot_tn(scores[:, c * 128 : (c + 1) * 128], values[:, c * 128 : (c + 1) * 128])
        parts.append(jnp.where(low_lane, full[:64], full[64:]))
    return jnp.concatenate(parts, axis=1)


def join_heads(w_ref, full_ref):
    for t in range(w_ref.shape[0]):
        width = w_ref.shape[3]
        for j in range(3):
            full_ref[j, :, t * width : (t + 1) * width] = w_ref[t, j]


def space_forward_kernel(
    x_ref, gain_ref, bias_ref, w_ref, wo_ref, x1_ref, a_ref, qkv_ref, p_ref, o_ref, wfull_ref
):
    @pl.when(pl.program_id(0) == 0)
    def _():
        join_heads(w_ref, wfull_ref)

    rows = x_ref.shape[1]
    x = x_ref[0].astype(F32)
    unit, _ = normalize(x)
    a_ref[0] = (unit * gain_ref[...] + bias_ref[...]).astype(BF16)
    for j in range(3):
        qkv_ref[0, :, j * 512 : (j + 1) * 512] = dot(a_ref[0], wfull_ref[j]).astype(BF16)
    mask = head_mask(BF16)
    low_lane = lax.broadcasted_iota(jnp.int32, (64, 128), 1) < HEAD_DIM
    for w in range(rows // AREA):
        for g in range(2):
            sl = slice(w * AREA, (w + 1) * AREA)
            q, k, v = (
                qkv_ref[0, sl, j * 512 + g * 256 : j * 512 + (g + 1) * 256] for j in range(3)
            )
            s = dot_nt(k, spread(q, mask)) * 0.125
            e = jnp.exp(s - jnp.max(s, axis=0, keepdims=True))
            p = (e * (1.0 / jnp.sum(e, axis=0, keepdims=True))).astype(BF16)
            p_ref[0, 2 * w + g] = p
            o_ref[0, sl, g * 256 : (g + 1) * 256] = pair_product(p, v, low_lane).astype(BF16)
    x1_ref[0] = x + dot(o_ref[0], wo_ref[...])


def space_forward(x, gain, bias, w, wo):
    clips, rows, width = x.shape
    windows = rows // AREA
    shape = jax.ShapeDtypeStruct
    outs = (
        shape((clips, rows, width), F32),
        shape((clips, rows, width), BF16),
        shape((clips, rows, 3 * width), BF16),
        shape((clips, 2 * windows, AREA, 256), BF16),
        shape((clips, rows, width), BF16),
    )
    return pl.pallas_call(
        space_forward_kernel,
        grid=(clips,),
        in_specs=[per_clip(x.shape), whole(gain.shape), whole(bias.shape), whole(w.shape), whole(wo.shape)],
        out_specs=[per_clip(o.shape) for o in outs],
        out_shape=outs,
        scratch_shapes=[pltpu.VMEM((3, width, width), BF16)],
        compiler_params=params(),
    )(x, gain, bias, w, wo)


def space_backward_kernel(
    dx1_ref, x_ref, gain_ref, w_ref, wo_ref, qkv_ref, p_ref,
    dx0_ref, low_ref, dqkv_ref, dg_ref, db_ref, wfull_ref, do_ref,
):
    @pl.when(pl.program_id(0) == 0)
    def _():
        join_heads(w_ref, wfull_ref)
        dg_ref[...] = jnp.zeros_like(dg_ref)
        db_ref[...] = jnp.zeros_like(db_ref)

    rows = x_ref.shape[1]
    low_ref[0] = dx1_ref[0].astype(BF16)
    do_ref[...] = dot_nt(low_ref[0], wo_ref[...]).astype(BF16)
    mask = head_mask(BF16)
    low_lane = lax.broadcasted_iota(jnp.int32, (64, 128), 1) < HEAD_DIM
    for w in range(rows // AREA):
        for g in range(2):
            sl = slice(w * AREA, (w + 1) * AREA)
            q, k, v = (
                qkv_ref[0, sl, j * 512 + g * 256 : j * 512 + (g + 1) * 256] for j in range(3)
            )
            p = p_ref[0, 2 * w + g]
            dob = spread(do_ref[sl, g * 256 : (g + 1) * 256], mask)
            dv = dot(p, dob)
            dp = dot_nt(v, dob)
            p = p.astype(F32)
            weighted = p * dp
            ds = (weighted - p * jnp.sum(weighted, axis=0, keepdims=True)).astype(BF16)
            dk = dot(ds, spread(q, mask)) * 0.125
            dq = pair_product(ds, k, low_lane) * 0.125
            for j, part in enumerate((dq, dk, dv)):
                dqkv_ref[0, sl, j * 512 + g * 256 : j * 512 + (g + 1) * 256] = part.astype(BF16)
    da = sum(dot_nt(dqkv_ref[0, :, j * 512 : (j + 1) * 512], wfull_ref[j]) for j in range(3))
    unit, scale = normalize(x_ref[0].astype(F32))
    dg_ref[...] += row_sums(da * unit)
    db_ref[...] += row_sums(da)
    dx0_ref[0] = (dx1_ref[0] + norm_backward(unit, scale, gain_ref[...], da)).astype(BF16)


def space_backward(dx1, x, gain, w, wo, qkv, p):
    clips, rows, width = x.shape
    shape = jax.ShapeDtypeStruct
    outs = (
        shape((clips, rows, width), BF16),
        shape((clips, rows, width), BF16),
        shape((clips, rows, 3 * width), BF16),
        shape((8, width), F32),
        shape((8, width), F32),
    )
    return pl.pallas_call(
        space_backward_kernel,
        grid=(clips,),
        in_specs=[per_clip(dx1.shape), per_clip(x.shape), whole(gain.shape), whole(w.shape), whole(wo.shape), per_clip(qkv.shape), per_clip(p.shape)],
        out_specs=[per_clip(o.shape) for o in outs[:3]] + [whole((8, width))] * 2,
        out_shape=outs,
        scratch_shapes=[pltpu.VMEM((3, width, width), BF16), pltpu.VMEM((rows, width), BF16)],
        compiler_params=params(),
    )(dx1, x, gain, w, wo, qkv, p)


def head_select(frame):
    rows = lax.broadcasted_iota(jnp.int32, (512, 128), 0) // HEAD_DIM
    cols = lax.broadcasted_iota(jnp.int32, (512, 128), 1) - 8 * frame
    return jnp.where(rows == cols, 1.0, 0.0).astype(BF16)


def head_expand(frame):
    rows = lax.broadcasted_iota(jnp.int32, (128, 512), 0) - 8 * frame
    cols = lax.broadcasted_iota(jnp.int32, (128, 512), 1) // HEAD_DIM
    return jnp.where(rows == cols, 1.0, 0.0).astype(BF16)


def head_sums(products, selector):
    high = products.astype(BF16)
    rest = (products - high.astype(F32)).astype(BF16)
    return dot(high, selector) + dot(rest, selector)


def time_scores(frames, left, right):
    totals = [None] * frames
    for t in range(frames):
        lhs = left(t).astype(F32)
        stacked = jnp.concatenate([lhs * right(f).astype(F32) for f in range(t + 1)], axis=0)
        sums = head_sums(stacked, head_select(t))
        for f in range(t + 1):
            part = sums[f * AREA : (f + 1) * AREA]
            totals[f] = part if totals[f] is None else totals[f] + part
    return totals


def time_forward_kernel(x_ref, gain_ref, bias_ref, w_ref, wo_ref, x2_ref, a_ref, qkv_ref, p_ref, o_ref, wfull_ref):
    @pl.when(pl.program_id(0) == 0)
    def _():
        join_heads(w_ref, wfull_ref)

    rows = x_ref.shape[1]
    frames = rows // AREA
    x = x_ref[0]
    unit, _ = normalize(x)
    a_ref[0] = (unit * gain_ref[...] + bias_ref[...]).astype(BF16)
    for j in range(3):
        qkv_ref[0, :, j * 512 : (j + 1) * 512] = dot(a_ref[0], wfull_ref[j]).astype(BF16)

    def part(j):
        return lambda f: qkv_ref[0, f * AREA : (f + 1) * AREA, j * 512 : (j + 1) * 512]

    scores = time_scores(frames, part(0), part(1))
    lane = lax.broadcasted_iota(jnp.int32, (AREA, 128), 1)
    scores = [jnp.where(lane >= 8 * f, s * 0.125, -1e30) for f, s in enumerate(scores)]
    top = scores[0]
    for s in scores[1:]:
        top = jnp.maximum(top, s)
    exps = [jnp.exp(s - top) for s in scores]
    inverse = 1.0 / sum(exps)
    probs = [e * inverse for e in exps]
    for f in range(frames):
        p_ref[0, f * AREA : (f + 1) * AREA, :] = probs[f]
    low = [p.astype(BF16) for p in probs]
    values = part(2)
    for t in range(frames):
        wide = dot(jnp.concatenate(low[: t + 1], axis=0), head_expand(t))
        total = None
        for f in range(t + 1):
            term = wide[f * AREA : (f + 1) * AREA] * values(f).astype(F32)
            total = term if total is None else total + term
        o_ref[0, t * AREA : (t + 1) * AREA, :] = total.astype(BF16)
    x2_ref[0] = x + dot(o_ref[0], wo_ref[...])


def time_forward(x, gain, bias, w, wo):
    clips, rows, width = x.shape
    shape = jax.ShapeDtypeStruct
    outs = (
        shape((clips, rows, width), F32),
        shape((clips, rows, width), BF16),
        shape((clips, rows, 3 * width), BF16),
        shape((clips, rows, 128), F32),
        shape((clips, rows, width), BF16),
    )
    return pl.pallas_call(
        time_forward_kernel,
        grid=(clips,),
        in_specs=[per_clip(x.shape), whole(gain.shape), whole(bias.shape), whole(w.shape), whole(wo.shape)],
        out_specs=[per_clip(o.shape) for o in outs],
        out_shape=outs,
        scratch_shapes=[pltpu.VMEM((3, width, width), BF16)],
        compiler_params=params(),
    )(x, gain, bias, w, wo)


def time_backward_kernel(
    dx2_ref, x_ref, gain_ref, w_ref, wo_ref, qkv_ref, p_ref,
    dx1_ref, low_ref, dqkv_ref, dg_ref, db_ref, wfull_ref, do_ref,
):
    @pl.when(pl.program_id(0) == 0)
    def _():
        join_heads(w_ref, wfull_ref)
        dg_ref[...] = jnp.zeros_like(dg_ref)
        db_ref[...] = jnp.zeros_like(db_ref)

    rows = x_ref.shape[1]
    frames = rows // AREA
    low_ref[0] = dx2_ref[0].astype(BF16)
    do_ref[...] = dot_nt(low_ref[0], wo_ref[...]).astype(BF16)

    def part(j):
        return lambda f: qkv_ref[0, f * AREA : (f + 1) * AREA, j * 512 : (j + 1) * 512]

    queries, key_rows, values = part(0), part(1), part(2)

    def grads(t):
        return do_ref[t * AREA : (t + 1) * AREA, :]

    dp = time_scores(frames, grads, values)
    probs = [p_ref[0, f * AREA : (f + 1) * AREA, :] for f in range(frames)]
    inner = sum(p * d for p, d in zip(probs, dp))
    ds = [(p * (d - inner)).astype(BF16) for p, d in zip(probs, dp)]
    low = [p.astype(BF16) for p in probs]
    dk = [None] * frames
    dv = [None] * frames
    for t in range(frames):
        wide = dot(jnp.concatenate(ds[: t + 1] + low[: t + 1], axis=0), head_expand(t))
        q, do = queries(t).astype(F32), grads(t).astype(F32)
        dq = None
        for f in range(t + 1):
            ds_wide = wide[f * AREA : (f + 1) * AREA]
            p_wide = wide[(t + 1 + f) * AREA : (t + 2 + f) * AREA]
            term = ds_wide * key_rows(f).astype(F32)
            dq = term if dq is None else dq + term
            dk[f] = ds_wide * q if dk[f] is None else dk[f] + ds_wide * q
            dv[f] = p_wide * do if dv[f] is None else dv[f] + p_wide * do
        dqkv_ref[0, t * AREA : (t + 1) * AREA, 0:512] = (dq * 0.125).astype(BF16)
    for f in range(frames):
        dqkv_ref[0, f * AREA : (f + 1) * AREA, 512:1024] = (dk[f] * 0.125).astype(BF16)
        dqkv_ref[0, f * AREA : (f + 1) * AREA, 1024:1536] = dv[f].astype(BF16)
    da = sum(dot_nt(dqkv_ref[0, :, j * 512 : (j + 1) * 512], wfull_ref[j]) for j in range(3))
    unit, scale = normalize(x_ref[0])
    dg_ref[...] += row_sums(da * unit)
    db_ref[...] += row_sums(da)
    dx1_ref[0] = dx2_ref[0] + norm_backward(unit, scale, gain_ref[...], da)


def time_backward(dx2, x, gain, w, wo, qkv, p):
    clips, rows, width = x.shape
    shape = jax.ShapeDtypeStruct
    outs = (
        shape((clips, rows, width), F32),
        shape((clips, rows, width), BF16),
        shape((clips, rows, 3 * width), BF16),
        shape((8, width), F32),
        shape((8, width), F32),
    )
    return pl.pallas_call(
        time_backward_kernel,
        grid=(clips,),
        in_specs=[per_clip(dx2.shape), per_clip(x.shape), whole(gain.shape), whole(w.shape), whole(wo.shape), per_clip(qkv.shape), per_clip(p.shape)],
        out_specs=[per_clip(o.shape) for o in outs[:3]] + [whole((8, width))] * 2,
        out_shape=outs,
        scratch_shapes=[pltpu.VMEM((3, width, width), BF16), pltpu.VMEM((rows, width), BF16)],
        compiler_params=params(),
    )(dx2, x, gain, w, wo, qkv, p)


def gelu_parts(h):
    e = jnp.exp(h * h * -0.5)
    t = 1.0 / (1.0 + (0.3275911 * math.sqrt(0.5)) * jnp.abs(h))
    tail = t * (0.127414796 + t * (-0.142248368 + t * (0.7107068705 + t * (-0.7265760135 + t * 0.5307027145)))) * e
    cdf = jnp.where(h >= 0, 1.0 - tail, tail)
    return h * cdf, cdf + h * (e * 0.3989422804014327)


def mlp_kernel(
    disc, sign_ref, count_ref, x_ref, gain_ref, bias_ref, win_ref, wout_ref, extra_ref,
    y_ref, dx_ref, c_ref, u_ref, gb_ref, dh_ref, dg_ref, db_ref, slope_ref,
):
    @pl.when(pl.program_id(0) == 0)
    def _():
        dg_ref[...] = jnp.zeros_like(dg_ref)
        db_ref[...] = jnp.zeros_like(db_ref)

    rows = x_ref.shape[1]
    tiles = win_ref.shape[0]
    x = x_ref[0]
    unit, scale = normalize(x)
    c_ref[0] = (unit * gain_ref[...] + bias_ref[...]).astype(BF16)
    y = x
    span = win_ref.shape[2]
    for j in range(tiles):
        h = dot(c_ref[0], win_ref[j])
        active, slope = gelu_parts(h)
        u_ref[0, :, j * span : (j + 1) * span] = active.astype(BF16)
        slope_ref[:, j * span : (j + 1) * span] = slope.astype(BF16)
        y = y + dot(u_ref[0, :, j * span : (j + 1) * span], wout_ref[j])
    y_ref[0] = y.astype(BF16)
    if disc:
        clip = pl.program_id(0)
        sign = sign_ref[clip]
        frame = lax.broadcasted_iota(jnp.int32, (rows, 1), 0) // AREA
        live = jnp.where(frame < count_ref[clip], -sign, 0.0)
        signed = sign * extra_ref[...]
        dy = live * extra_ref[...] * jax.nn.sigmoid(1.0 - signed * y)
    else:
        dy = extra_ref[0].astype(F32)
    gb_ref[0] = dy.astype(BF16)
    dc = None
    for j in range(tiles):
        du = dot_nt(gb_ref[0], wout_ref[j])
        dh = (du * slope_ref[:, j * span : (j + 1) * span].astype(F32)).astype(BF16)
        dh_ref[0, :, j * span : (j + 1) * span] = dh
        term = dot_nt(dh_ref[0, :, j * span : (j + 1) * span], win_ref[j])
        dc = term if dc is None else dc + term
    dg_ref[...] += row_sums(dc * unit)
    db_ref[...] += row_sums(dc)
    dx_ref[0] = dy + norm_backward(unit, scale, gain_ref[...], dc)


def mlp(disc, sign, count, x, gain, bias, win, wout, extra):
    clips, rows, width = x.shape
    hidden = win.shape[0] * win.shape[2]
    shape = jax.ShapeDtypeStruct
    outs = (
        shape((clips, rows, width), BF16),
        shape((clips, rows, width), F32),
        shape((clips, rows, width), BF16),
        shape((clips, rows, hidden), BF16),
        shape((clips, rows, width), BF16),
        shape((clips, rows, hidden), BF16),
        shape((8, width), F32),
        shape((8, width), F32),
    )
    smem = pl.BlockSpec(memory_space=pltpu.SMEM)
    return pl.pallas_call(
        partial(mlp_kernel, disc),
        grid=(clips,),
        in_specs=[smem, smem, per_clip(x.shape), whole(gain.shape), whole(bias.shape), whole(win.shape), whole(wout.shape),
                  whole(extra.shape) if disc else per_clip(extra.shape)],
        out_specs=[per_clip(o.shape) for o in outs[:6]] + [whole((8, width))] * 2,
        out_shape=outs,
        scratch_shapes=[pltpu.VMEM((rows, hidden), BF16)],
        compiler_params=params(),
    )(sign, count, x, gain, bias, win, wout, extra)


def one_hot(source, count):
    rows = source.shape[0]
    inside = lax.broadcasted_iota(jnp.int32, (rows, count), 0) % 8
    cols = lax.broadcasted_iota(jnp.int32, (rows, count), 1)
    return jnp.where((source >= 0) & (cols == source * 8 + inside), 1.0, 0.0).astype(BF16)


def chunk_ids():
    return lax.broadcasted_iota(jnp.int32, (AREA, 1), 0) // 8


def send_source(aspect, t):
    c = chunk_ids()
    square = jnp.where(c < 4, 2 * c + 1 - t % 2, -1)
    wide = jnp.where(
        c < 2, 4 * c + (t ^ 1), jnp.where(c < 4, -1, jnp.where(c < 6, 4 * (c - 4) + (t ^ 2), 4 * (c - 6) + (t ^ 3)))
    )
    return jnp.where(aspect == 0, square, jnp.where(aspect == 1, wide, -1))


def window_source(aspect, t):
    c = chunk_ids()
    square = jnp.where(c < 4, 2 * c + t % 2, c + 4)
    wide = jnp.where(c < 2, 4 * c + t, jnp.where(c < 4, c + 10, jnp.where(c < 6, c + 4, c + 8)))
    return jnp.where(aspect == 0, square, jnp.where(aspect == 1, wide, c))


def raster_source(aspect, t):
    c = chunk_ids()
    square = c // 2 + jnp.where(c % 2 == t % 2, 0, 8)
    way = (c % 4) ^ t
    wide = c // 4 + jnp.where(way == 0, 0, jnp.where(way == 1, 8, jnp.where(way == 2, 12, 14)))
    return jnp.where(aspect == 0, square, jnp.where(aspect == 1, wide, c))


def write_sends(values, refs):
    for f in range(values.shape[0] // AREA):
        base = f * AREA
        refs[0][0, f * 32 : (f + 1) * 32, :] = values[base + 32 : base + 64]
        refs[1][0, f * 16 : (f + 1) * 16, :] = values[base + 16 : base + 32]
        refs[2][0, f * 16 : (f + 1) * 16, :] = values[base + 48 : base + 64]


def pack_rows(values, select, refs):
    for f in range(values.shape[0] // AREA):
        moved = dot(select, values[f * AREA : (f + 1) * AREA]).astype(BF16)
        refs[0][0, f * 32 : (f + 1) * 32, :] = moved[:32]
        refs[1][0, f * 16 : (f + 1) * 16, :] = moved[32:48]
        refs[2][0, f * 16 : (f + 1) * 16, :] = moved[48:]


def pack_kernel(place_ref, aspect_ref, x_ref, *send_refs):
    select = one_hot(send_source(aspect_ref[pl.program_id(0)], place_ref[0]), AREA)
    pack_rows(x_ref[0], select, send_refs)


def pack_grad_kernel(place_ref, aspect_ref, count_ref, ramp_ref, rec_ref, adv_ref, dy_ref, *send_refs):
    clip = pl.program_id(0)
    frame = lax.broadcasted_iota(jnp.int32, (rec_ref.shape[1], 1), 0) // AREA
    total = rec_ref[0].astype(F32) + ramp_ref[0] * adv_ref[0].astype(F32)
    dy_ref[0] = jnp.where(frame < count_ref[clip], total, 0.0).astype(BF16)
    select = one_hot(send_source(aspect_ref[clip], place_ref[0]), AREA)
    pack_rows(dy_ref[0], select, send_refs)


def join_kernel(source, place_ref, aspect_ref, own_ref, r1_ref, r2_ref, r3_ref, out_ref):
    select = one_hot(source(aspect_ref[pl.program_id(0)], place_ref[0]), 2 * AREA)
    for f in range(out_ref.shape[1] // AREA):
        rows = jnp.concatenate(
            [
                own_ref[0, f * AREA : (f + 1) * AREA, :],
                r1_ref[0, f * 32 : (f + 1) * 32, :],
                r2_ref[0, f * 16 : (f + 1) * 16, :],
                r3_ref[0, f * 16 : (f + 1) * 16, :],
            ],
            axis=0,
        )
        out_ref[0, f * AREA : (f + 1) * AREA, :] = dot(select, rows).astype(BF16)


SMEM = pl.BlockSpec(memory_space=pltpu.SMEM)


def send_shapes(x):
    clips, rows, width = x.shape
    return tuple(jax.ShapeDtypeStruct((clips, rows // part, width), BF16) for part in (2, 4, 4))


def pack(place, aspect, x):
    outs = send_shapes(x)
    return pl.pallas_call(
        pack_kernel,
        grid=(x.shape[0],),
        in_specs=[SMEM, SMEM, per_clip(x.shape)],
        out_specs=[per_clip(o.shape) for o in outs],
        out_shape=outs,
        compiler_params=params(),
    )(place, aspect, x)


def pack_grad(place, aspect, count, ramp, rec, adv):
    outs = (jax.ShapeDtypeStruct(rec.shape, BF16),) + send_shapes(rec)
    return pl.pallas_call(
        pack_grad_kernel,
        grid=(rec.shape[0],),
        in_specs=[SMEM, SMEM, SMEM, SMEM, per_clip(rec.shape), per_clip(adv.shape)],
        out_specs=[per_clip(o.shape) for o in outs],
        out_shape=outs,
        compiler_params=params(),
    )(place, aspect, count, ramp, rec, adv)


def join(source, place, aspect, own, parts):
    return pl.pallas_call(
        partial(join_kernel, source),
        grid=(own.shape[0],),
        in_specs=[SMEM, SMEM, per_clip(own.shape)] + [per_clip(p.shape) for p in parts],
        out_specs=per_clip(own.shape),
        out_shape=jax.ShapeDtypeStruct(own.shape, BF16),
        compiler_params=params(),
    )(place, aspect, own, *parts)


def exchange(parts):
    return tuple(
        lax.ppermute(part, "tensor", [(i, i ^ way) for i in range(4)]) for way, part in zip((1, 2, 3), parts)
    )


def window_maps(aspect, tokens_frame):
    grid_side = math.isqrt(tokens_frame)
    grid_width = jnp.where(
        aspect == 1, 2 * grid_side, jnp.where(aspect == 2, grid_side // 2, grid_side)
    ).astype(jnp.int32)[:, None]
    across = grid_width // WIN
    places = jnp.arange(tokens_frame, dtype=jnp.int32)[None, :]
    window = places // AREA
    inside = places % AREA
    grid_row = window // across * WIN + inside // WIN
    grid_col = window % across * WIN + inside % WIN
    forward_order = grid_row * grid_width + grid_col
    raster_row = places // grid_width
    raster_col = places % grid_width
    back_order = (
        (raster_row // WIN * across + raster_col // WIN) * AREA + raster_row % WIN * WIN + raster_col % WIN
    )
    return (forward_order, back_order)


def reorder(values, order):
    return jax.vmap(partial(jnp.take, axis=1))(values, order)


def pad_clips(values, split):
    return jnp.pad(values, [(0, -values.shape[0] % split)] + [(0, 0)] * (values.ndim - 1))


def gather_window(x, aspect, split):
    whole_x = pad_clips(lax.all_gather(x, "tensor", axis=2, tiled=True), split)
    aspect = pad_clips(aspect, split)
    t = lax.axis_index("tensor")
    clips = aspect.shape[0] // split
    mine = lax.dynamic_slice_in_dim(whole_x, t % split * clips, clips, 0)
    kinds = lax.dynamic_slice_in_dim(aspect, t % split * clips, clips, 0)
    order, _ = window_maps(kinds, whole_x.shape[2])
    return reorder(mine, lax.dynamic_slice_in_dim(order, t // split * AREA, AREA, 1))


def gather_raster(y, aspect, split, patches):
    every = lax.all_gather(y, "tensor", axis=0)
    count, clips, frames, _, width = every.shape
    every = every.reshape(count // split, split, clips, frames, AREA, width)
    every = jnp.transpose(every, (1, 2, 3, 0, 4, 5)).reshape(split * clips, frames, -1, width)
    _, back = window_maps(aspect, every.shape[2])
    t = lax.axis_index("tensor")
    return reorder(every[: aspect.shape[0]], lax.dynamic_slice_in_dim(back, t * patches, patches, 1))


def gather_weight(shard):
    rows = shard.shape[0] // lax.axis_size("dp")
    piece = lax.dynamic_slice_in_dim(shard, lax.axis_index("dp") * rows, rows, 0)
    whole_w = lax.all_gather(piece, ("tensor", "dp"), axis=0, tiled=True)
    return whole_w.reshape((-1,) + shard.shape)


def scatter_grad(grads):
    flat = jnp.concatenate([g.astype(BF16).reshape(g.shape[0], -1) for g in grads], axis=1)
    flat = lax.psum_scatter(flat, "dp", scatter_dimension=0, tiled=True)
    pieces, offset = [], 0
    count = lax.axis_size("tensor")
    for g in grads:
        size = math.prod(g.shape[1:])
        piece = flat[:, offset : offset + size].reshape((flat.shape[0],) + g.shape[1:])
        pieces.append(jnp.moveaxis(piece, 2, 0).reshape(count, flat.shape[0], -1))
        offset += size
    mine = lax.psum_scatter(jnp.concatenate(pieces, axis=2), "tensor", scatter_dimension=0, tiled=True)[0]
    results, offset = [], 0
    for g in grads:
        size = g.shape[1] * g.shape[3]
        results.append(mine[:, offset : offset + size].reshape(-1, g.shape[1], g.shape[3]).astype(F32))
        offset += size
    return results


def product_sum(lefts, rights):
    return sum(
        lax.dot_general(a, b, (((0, 1), (0, 1)), ((), ())), preferred_element_type=F32)
        for a, b in zip(lefts, rights)
    )


def shards(
    gen_tokens, rec_grad, adv_grad, gen_aspect, gen_frames, disc_tokens, disc_aspect, disc_frames, disc_labels,
    logit_gain, adv_weight, train_step, ln1_gain, ln1_bias, spatial_qkv, spatial_out, ln2_gain, ln2_bias,
    temporal_qkv, temporal_out, ln3_gain, ln3_bias, mlp_in, mlp_out,
):
    tensor = lax.axis_size("tensor")
    dp_at, tensor_at = lax.axis_index("dp"), lax.axis_index("tensor")
    local, frames, patches, width = gen_tokens.shape
    windows = patches * tensor // AREA
    direct = tensor == 4 and windows == 4
    split = max(tensor // windows, 1)
    clips = -(-local // split)
    place = tensor_at.astype(jnp.int32)[None]
    vectors = [v.reshape(1, -1) for v in (ln1_gain, ln1_bias, ln2_gain, ln2_bias, ln3_gain, ln3_bias, logit_gain)]
    g1, b1, g2, b2, g3, b3, logit = vectors

    step_value = train_step.astype(F32)
    ramp = adv_weight * step_value / (step_value + HALF)

    def mine(values):
        return lax.dynamic_slice_in_dim(pad_clips(values, split), tensor_at % split * clips, clips, 0)

    counts = (mine(gen_frames), mine(disc_frames))
    signs = (2 * mine(disc_labels) - 1).astype(F32)

    def flat(x):
        return x.reshape(x.shape[0], -1, width)

    def to_window(x, aspect):
        if direct:
            return join(window_source, place, aspect, flat(x), exchange(pack(place, aspect, flat(x))))
        return flat(gather_window(x, aspect, split))

    def to_raster(y, aspect):
        if direct:
            by_frame = y.reshape(clips, frames, AREA, width)
            parts = [by_frame[:, :, a:b].reshape(clips, -1, width) for a, b in ((32, 64), (16, 32), (48, 64))]
            return join(raster_source, place, aspect, y, exchange(parts)).reshape(gen_tokens.shape)
        return gather_raster(y.reshape(clips, frames, AREA, width), aspect, split, patches)

    x_gen = to_window(gen_tokens, gen_aspect)
    space_w = gather_weight(spatial_qkv.reshape(3 * width, -1)).reshape(tensor, 3, width, -1)
    space_wo = gather_weight(spatial_out).reshape(width, width)
    time_w = gather_weight(temporal_qkv.reshape(3 * width, -1)).reshape(tensor, 3, width, -1)
    time_wo = gather_weight(temporal_out).reshape(width, width)
    x_disc = to_window(disc_tokens, disc_aspect)
    if direct:
        dy, *parts = pack_grad(place, gen_aspect, gen_frames, ramp, flat(rec_grad), flat(adv_grad))
        dy = join(window_source, place, gen_aspect, dy, exchange(parts))
    else:
        live = jnp.arange(frames, dtype=jnp.int32)[None, :] < gen_frames[:, None]
        total = rec_grad.astype(F32) + ramp[0] * adv_grad.astype(F32)
        dy = jnp.where(live[:, :, None, None], total, 0.0).astype(BF16)
        dy = flat(gather_window(dy, gen_aspect, split))
    w_in = gather_weight(mlp_in)
    w_out = gather_weight(mlp_out)

    xs = (x_gen, x_disc)
    space = [space_forward(x, g1, b1, space_w, space_wo) for x in xs]
    time = [time_forward(s[0], g2, b2, time_w, time_wo) for s in space]
    ff = [
        mlp(bool(i), signs, counts[i], t[0], g3, b3, w_in, w_out, logit if i else dy) for i, t in enumerate(time)
    ]
    outs = [to_raster(m[0], a) for m, a in zip(ff, (gen_aspect, disc_aspect))]
    grad_in = product_sum([m[2] for m in ff], [m[5] for m in ff])
    grad_out = product_sum([m[4] for m in ff], [m[3] for m in ff])
    tb = [time_backward(m[1], s[0], g2, time_w, time_wo, t[2], t[3]) for m, s, t in zip(ff, space, time)]
    time_grad = product_sum([t[1] for t in time], [b[2] for b in tb])
    time_out_grad = product_sum([b[1] for b in tb], [t[4] for t in time])
    sb = [space_backward(b[0], x, g1, space_w, space_wo, s[2], s[3]) for b, x, s in zip(tb, xs, space)]
    ins = [to_raster(b[0], a) for b, a in zip(sb, (gen_aspect, disc_aspect))]
    space_grad = product_sum([s[1] for s in space], [b[2] for b in sb])
    space_out_grad = product_sum([b[1] for b in sb], [s[4] for s in space])

    hidden = mlp_in.shape[1]
    in_share, out_share = scatter_grad(
        [grad_in.reshape(width, 1, tensor, hidden), grad_out.reshape(width, 1, tensor, hidden)]
    )
    part = width // tensor
    time_share, time_out_share = scatter_grad(
        [time_grad.reshape(width, 3, tensor, part), time_out_grad.reshape(width, 1, tensor, part)]
    )
    space_share, space_out_share = scatter_grad(
        [space_grad.reshape(width, 3, tensor, part), space_out_grad.reshape(width, 1, tensor, part)]
    )

    small = jnp.stack(
        [
            jnp.sum(jnp.concatenate([stage[0][k], stage[1][k]], axis=0), axis=0)
            for stage, k in ((sb, 3), (sb, 4), (tb, 3), (tb, 4), (ff, 6), (ff, 7))
        ]
    )
    small = lax.psum(small, ("dp", "tensor"))
    piece = width // lax.axis_size("dp")
    small = lax.dynamic_slice_in_dim(small, dp_at * piece, piece, 1)

    return (
        outs[0], ins[0], outs[1], ins[1],
        small[0], small[1], jnp.transpose(space_share, (1, 0, 2)), space_out_share[:, 0].T,
        small[2], small[3], jnp.transpose(time_share, (1, 0, 2)), time_out_share[:, 0].T,
        small[4], small[5], in_share[:, 0], out_share[:, 0].T,
    )


def solution(mesh):
    tokens = P("dp", None, "tensor", None)
    vector, clip = P(), P("dp")
    qkv, rows, cols = P(None, None, "tensor"), P("tensor", None), P(None, "tensor")
    in_specs = (
        (tokens,) * 3 + (clip,) * 2 + (tokens,) + (clip,) * 3 + (vector,) * 5
        + (qkv, rows, vector, vector, qkv, rows, vector, vector, cols, rows)
    )
    block = (clip, clip, P(None, "dp", "tensor"), P("tensor", "dp"))
    out_specs = (tokens,) * 4 + block * 2 + (clip, clip, P("dp", "tensor"), P("tensor", "dp"))
    return jax.shard_map(shards, mesh=mesh, in_specs=in_specs, out_specs=out_specs, check_vma=False)
```

```python
from functools import partial
import math

import jax
import jax.numpy as jnp
from jax import lax
from jax.experimental import pallas as pl
from jax.experimental.pallas import tpu as pltpu
from jax.sharding import PartitionSpec as P

HEAD_DIM = 64
WIN = 8
AREA = WIN * WIN
HALF = 5000
EPS = 1e-05
F32 = jnp.float32
BF16 = jnp.bfloat16
VMEM_LIMIT = 56 * 1024 * 1024

NT = (((1,), (1,)), ((), ()))
TN = (((0,), (0,)), ((), ()))


def dot(lhs, rhs):
    return jnp.dot(lhs, rhs, preferred_element_type=F32)


def dot_nt(lhs, rhs):
    return lax.dot_general(lhs, rhs, NT, preferred_element_type=F32)


def dot_tn(lhs, rhs):
    return lax.dot_general(lhs, rhs, TN, preferred_element_type=F32)


def normalize(value):
    average = jnp.mean(value, axis=-1, keepdims=True)
    centred = value - average
    variance = jnp.mean(centred * centred, axis=-1, keepdims=True)
    scale = lax.rsqrt(variance + EPS)
    return centred * scale, scale


def norm_backward(unit, scale, gain, grad):
    scaled = grad * gain
    inner = scaled - jnp.mean(scaled, axis=-1, keepdims=True)
    return scale * (inner - unit * jnp.mean(scaled * unit, axis=-1, keepdims=True))


def row_sums(values):
    return jnp.sum(values.reshape(-1, 8, values.shape[-1]), axis=0)


ANY = pl.BlockSpec(memory_space=pl.ANY)
SMEM = pl.BlockSpec(memory_space=pltpu.SMEM)


def run(kernel, microseconds, grid, ins, in_specs, outs, out_specs, scratch=(), after=(), prefetch=0):
    ins, after = tuple(ins), tuple(after)
    count = len(ins)

    def body(*refs):
        kernel(*refs[:count], *refs[count + len(after) :])

    return pl.pallas_call(
        body,
        grid_spec=pltpu.PrefetchScalarGridSpec(
            num_scalar_prefetch=prefetch,
            grid=grid,
            in_specs=list(in_specs) + [ANY] * len(after),
            out_specs=list(out_specs),
            scratch_shapes=list(scratch),
        ),
        out_shape=list(outs),
        cost_estimate=pl.CostEstimate(flops=int(microseconds * 2.5e9), bytes_accessed=0, transcendentals=0),
        compiler_params=pltpu.CompilerParams(
            dimension_semantics=("arbitrary",) * len(grid), vmem_limit_bytes=VMEM_LIMIT
        ),
    )(*ins, *after)


def shape(dims, dtype=BF16):
    return jax.ShapeDtypeStruct(tuple(dims), dtype)


def whole(dims):
    zeros = (0,) * len(dims)
    return pl.BlockSpec(tuple(dims), lambda i: zeros)


def per_clip(dims):
    zeros = (0,) * (len(dims) - 1)
    return pl.BlockSpec((1,) + tuple(dims[1:]), lambda i: (i,) + zeros)


def join_rows(w_ref, part):
    return jnp.concatenate(
        [
            jnp.concatenate([part(w_ref, i, j) for j in range(w_ref.shape[1])], axis=1)
            for i in range(w_ref.shape[0])
        ],
        axis=0,
    )


def head_weight(w_ref, m):
    return join_rows(w_ref, lambda ref, i, j: ref[i, j, :, m * 128 : (m + 1) * 128])


def out_weight(w_ref):
    part = w_ref.shape[2] // 4
    return jnp.concatenate(
        [
            jnp.concatenate([w_ref[i, j, c * part : (c + 1) * part, 384:512] for c in range(4)], axis=1)
            for j in range(w_ref.shape[1])
            for i in range(w_ref.shape[0])
        ],
        axis=0,
    )


def hidden_weight(w_ref, j, n):
    part = w_ref.shape[2] // 2
    return jnp.concatenate([w_ref[i, j, n * part : (n + 1) * part, :] for i in range(w_ref.shape[0])], axis=0)


def head_mask(dtype):
    rows = lax.broadcasted_iota(jnp.int32, (256, 256), 0) // HEAD_DIM
    cols = lax.broadcasted_iota(jnp.int32, (256, 256), 1) // HEAD_DIM
    return jnp.where(rows == cols, 1.0, 0.0).astype(dtype)


def spread(values, mask):
    return jnp.concatenate([values] * 4, axis=0) * mask


def pair_product(scores, values, low_lane):
    parts = []
    for c in range(2):
        full = dot_tn(scores[:, c * 128 : (c + 1) * 128], values[:, c * 128 : (c + 1) * 128])
        parts.append(jnp.where(low_lane, full[:64], full[64:]))
    return jnp.concatenate(parts, axis=1)


def one_hot(source, count):
    rows = source.shape[0]
    inside = lax.broadcasted_iota(jnp.int32, (rows, count), 0) % 8
    cols = lax.broadcasted_iota(jnp.int32, (rows, count), 1)
    return jnp.where((source >= 0) & (cols == source * 8 + inside), 1.0, 0.0).astype(BF16)


def chunk_ids():
    return lax.broadcasted_iota(jnp.int32, (AREA, 1), 0) // 8


def send_source(aspect, t):
    c = chunk_ids()
    square = jnp.where(c < 4, 2 * c + 1 - t % 2, -1)
    wide = jnp.where(
        c < 2, 4 * c + (t ^ 1), jnp.where(c < 4, -1, jnp.where(c < 6, 4 * (c - 4) + (t ^ 2), 4 * (c - 6) + (t ^ 3)))
    )
    return jnp.where(aspect == 0, square, jnp.where(aspect == 1, wide, -1))


def window_source(aspect, t):
    c = chunk_ids()
    square = jnp.where(c < 4, 2 * c + t % 2, c + 4)
    wide = jnp.where(c < 2, 4 * c + t, jnp.where(c < 4, c + 10, jnp.where(c < 6, c + 4, c + 8)))
    return jnp.where(aspect == 0, square, jnp.where(aspect == 1, wide, c))


def raster_source(aspect, t):
    c = chunk_ids()
    square = c // 2 + jnp.where(c % 2 == t % 2, 0, 8)
    way = (c % 4) ^ t
    wide = c // 4 + jnp.where(way == 0, 0, jnp.where(way == 1, 8, jnp.where(way == 2, 12, 14)))
    return jnp.where(aspect == 0, square, jnp.where(aspect == 1, wide, c))


def write_sends(values, refs):
    if not refs:
        return
    for f in range(values.shape[0] // AREA):
        base = f * AREA
        refs[0][0, f * 32 : (f + 1) * 32, :] = values[base + 32 : base + 64]
        refs[1][0, f * 16 : (f + 1) * 16, :] = values[base + 16 : base + 32]
        refs[2][0, f * 16 : (f + 1) * 16, :] = values[base + 48 : base + 64]


def pack_rows(values, select, refs):
    for f in range(values.shape[0] // AREA):
        moved = dot(select, values[f * AREA : (f + 1) * AREA]).astype(BF16)
        refs[0][0, f * 32 : (f + 1) * 32, :] = moved[:32]
        refs[1][0, f * 16 : (f + 1) * 16, :] = moved[32:48]
        refs[2][0, f * 16 : (f + 1) * 16, :] = moved[48:]


def join_parts(source, own_ref, part_refs, out_ref):
    select = one_hot(source, 2 * AREA)
    for f in range(out_ref.shape[1] // AREA):
        rows = [own_ref[0, f * AREA : (f + 1) * AREA, :]]
        rows += [ref[0, f * size : (f + 1) * size, :] for ref, size in zip(part_refs, (32, 16, 16))]
        out_ref[0, f * AREA : (f + 1) * AREA, :] = dot(select, jnp.concatenate(rows, axis=0)).astype(BF16)


def pack_kernel(place_ref, aspect_ref, x_ref, *send_refs):
    select = one_hot(send_source(aspect_ref[pl.program_id(0)], place_ref[0]), AREA)
    pack_rows(x_ref[0], select, send_refs)


def pack_grad_kernel(place_ref, aspect_ref, count_ref, ramp_ref, rec_ref, adv_ref, dy_ref, *send_refs):
    clip = pl.program_id(0)
    frame = lax.broadcasted_iota(jnp.int32, (rec_ref.shape[1], 1), 0) // AREA
    total = rec_ref[0].astype(F32) + ramp_ref[0] * adv_ref[0].astype(F32)
    dy_ref[0] = jnp.where(frame < count_ref[clip], total, 0.0).astype(BF16)
    select = one_hot(send_source(aspect_ref[clip], place_ref[0]), AREA)
    pack_rows(dy_ref[0], select, send_refs)


def join_kernel(place_ref, aspect_ref, own_ref, r1_ref, r2_ref, r3_ref, out_ref):
    source = raster_source(aspect_ref[pl.program_id(0)], place_ref[0])
    join_parts(source, own_ref, (r1_ref, r2_ref, r3_ref), out_ref)


def send_shapes(x):
    clips, rows, width = x.shape
    return [shape((clips, rows // part, width)) for part in (2, 4, 4)]


def late_spec(w, rows, index):
    if w.shape[2] != 192:
        return whole(w.shape)
    return pl.BlockSpec(w.shape[:2] + (rows, w.shape[3]), lambda i: (0, 0, index, 0))


def clip_specs(arrays):
    return [per_clip(a.shape) for a in arrays]


def whole_specs(arrays):
    return [whole(a.shape) for a in arrays]


def pack(place, aspect, x, after=()):
    outs = send_shapes(x)
    return run(
        pack_kernel, 3, x.shape[:1], (place, aspect, x), [SMEM, SMEM, per_clip(x.shape)], outs, clip_specs(outs), after=after
    )


def pack_grad(place, aspect, count, ramp, rec, adv, after=()):
    outs = [shape(rec.shape)] + send_shapes(rec)
    ins = (place, aspect, count, ramp, rec, adv)
    return run(
        pack_grad_kernel, 4, rec.shape[:1], ins, [SMEM] * 4 + clip_specs((rec, adv)), outs, clip_specs(outs), after=after
    )


def join_raster(place, aspect, own, parts, after=()):
    outs = [shape(own.shape)]
    ins = (place, aspect, own, *parts)
    return run(join_kernel, 4, own.shape[:1], ins, [SMEM] * 2 + clip_specs(ins[2:]), outs, clip_specs(outs), after=after)[0]


def exchange(parts):
    return tuple(swap(part, "tensor", way) for way, part in zip((1, 2, 3), parts))


def swap(x, axis, way):
    return lax.ppermute(x, axis, [(i, i ^ way) for i in range(lax.axis_size(axis))])


def space_forward_kernel(parts, place_ref, aspect_ref, x_ref, *refs):
    part_refs = refs[:parts]
    gain_ref, bias_ref, w_ref, x1_ref, a_ref, qkv_ref, p_ref, o_ref, *joined = refs[parts:]
    rows = x_ref.shape[1]
    if parts:
        join_parts(window_source(aspect_ref[pl.program_id(0)], place_ref[0]), x_ref, part_refs, joined[0])
        x = joined[0][0].astype(F32)
    else:
        x = x_ref[0].astype(F32)
    unit, _ = normalize(x)
    a_ref[0] = (unit * gain_ref[...] + bias_ref[...]).astype(BF16)
    for j in range(3):
        qkv_ref[0, :, j * 512 : (j + 1) * 512] = dot(a_ref[0], head_weight(w_ref, j)).astype(BF16)
    mask = head_mask(BF16)
    low_lane = lax.broadcasted_iota(jnp.int32, (64, 128), 1) < HEAD_DIM
    for w in range(rows // AREA):
        for g in range(2):
            sl = slice(w * AREA, (w + 1) * AREA)
            q, k, v = (
                qkv_ref[0, sl, j * 512 + g * 256 : j * 512 + (g + 1) * 256] for j in range(3)
            )
            s = dot_nt(k, spread(q, mask)) * 0.125
            e = jnp.exp(s - jnp.max(s, axis=0, keepdims=True))
            p = (e * (1.0 / jnp.sum(e, axis=0, keepdims=True))).astype(BF16)
            p_ref[0, 2 * w + g] = p
            o_ref[0, sl, g * 256 : (g + 1) * 256] = pair_product(p, v, low_lane).astype(BF16)
    x1_ref[0] = x + dot(o_ref[0], out_weight(w_ref))


def space_forward(place, aspect, x, parts, gain, bias, w, after=()):
    clips, rows, width = x.shape
    outs = [
        shape((clips, rows, width), F32),
        shape((clips, rows, width)),
        shape((clips, rows, 3 * width)),
        shape((clips, 2 * rows // AREA, AREA, 256)),
        shape((clips, rows, width)),
    ] + [shape(x.shape)] * bool(parts)
    vectors = (gain, bias, w)
    return run(
        partial(space_forward_kernel, len(parts)), 15, (clips,), (place, aspect, x, *parts, *vectors),
        [SMEM] * 2 + clip_specs((x, *parts)) + whole_specs(vectors), outs, clip_specs(outs), after=after,
    )


def space_backward_kernel(
    dx1_ref, x_ref, gain_ref, w_ref, qkv_ref, p_ref,
    dx0_ref, low_ref, dqkv_ref, dg_ref, db_ref, *rest
):
    *send_refs, do_ref = rest

    @pl.when(pl.program_id(0) == 0)
    def _():
        dg_ref[...] = jnp.zeros_like(dg_ref)
        db_ref[...] = jnp.zeros_like(db_ref)

    rows = x_ref.shape[1]
    low_ref[0] = dx1_ref[0].astype(BF16)
    do_ref[...] = dot_nt(low_ref[0], out_weight(w_ref)).astype(BF16)
    mask = head_mask(BF16)
    low_lane = lax.broadcasted_iota(jnp.int32, (64, 128), 1) < HEAD_DIM
    for w in range(rows // AREA):
        for g in range(2):
            sl = slice(w * AREA, (w + 1) * AREA)
            q, k, v = (
                qkv_ref[0, sl, j * 512 + g * 256 : j * 512 + (g + 1) * 256] for j in range(3)
            )
            p = p_ref[0, 2 * w + g]
            dob = spread(do_ref[sl, g * 256 : (g + 1) * 256], mask)
            dv = dot(p, dob)
            dp = dot_nt(v, dob)
            p = p.astype(F32)
            weighted = p * dp
            ds = (weighted - p * jnp.sum(weighted, axis=0, keepdims=True)).astype(BF16)
            dk = dot(ds, spread(q, mask)) * 0.125
            dq = pair_product(ds, k, low_lane) * 0.125
            for j, part in enumerate((dq, dk, dv)):
                dqkv_ref[0, sl, j * 512 + g * 256 : j * 512 + (g + 1) * 256] = part.astype(BF16)
    da = sum(dot_nt(dqkv_ref[0, :, j * 512 : (j + 1) * 512], head_weight(w_ref, j)) for j in range(3))
    unit, scale = normalize(x_ref[0].astype(F32))
    dg_ref[...] += row_sums(da * unit)
    db_ref[...] += row_sums(da)
    dx0_ref[0] = (dx1_ref[0] + norm_backward(unit, scale, gain_ref[...], da)).astype(BF16)
    write_sends(dx0_ref[0], send_refs)


def space_backward(direct, dx1, x, gain, w, qkv, p, after=()):
    clips, rows, width = x.shape
    sends = send_shapes(x) if direct else []
    outs = [shape(x.shape), shape(x.shape), shape(qkv.shape)]
    sums = [shape((8, width), F32)] * 2
    return run(
        space_backward_kernel, 15, (clips,), (dx1, x, gain, w, qkv, p),
        clip_specs((dx1, x)) + whole_specs((gain, w)) + clip_specs((qkv, p)),
        outs + sums + sends, clip_specs(outs) + whole_specs(sums) + clip_specs(sends),
        [pltpu.VMEM((rows, width), BF16)], after,
    )


def head_select(frame):
    rows = lax.broadcasted_iota(jnp.int32, (512, 128), 0) // HEAD_DIM
    cols = lax.broadcasted_iota(jnp.int32, (512, 128), 1) - 8 * frame
    return jnp.where(rows == cols, 1.0, 0.0).astype(BF16)


def head_expand(frame):
    rows = lax.broadcasted_iota(jnp.int32, (128, 512), 0) - 8 * frame
    cols = lax.broadcasted_iota(jnp.int32, (128, 512), 1) // HEAD_DIM
    return jnp.where(rows == cols, 1.0, 0.0).astype(BF16)


def head_sums(products, selector):
    high = products.astype(BF16)
    rest = (products - high.astype(F32)).astype(BF16)
    return dot(high, selector) + dot(rest, selector)


def time_scores(frames, left, right):
    totals = [None] * frames
    for t in range(frames):
        lhs = left(t).astype(F32)
        stacked = jnp.concatenate([lhs * right(f).astype(F32) for f in range(t + 1)], axis=0)
        sums = head_sums(stacked, head_select(t))
        for f in range(t + 1):
            part = sums[f * AREA : (f + 1) * AREA]
            totals[f] = part if totals[f] is None else totals[f] + part
    return totals


def time_forward_kernel(x_ref, gain_ref, bias_ref, w_ref, x2_ref, a_ref, qkv_ref, p_ref, o_ref):
    rows = x_ref.shape[1]
    frames = rows // AREA
    x = x_ref[0]
    unit, _ = normalize(x)
    a_ref[0] = (unit * gain_ref[...] + bias_ref[...]).astype(BF16)
    for j in range(3):
        qkv_ref[0, :, j * 512 : (j + 1) * 512] = dot(a_ref[0], head_weight(w_ref, j)).astype(BF16)

    def part(j):
        return lambda f: qkv_ref[0, f * AREA : (f + 1) * AREA, j * 512 : (j + 1) * 512]

    scores = time_scores(frames, part(0), part(1))
    lane = lax.broadcasted_iota(jnp.int32, (AREA, 128), 1)
    scores = [jnp.where(lane >= 8 * f, s * 0.125, -1e30) for f, s in enumerate(scores)]
    top = scores[0]
    for s in scores[1:]:
        top = jnp.maximum(top, s)
    exps = [jnp.exp(s - top) for s in scores]
    inverse = 1.0 / sum(exps)
    probs = [e * inverse for e in exps]
    for f in range(frames):
        p_ref[0, f * AREA : (f + 1) * AREA, :] = probs[f]
    low = [p.astype(BF16) for p in probs]
    values = part(2)
    for t in range(frames):
        wide = dot(jnp.concatenate(low[: t + 1], axis=0), head_expand(t))
        total = None
        for f in range(t + 1):
            term = wide[f * AREA : (f + 1) * AREA] * values(f).astype(F32)
            total = term if total is None else total + term
        o_ref[0, t * AREA : (t + 1) * AREA, :] = total.astype(BF16)
    x2_ref[0] = x + dot(o_ref[0], out_weight(w_ref))


def time_forward(x, gain, bias, w, after=()):
    clips, rows, width = x.shape
    outs = [
        shape((clips, rows, width), F32),
        shape((clips, rows, width)),
        shape((clips, rows, 3 * width)),
        shape((clips, rows, 128), F32),
        shape((clips, rows, width)),
    ]
    ins = (x, gain, bias, w)
    return run(
        time_forward_kernel, 10, (clips,), ins, [per_clip(x.shape)] + whole_specs((gain, bias)) + [late_spec(w, 64, 2)], outs,
        clip_specs(outs), after=after,
    )


def time_backward_kernel(
    dx2_ref, x_ref, gain_ref, w_ref, qkv_ref, p_ref,
    dx1_ref, low_ref, dqkv_ref, dg_ref, db_ref, do_ref,
):
    @pl.when(pl.program_id(0) == 0)
    def _():
        dg_ref[...] = jnp.zeros_like(dg_ref)
        db_ref[...] = jnp.zeros_like(db_ref)

    rows = x_ref.shape[1]
    frames = rows // AREA
    low_ref[0] = dx2_ref[0].astype(BF16)
    do_ref[...] = dot_nt(low_ref[0], out_weight(w_ref)).astype(BF16)

    def part(j):
        return lambda f: qkv_ref[0, f * AREA : (f + 1) * AREA, j * 512 : (j + 1) * 512]

    queries, key_rows, values = part(0), part(1), part(2)

    def grads(t):
        return do_ref[t * AREA : (t + 1) * AREA, :]

    dp = time_scores(frames, grads, values)
    probs = [p_ref[0, f * AREA : (f + 1) * AREA, :] for f in range(frames)]
    inner = sum(p * d for p, d in zip(probs, dp))
    ds = [(p * (d - inner)).astype(BF16) for p, d in zip(probs, dp)]
    low = [p.astype(BF16) for p in probs]
    dk = [None] * frames
    dv = [None] * frames
    for t in range(frames):
        wide = dot(jnp.concatenate(ds[: t + 1] + low[: t + 1], axis=0), head_expand(t))
        q, do = queries(t).astype(F32), grads(t).astype(F32)
        dq = None
        for f in range(t + 1):
            ds_wide = wide[f * AREA : (f + 1) * AREA]
            p_wide = wide[(t + 1 + f) * AREA : (t + 2 + f) * AREA]
            term = ds_wide * key_rows(f).astype(F32)
            dq = term if dq is None else dq + term
            dk[f] = ds_wide * q if dk[f] is None else dk[f] + ds_wide * q
            dv[f] = p_wide * do if dv[f] is None else dv[f] + p_wide * do
        dqkv_ref[0, t * AREA : (t + 1) * AREA, 0:512] = (dq * 0.125).astype(BF16)
    for f in range(frames):
        dqkv_ref[0, f * AREA : (f + 1) * AREA, 512:1024] = (dk[f] * 0.125).astype(BF16)
        dqkv_ref[0, f * AREA : (f + 1) * AREA, 1024:1536] = dv[f].astype(BF16)
    da = sum(dot_nt(dqkv_ref[0, :, j * 512 : (j + 1) * 512], head_weight(w_ref, j)) for j in range(3))
    unit, scale = normalize(x_ref[0])
    dg_ref[...] += row_sums(da * unit)
    db_ref[...] += row_sums(da)
    dx1_ref[0] = dx2_ref[0] + norm_backward(unit, scale, gain_ref[...], da)


def time_backward(dx2, x, gain, w, qkv, p, after=()):
    clips, rows, width = x.shape
    outs = [shape(x.shape, F32), shape(x.shape), shape(qkv.shape)]
    sums = [shape((8, width), F32)] * 2
    return run(
        time_backward_kernel, 12, (clips,), (dx2, x, gain, w, qkv, p),
        clip_specs((dx2, x)) + [whole(gain.shape), late_spec(w, 64, 2)] + clip_specs((qkv, p)),
        outs + sums, clip_specs(outs) + whole_specs(sums), [pltpu.VMEM((rows, width), BF16)], after,
    )


def gelu_parts(h):
    e = jnp.exp(h * h * -0.5)
    t = 1.0 / (1.0 + (0.3275911 * math.sqrt(0.5)) * jnp.abs(h))
    tail = t * (0.127414796 + t * (-0.142248368 + t * (0.7107068705 + t * (-0.7265760135 + t * 0.5307027145)))) * e
    cdf = jnp.where(h >= 0, 1.0 - tail, tail)
    return h * cdf, cdf + h * (e * 0.3989422804014327)


def mlp_kernel(
    disc, parts, sign_ref, count_ref, place_ref, aspect_ref, x_ref, gain_ref, bias_ref, w_ref, extra_ref, *rest
):
    part_refs = rest[:parts]
    y_ref, dx_ref, c_ref, u_ref, gb_ref, dh_ref, dg_ref, db_ref, *send_refs, slope_ref = rest[parts:]

    @pl.when(pl.program_id(0) == 0)
    def _():
        dg_ref[...] = jnp.zeros_like(dg_ref)
        db_ref[...] = jnp.zeros_like(db_ref)

    rows = x_ref.shape[1]
    tiles = w_ref.shape[1]
    x = x_ref[0]
    unit, scale = normalize(x)
    c_ref[0] = (unit * gain_ref[...] + bias_ref[...]).astype(BF16)
    y = x
    span = w_ref.shape[3]
    for j in range(tiles):
        h = dot(c_ref[0], hidden_weight(w_ref, j, 0))
        active, slope = gelu_parts(h)
        u_ref[0, :, j * span : (j + 1) * span] = active.astype(BF16)
        slope_ref[:, j * span : (j + 1) * span] = slope.astype(BF16)
        y = y + dot(u_ref[0, :, j * span : (j + 1) * span], hidden_weight(w_ref, j, 1))
    y_ref[0] = y.astype(BF16)
    write_sends(y_ref[0], send_refs)
    if disc:
        clip = pl.program_id(0)
        sign = sign_ref[clip]
        frame = lax.broadcasted_iota(jnp.int32, (rows, 1), 0) // AREA
        live = jnp.where(frame < count_ref[clip], -sign, 0.0)
        signed = sign * extra_ref[...]
        dy = live * extra_ref[...] * jax.nn.sigmoid(1.0 - signed * y)
        gb_ref[0] = dy.astype(BF16)
    else:
        if parts:
            join_parts(window_source(aspect_ref[pl.program_id(0)], place_ref[0]), extra_ref, part_refs, gb_ref)
        else:
            gb_ref[0] = extra_ref[0]
        dy = gb_ref[0].astype(F32)
    dc = None
    for j in range(tiles):
        du = dot_nt(gb_ref[0], hidden_weight(w_ref, j, 1))
        dh = (du * slope_ref[:, j * span : (j + 1) * span].astype(F32)).astype(BF16)
        dh_ref[0, :, j * span : (j + 1) * span] = dh
        term = dot_nt(dh_ref[0, :, j * span : (j + 1) * span], hidden_weight(w_ref, j, 0))
        dc = term if dc is None else dc + term
    dg_ref[...] += row_sums(dc * unit)
    db_ref[...] += row_sums(dc)
    dx_ref[0] = dy + norm_backward(unit, scale, gain_ref[...], dc)


def mlp(direct, disc, sign, count, place, aspect, x, gain, bias, w, extra, parts=(), after=()):
    clips, rows, width = x.shape
    hidden = w.shape[1] * w.shape[3]
    sends = send_shapes(x) if direct else []
    outs = [shape(x.shape), shape(x.shape, F32), shape(x.shape)]
    outs += [shape((clips, rows, hidden)), shape(x.shape), shape((clips, rows, hidden))]
    sums = [shape((8, width), F32)] * 2
    ins = (sign, count, place, aspect, x, gain, bias, w, extra, *parts)
    return run(
        partial(mlp_kernel, disc, len(parts)), 20, (clips,), ins,
        [SMEM] * 4 + [per_clip(x.shape)] + whole_specs((gain, bias)) + [late_spec(w, 128, 0)]
        + (whole_specs if disc else clip_specs)((extra,)) + clip_specs(parts),
        outs + sums + sends, clip_specs(outs) + whole_specs(sums) + clip_specs(sends),
        [pltpu.VMEM((rows, hidden), BF16)], after,
    )


def window_maps(aspect, tokens_frame):
    grid_side = math.isqrt(tokens_frame)
    grid_width = jnp.where(
        aspect == 1, 2 * grid_side, jnp.where(aspect == 2, grid_side // 2, grid_side)
    ).astype(jnp.int32)[:, None]
    across = grid_width // WIN
    places = jnp.arange(tokens_frame, dtype=jnp.int32)[None, :]
    window = places // AREA
    inside = places % AREA
    grid_row = window // across * WIN + inside // WIN
    grid_col = window % across * WIN + inside % WIN
    forward_order = grid_row * grid_width + grid_col
    raster_row = places // grid_width
    raster_col = places % grid_width
    back_order = (
        (raster_row // WIN * across + raster_col // WIN) * AREA + raster_row % WIN * WIN + raster_col % WIN
    )
    return (forward_order, back_order)


def reorder(values, order):
    return jax.vmap(partial(jnp.take, axis=1))(values, order)


def pad_clips(values, split):
    return jnp.pad(values, [(0, -values.shape[0] % split)] + [(0, 0)] * (values.ndim - 1))


def gather_window(x, aspect, split):
    whole_x = pad_clips(lax.all_gather(x, "tensor", axis=2, tiled=True), split)
    aspect = pad_clips(aspect, split)
    t = lax.axis_index("tensor")
    clips = aspect.shape[0] // split
    mine = lax.dynamic_slice_in_dim(whole_x, t % split * clips, clips, 0)
    kinds = lax.dynamic_slice_in_dim(aspect, t % split * clips, clips, 0)
    order, _ = window_maps(kinds, whole_x.shape[2])
    return reorder(mine, lax.dynamic_slice_in_dim(order, t // split * AREA, AREA, 1))


def gather_raster(y, aspect, split, patches):
    every = lax.all_gather(y, "tensor", axis=0)
    count, clips, frames, _, width = every.shape
    every = every.reshape(count // split, split, clips, frames, AREA, width)
    every = jnp.transpose(every, (1, 2, 3, 0, 4, 5)).reshape(split * clips, frames, -1, width)
    _, back = window_maps(aspect, every.shape[2])
    t = lax.axis_index("tensor")
    return reorder(every[: aspect.shape[0]], lax.dynamic_slice_in_dim(back, t * patches, patches, 1))


def attention_piece(d, w_ref, wo_ref):
    rows = w_ref.shape[1] // 8
    part = wo_ref.shape[0] // 8
    qkv = [w_ref[m, pl.ds(pl.multiple_of(d * rows, rows), rows), :] for m in range(3)]
    out = wo_ref[pl.ds(pl.multiple_of(d * part, part), part), :]
    squares = [out[:, c * 128 : (c + 1) * 128] for c in range(out.shape[1] // 128)]
    return jnp.concatenate(qkv + [jnp.concatenate(squares, axis=0)], axis=1)


def pack_weights_kernel(place_ref, sw_ref, swo_ref, tw_ref, two_ref, w_in_ref, w_out_ref, first_ref, rest_ref):
    d = place_ref[1]
    first_ref[...] = attention_piece(d, sw_ref, swo_ref)
    rows = pl.ds(pl.multiple_of(d * 64, 64), 64)
    rest_ref[0:64, :] = w_in_ref[rows, :]
    rest_ref[64:128, :] = w_out_ref[rows, :]
    rest_ref[128:192, :] = attention_piece(d, tw_ref, two_ref)


def pack_weights(place, *weights):
    outs = [shape((64, 512)), shape((192, 512))]
    return run(pack_weights_kernel, 2, (1,), (place, *weights), [SMEM] + whole_specs(weights), outs, whole_specs(outs))


def stack_kernel(*refs):
    ins, outs = refs[:4], refs[4:]
    for j, ref in enumerate(ins):
        at = 0
        for out in outs:
            rows = out.shape[1]
            out[j] = ref[at : at + rows]
            at += rows


def stack_pieces(pieces, rows, after=()):
    outs = [shape((4, count) + pieces[0].shape[1:]) for count in rows]
    return run(stack_kernel, 2, (1,), pieces, whole_specs(pieces), outs, whole_specs(outs), after=after)


def order_kernel(place_ref, even_ref, odd_ref, out_ref):
    t, d = place_ref[0], place_ref[1]
    for i in range(4):
        for j in range(4):
            out_ref[d ^ (2 * i), t ^ j] = even_ref[i, j]
            out_ref[d ^ (2 * i + 1), t ^ j] = odd_ref[i, j]


def gather_pieces(place, across, after=()):
    even = stack_pieces([across] + [swap(across, "dp", k) for k in (2, 4, 6)], (4,), after)[0]
    ins = (place, even, swap(even, "dp", 1))
    outs = [shape((8,) + across.shape)]
    return run(order_kernel, 2, (1,), ins, [SMEM] + whole_specs(ins[1:]), outs, whole_specs(outs))[0]


def gather_shard(shard):
    rows = shard.shape[0] // lax.axis_size("dp")
    piece = lax.dynamic_slice_in_dim(shard, lax.axis_index("dp") * rows, rows, 0)
    whole_w = lax.all_gather(piece, ("tensor", "dp"), axis=0, tiled=True)
    return whole_w.reshape((-1,) + shard.shape)


def gather_attention(w, wo):
    width = wo.shape[1]
    heads = gather_shard(w.reshape(-1, w.shape[2])).reshape((-1,) + w.shape)
    heads = jnp.moveaxis(heads, 0, 2).reshape(3, width, 4, -1).transpose(2, 1, 0, 3).reshape(4, width, -1)
    out = gather_shard(wo).reshape(4, width // 4, 4, width // 4).transpose(0, 2, 1, 3).reshape(4, width, -1)
    return jnp.concatenate([heads, out], axis=2)[None]


def gather_hidden(w_in, w_out):
    columns = jnp.moveaxis(gather_shard(w_in), 0, 1).reshape(w_in.shape[0], 4, -1)
    rows = gather_shard(w_out).reshape(4, -1, w_out.shape[1])
    return jnp.concatenate([jnp.moveaxis(columns, 1, 0), rows], axis=1)[None]


def transpose_rows(left_refs, turned_ref):
    at = 0
    for ref in left_refs:
        rows = ref.shape[0]
        turned_ref[:, at : at + rows] = ref[...].T
        at += rows


def product_rows(turned_ref, right_refs, cols):
    total, at = None, 0
    for ref in right_refs:
        rows = ref.shape[0]
        term = dot(turned_ref[:, at : at + rows], ref[:, cols])
        total = term if total is None else total + term
        at += rows
    return total


def attention_grad_kernel(count, relative, place_ref, *refs):
    a, dqkv, low, o = (refs[i * count : (i + 1) * count] for i in range(4))
    *norms, turned_ref, block_ref = refs[4 * count :]
    split = 2 if relative else 1
    norms, out_refs = norms[:-split], norms[-split:]

    def place_block(cols):
        for k in range(8):
            at = (place_ref[1] ^ k) * 64 if relative else k * 64
            rows = pl.ds(pl.multiple_of(at, 64), 64)
            for j in range(4):
                lanes = pl.ds(pl.multiple_of((place_ref[0] ^ j) * 128, 128), 128)
                out_refs[k % split][k // split, j, 0:64, cols] = block_ref[rows, lanes].astype(BF16)

    transpose_rows(a, turned_ref)
    for m in range(3):
        block_ref[...] = product_rows(turned_ref, dqkv, slice(m * 512, (m + 1) * 512))
        place_block(slice(m * 128, (m + 1) * 128))
    transpose_rows(low, turned_ref)
    block_ref[...] = product_rows(turned_ref, o, slice(None))
    place_block(slice(384, 512))
    if norms:
        sums = [jnp.sum(n[...] + m[...], axis=0, keepdims=True) for n, m in zip(norms[::2], norms[1::2])]
        sums = jnp.concatenate(sums + [jnp.zeros((16 - len(sums), 512), F32)], axis=0).astype(BF16)
        for ref in out_refs:
            for k in range(ref.shape[0]):
                for j in range(4):
                    ref[k, j, 64:80, :] = sums


def attention_grad(relative, place, block, norms=(), after=()):
    flats = [v.reshape(-1, v.shape[-1]) for kind in block for v in kind]
    count = len(block[0])
    depth = sum(f.shape[0] for f in flats[:count])
    ins = (place, *flats, *norms)
    outs = [shape((4, 4, 80, 512))] * 2 if relative else [shape((8, 4, 64, 512))]
    return run(
        partial(attention_grad_kernel, count, relative), 11, (1,), ins, [SMEM] + whole_specs(ins[1:]), outs, whole_specs(outs),
        [pltpu.VMEM((512, depth), BF16), pltpu.VMEM((512, 512), F32)], after,
    )


def mlp_grad_kernel(count, place_ref, *refs):
    c, dh, gb, u = (refs[i * count : (i + 1) * count] for i in range(4))
    out_ref, turned_ref, block_ref = refs[-3:]

    @pl.when(pl.program_id(0) == 0)
    def _():
        transpose_rows(c, turned_ref.at[0])
        transpose_rows(gb, turned_ref.at[1])

    for n, right in enumerate((dh, u)):
        block_ref[...] = product_rows(turned_ref.at[n], right, slice(None))
        for k in range(8):
            out_ref[k, 0, n * 64 : (n + 1) * 64, :] = block_ref[k * 64 : (k + 1) * 64, :].astype(BF16)


def mlp_grad(place, c, dh, gb, u, after=()):
    flats = [v.reshape(-1, v.shape[-1]) for v in (*c, *dh, *gb, *u)]
    outs = [shape((8, 4, 128, 512))]
    depth = sum(f.shape[0] for f in flats[: len(c)])
    specs = [
        pl.BlockSpec((f.shape[0], 512), (lambda j, place: (0, 0)) if f.shape[1] == 512 else (lambda j, place: (0, place[0] ^ j)))
        for f in flats
    ]
    return run(
        partial(mlp_grad_kernel, len(c)), 17, (4,), (place, *flats), specs, outs,
        [pl.BlockSpec((8, 1, 128, 512), lambda j, place: (0, j, 0, 0))],
        [pltpu.VMEM((2, 512, depth), BF16), pltpu.VMEM((512, 512), F32)], after, 1,
    )[0]


def add_kernel(count, *refs):
    operands, outs = refs[:count], refs[count:]
    for i, out in enumerate(outs):
        total = operands[0][i].astype(F32)
        for operand in operands[1:]:
            total = total + operand[i].astype(F32)
        out[...] = total.astype(out.dtype)


def add_blocks(operands, dtype=BF16, after=()):
    outs = [shape(operands[0].shape[1:], dtype)] * operands[0].shape[0]
    return run(
        partial(add_kernel, len(operands)), 2, (1,), operands, whole_specs(operands), outs, whole_specs(outs), after=after
    )


def reduce_core(even, odd, after=()):
    return add_blocks([even, swap(odd, "dp", 1)], after=after)


def chips_kernel(near_ref, r1_ref, r2_ref, r3_ref, more_ref, *out_refs):
    rows = near_ref.shape[1]
    for j, out in enumerate(out_refs):
        total = sum(ref[j].astype(F32) for ref in (near_ref, r1_ref, r2_ref, r3_ref))
        out[0:rows] = total.astype(BF16)
        out[rows:] = more_ref[j]


def reduce_chips(near, more, after=()):
    ins = [near[0]] + [swap(near[i], "dp", 2 * i) for i in (1, 2, 3)] + [more]
    outs = [shape((near[0].shape[1] + more.shape[1], more.shape[2]))] * 4
    return run(chips_kernel, 2, (1,), ins, whole_specs(ins), outs, whole_specs(outs), after=after)


def reduce_tensor(mine, after=()):
    parts = [mine[0]] + [swap(mine[j], "tensor", j) for j in (1, 2, 3)]
    return add_blocks([p[None] for p in parts], F32, after)[0]


def scatter_grad(grads):
    flat = jnp.concatenate([g.astype(BF16).reshape(g.shape[0], -1) for g in grads], axis=1)
    flat = lax.psum_scatter(flat, "dp", scatter_dimension=0, tiled=True)
    pieces, offset = [], 0
    count = lax.axis_size("tensor")
    for g in grads:
        size = math.prod(g.shape[1:])
        piece = flat[:, offset : offset + size].reshape((flat.shape[0],) + g.shape[1:])
        pieces.append(jnp.moveaxis(piece, 2, 0).reshape(count, flat.shape[0], -1))
        offset += size
    mine = lax.psum_scatter(jnp.concatenate(pieces, axis=2), "tensor", scatter_dimension=0, tiled=True)[0]
    results, offset = [], 0
    for g in grads:
        size = g.shape[1] * g.shape[3]
        results.append(mine[:, offset : offset + size].reshape(-1, g.shape[1], g.shape[3]).astype(F32))
        offset += size
    return results


def product_sum(lefts, rights):
    return sum(
        lax.dot_general(a, b, (((0, 1), (0, 1)), ((), ())), preferred_element_type=F32)
        for a, b in zip(lefts, rights)
    )


def shards(
    gen_tokens, rec_grad, adv_grad, gen_aspect, gen_frames, disc_tokens, disc_aspect, disc_frames, disc_labels,
    logit_gain, adv_weight, train_step, ln1_gain, ln1_bias, spatial_qkv, spatial_out, ln2_gain, ln2_bias,
    temporal_qkv, temporal_out, ln3_gain, ln3_bias, mlp_in, mlp_out,
):
    tensor = lax.axis_size("tensor")
    dp_at, tensor_at = lax.axis_index("dp"), lax.axis_index("tensor")
    local, frames, patches, width = gen_tokens.shape
    windows = patches * tensor // AREA
    direct = tensor == 4 and windows == 4 and lax.axis_size("dp") == 8
    split = max(tensor // windows, 1)
    clips = -(-local // split)
    place = jnp.stack([tensor_at, dp_at]).astype(jnp.int32)
    vectors = [v.reshape(1, -1) for v in (ln1_gain, ln1_bias, ln2_gain, ln2_bias, ln3_gain, ln3_bias, logit_gain)]
    g1, b1, g2, b2, g3, b3, logit = vectors

    step_value = train_step.astype(F32)
    ramp = adv_weight * step_value / (step_value + HALF)

    def mine(values):
        return lax.dynamic_slice_in_dim(pad_clips(values, split), tensor_at % split * clips, clips, 0)

    counts = (mine(gen_frames), mine(disc_frames))
    signs = (2 * mine(disc_labels) - 1).astype(F32)

    def flat(x):
        return x.reshape(x.shape[0], -1, width)

    def to_raster(y, aspect, parts=(), after=()):
        if direct:
            return join_raster(place, aspect, y, parts, after).reshape(gen_tokens.shape)
        return gather_raster(y.reshape(clips, frames, AREA, width), aspect, split, patches)

    aspects = (mine(gen_aspect), mine(disc_aspect))
    if direct:
        x_gen, x_disc, rec, adv = (flat(v) for v in (gen_tokens, disc_tokens, rec_grad, adv_grad))
        first, rest = pack_weights(place, spatial_qkv, spatial_out, temporal_qkv, temporal_out, mlp_in, mlp_out)
        rest = lax.all_gather(rest, ("dp", "tensor"), axis=0).reshape(8, 4, 192, 512)
        time_w = mlp_w = rest
        gen_parts = exchange(pack(place, gen_aspect, x_gen, (first,)))
        space_piece = stack_pieces([first] + [swap(first, "tensor", j) for j in (1, 2, 3)], (64,), gen_parts[:1])[0]
        disc_parts = pack(place, disc_aspect, x_disc, (space_piece,))
        dy, *dy_parts = pack_grad(place, gen_aspect, gen_frames, ramp, rec, adv, disc_parts)
        space_w = gather_pieces(place, space_piece, (*gen_parts[1:], dy))
        disc_parts, dy_parts = exchange(disc_parts), exchange(dy_parts)
    else:
        space_w, time_w = gather_attention(spatial_qkv, spatial_out), gather_attention(temporal_qkv, temporal_out)
        mlp_w = gather_hidden(mlp_in, mlp_out)
        x_gen = flat(gather_window(gen_tokens, gen_aspect, split))
        x_disc = flat(gather_window(disc_tokens, disc_aspect, split))
        live = jnp.arange(frames, dtype=jnp.int32)[None, :] < gen_frames[:, None]
        total = rec_grad.astype(F32) + ramp[0] * adv_grad.astype(F32)
        dy = jnp.where(live[:, :, None, None], total, 0.0).astype(BF16)
        dy = flat(gather_window(dy, gen_aspect, split))
        gen_parts, disc_parts, dy_parts = (), (), ()

    sf_g = space_forward(place, aspects[0], x_gen, gen_parts, g1, b1, space_w)
    sf_d = space_forward(place, aspects[1], x_disc, disc_parts, g1, b1, space_w, (sf_g[0],))
    tf_g = time_forward(sf_g[0], g2, b2, time_w, (sf_d[0],))
    tf_d = time_forward(sf_d[0], g2, b2, time_w, (tf_g[0],))
    ff_g = mlp(direct, False, signs, counts[0], place, aspects[0], tf_g[0], g3, b3, mlp_w, dy, dy_parts, tf_d[:1])
    out_g = exchange(ff_g[8:]) if direct else ()
    ff_d = mlp(direct, True, signs, counts[1], place, aspects[1], tf_d[0], g3, b3, mlp_w, logit, (), ff_g[:1])
    out_d = exchange(ff_d[8:]) if direct else ()
    c, u, gb, dh = ([f[i] for f in (ff_g, ff_d)] for i in (2, 3, 4, 5))
    if direct:
        ff_blocks = mlp_grad(place, c, dh, gb, u, ff_d[:1])
        ff_mine = lax.psum_scatter(ff_blocks, "dp", scatter_dimension=0)
        tokens = (ff_blocks,)
    else:
        tokens = ()
    tb_g = time_backward(ff_g[1], sf_g[0], g2, time_w, tf_g[2], tf_g[3], (*tokens, *out_g))
    tb_d = time_backward(ff_d[1], sf_d[0], g2, time_w, tf_d[2], tf_d[3], (tb_g[0],))
    tokens = (tb_d[0],)
    temporal = ([tf_g[1], tf_d[1]], [tb_g[2], tb_d[2]], [tb_g[1], tb_d[1]], [tf_g[4], tf_d[4]])
    tokens = (tb_d[0], *out_d)
    if direct:
        time_blocks = attention_grad(False, place, temporal, (), (tb_d[0],))
        time_mine = lax.psum_scatter(time_blocks[0], "dp", scatter_dimension=0)
        tokens = (*time_blocks, *out_d)
    xs = [f[5] if direct else x for f, x in ((sf_g, x_gen), (sf_d, x_disc))]
    sb_g = space_backward(direct, tb_g[0], xs[0], g1, space_w, sf_g[2], sf_g[3], tokens)
    in_g = exchange(sb_g[5:]) if direct else ()
    tokens = (sb_g[0],)
    sb_d = space_backward(direct, tb_d[0], xs[1], g1, space_w, sf_d[2], sf_d[3], (sb_g[0], ff_mine) if direct else ())
    in_d = exchange(sb_d[5:]) if direct else ()
    spatial = ([sf_g[1], sf_d[1]], [sb_g[2], sb_d[2]], [sb_g[1], sb_d[1]], [sf_g[4], sf_d[4]])
    norms = [
        stage[k] for stages, k in (((sb_g, sb_d), 3), ((sb_g, sb_d), 4), ((tb_g, tb_d), 3), ((tb_g, tb_d), 4), ((ff_g, ff_d), 6), ((ff_g, ff_d), 7))
        for stage in stages
    ]
    part = width // tensor
    if direct:
        ff_share = reduce_tensor(ff_mine)
        even, odd = attention_grad(True, place, spatial, norms, (sb_d[0], ff_share, *in_g))
        near = reduce_core(even, odd, (time_mine,))
        y_gen = to_raster(ff_g[0], gen_aspect, out_g, near[:1])
        y_disc = to_raster(ff_d[0], disc_aspect, out_d, near[:1])
        dx_gen = to_raster(sb_g[0], gen_aspect, in_g, near[:1])
        mine = reduce_chips(near, time_mine, (y_gen, y_disc, dx_gen))
        dx_disc = to_raster(sb_d[0], disc_aspect, in_d, mine[:1])
        share = reduce_tensor(mine)
        time_block = share[80:]
        small = share[64:70]
        in_share, out_share = ff_share[:64], ff_share[64:]
        shares = []
        for block in (share[:64], time_block):
            shares += [jnp.moveaxis(block[:, : 3 * part].reshape(-1, 3, part), 1, 0), block[:, 3 * part :].T]
    else:
        y_gen, y_disc, dx_gen, dx_disc = (
            to_raster(v[0], a) for v, a in zip((ff_g, ff_d, sb_g, sb_d), (gen_aspect, disc_aspect) * 2)
        )
        in_share, out_share = scatter_grad(
            [product_sum(x, y).reshape(width, 1, tensor, -1) for x, y in ((c, dh), (gb, u))]
        )
        in_share, out_share = in_share[:, 0], out_share[:, 0]
        shares = []
        for a, dqkv, low, o in (spatial, temporal):
            qkv_share, o_share = scatter_grad(
                [product_sum(a, dqkv).reshape(width, 3, tensor, part), product_sum(low, o).reshape(width, 1, tensor, part)]
            )
            shares += [jnp.moveaxis(qkv_share, 1, 0), o_share[:, 0].T]
        small = jnp.stack([jnp.sum(n + m, axis=0) for n, m in zip(norms[::2], norms[1::2])])
        small = lax.psum(small, ("dp", "tensor"))
    piece = width // lax.axis_size("dp")
    small = lax.dynamic_slice_in_dim(small, dp_at * piece, piece, 1)

    return (
        y_gen, dx_gen, y_disc, dx_disc,
        small[0], small[1], shares[0], shares[1], small[2], small[3], shares[2], shares[3],
        small[4], small[5], in_share, out_share.T,
    )


def solution(mesh):
    tokens = P("dp", None, "tensor", None)
    vector, clip = P(), P("dp")
    qkv, rows, cols = P(None, None, "tensor"), P("tensor", None), P(None, "tensor")
    in_specs = (
        (tokens,) * 3 + (clip,) * 2 + (tokens,) + (clip,) * 3 + (vector,) * 5
        + (qkv, rows, vector, vector, qkv, rows, vector, vector, cols, rows)
    )
    block = (clip, clip, P(None, "dp", "tensor"), P("tensor", "dp"))
    out_specs = (tokens,) * 4 + block * 2 + (clip, clip, P("dp", "tensor"), P("tensor", "dp"))
    return jax.shard_map(shards, mesh=mesh, in_specs=in_specs, out_specs=out_specs, check_vma=False)
```

```python
from functools import partial
import math

import jax
import jax.numpy as jnp
from jax import lax
from jax.experimental import pallas as pl
from jax.experimental.pallas import tpu as pltpu
from jax.sharding import PartitionSpec as P

HEAD_DIM = 64
WIN = 8
AREA = WIN * WIN
HALF = 5000
EPS = 1e-05
F32 = jnp.float32
BF16 = jnp.bfloat16
VMEM_LIMIT = 58 * 1024 * 1024
COST = (10, 10, 26, 42)
COEFS = tuple(math.sqrt(math.pi / 2.0) * a for a in (0.254829592, -0.284496736, 1.421413741, -1.453152027, 1.061405429))

NT = (((1,), (1,)), ((), ()))
TN = (((0,), (0,)), ((), ()))


def dot(lhs, rhs):
    return jnp.dot(lhs, rhs, preferred_element_type=F32)


def dot_nt(lhs, rhs):
    return lax.dot_general(lhs, rhs, NT, preferred_element_type=F32)


def dot_tn(lhs, rhs):
    return lax.dot_general(lhs, rhs, TN, preferred_element_type=F32)


def normalize(value):
    average = jnp.mean(value, axis=-1, keepdims=True)
    centred = value - average
    variance = jnp.mean(centred * centred, axis=-1, keepdims=True)
    scale = lax.rsqrt(variance + EPS)
    return centred * scale, scale


def norm_backward(unit, scale, gain, grad):
    scaled = grad * gain
    inner = scaled - jnp.mean(scaled, axis=-1, keepdims=True)
    return scale * (inner - unit * jnp.mean(scaled * unit, axis=-1, keepdims=True))


def row_sums(values):
    return jnp.sum(values.reshape(-1, 8, values.shape[-1]), axis=0)


ANY = pl.BlockSpec(memory_space=pl.ANY)
SMEM = pl.BlockSpec(memory_space=pltpu.SMEM)


def run(kernel, microseconds, grid, ins, in_specs, outs, out_specs, scratch=(), after=(), bases=()):
    ins, after, bases = tuple(ins), tuple(after), tuple(bases)
    count, extra = len(ins), len(after) + len(bases)

    def body(*refs):
        kernel(*refs[:count], *refs[count + extra :])

    return pl.pallas_call(
        body,
        grid=grid,
        in_specs=list(in_specs) + [ANY] * extra,
        out_specs=list(out_specs),
        out_shape=list(outs),
        scratch_shapes=list(scratch),
        input_output_aliases={count + len(after) + i: i for i in range(len(bases))},
        cost_estimate=pl.CostEstimate(flops=int(microseconds * 2.5e9), bytes_accessed=0, transcendentals=0),
        compiler_params=pltpu.CompilerParams(
            dimension_semantics=("arbitrary",) * len(grid), vmem_limit_bytes=VMEM_LIMIT
        ),
    )(*ins, *after, *bases)


def shape(dims, dtype=BF16):
    return jax.ShapeDtypeStruct(tuple(dims), dtype)


def whole(dims):
    zeros = (0,) * len(dims)
    return pl.BlockSpec(tuple(dims), lambda i: zeros)


def per_clip(dims, first=0, count=None):
    zeros = (0,) * (len(dims) - 1)
    count = count or dims[0]
    return pl.BlockSpec((1,) + tuple(dims[1:]), lambda i: (first + jnp.clip(i, 0, count - 1),) + zeros)


def join_rows(w_ref, part):
    return jnp.concatenate(
        [
            jnp.concatenate([part(w_ref, i, j) for j in range(w_ref.shape[1])], axis=1)
            for i in range(w_ref.shape[0])
        ],
        axis=0,
    )


def head_weight(w_ref, m):
    return join_rows(w_ref, lambda ref, i, j: ref[i, j, :, m * 128 : (m + 1) * 128])


def out_weight(w_ref):
    part = w_ref.shape[2] // 4
    return jnp.concatenate(
        [
            jnp.concatenate([w_ref[i, j, c * part : (c + 1) * part, 384:512] for c in range(4)], axis=1)
            for j in range(w_ref.shape[1])
            for i in range(w_ref.shape[0])
        ],
        axis=0,
    )


def hidden_weight(w_ref, j, n):
    part = w_ref.shape[2] // 2
    return jnp.concatenate([w_ref[i, j, n * part : (n + 1) * part, :] for i in range(w_ref.shape[0])], axis=0)


def head_mask(dtype):
    rows = lax.broadcasted_iota(jnp.int32, (256, 256), 0) // HEAD_DIM
    cols = lax.broadcasted_iota(jnp.int32, (256, 256), 1) // HEAD_DIM
    return jnp.where(rows == cols, 1.0, 0.0).astype(dtype)


def spread(values, mask):
    return jnp.concatenate([values] * 4, axis=0) * mask


def pair_product(scores, values, low_lane):
    parts = []
    for c in range(2):
        full = dot_tn(scores[:, c * 128 : (c + 1) * 128], values[:, c * 128 : (c + 1) * 128])
        parts.append(jnp.where(low_lane, full[:64], full[64:]))
    return jnp.concatenate(parts, axis=1)


def one_hot(source, count):
    rows = source.shape[0]
    inside = lax.broadcasted_iota(jnp.int32, (rows, count), 0) % 8
    cols = lax.broadcasted_iota(jnp.int32, (rows, count), 1)
    return jnp.where((source >= 0) & (cols == source * 8 + inside), 1.0, 0.0).astype(BF16)


def chunk_ids():
    return lax.broadcasted_iota(jnp.int32, (AREA, 1), 0) // 8


def send_source(aspect, t):
    c = chunk_ids()
    square = jnp.where(c < 4, 2 * c + 1 - t % 2, -1)
    wide = jnp.where(
        c < 2, 4 * c + (t ^ 1), jnp.where(c < 4, -1, jnp.where(c < 6, 4 * (c - 4) + (t ^ 2), 4 * (c - 6) + (t ^ 3)))
    )
    return jnp.where(aspect == 0, square, jnp.where(aspect == 1, wide, -1))


def window_source(aspect, t):
    c = chunk_ids()
    square = jnp.where(c < 4, 2 * c + t % 2, c + 4)
    wide = jnp.where(c < 2, 4 * c + t, jnp.where(c < 4, c + 10, jnp.where(c < 6, c + 4, c + 8)))
    return jnp.where(aspect == 0, square, jnp.where(aspect == 1, wide, c))


def raster_source(aspect, t):
    c = chunk_ids()
    square = c // 2 + jnp.where(c % 2 == t % 2, 0, 8)
    way = (c % 4) ^ t
    wide = c // 4 + jnp.where(way == 0, 0, jnp.where(way == 1, 8, jnp.where(way == 2, 12, 14)))
    return jnp.where(aspect == 0, square, jnp.where(aspect == 1, wide, c))


def write_sends(values, refs):
    if not refs:
        return
    for f in range(values.shape[0] // AREA):
        base = f * AREA
        refs[0][0, f * 32 : (f + 1) * 32, :] = values[base + 32 : base + 64]
        refs[1][0, f * 16 : (f + 1) * 16, :] = values[base + 16 : base + 32]
        refs[2][0, f * 16 : (f + 1) * 16, :] = values[base + 48 : base + 64]


def pack_rows(values, select, refs):
    for f in range(values.shape[0] // AREA):
        moved = dot(select, values[f * AREA : (f + 1) * AREA]).astype(BF16)
        refs[0][0, f * 32 : (f + 1) * 32, :] = moved[:32]
        refs[1][0, f * 16 : (f + 1) * 16, :] = moved[32:48]
        refs[2][0, f * 16 : (f + 1) * 16, :] = moved[48:]


def join_parts(source, own_ref, part_refs, out_ref):
    select = one_hot(source, 2 * AREA)
    for f in range(out_ref.shape[1] // AREA):
        rows = [own_ref[0, f * AREA : (f + 1) * AREA, :]]
        rows += [ref[0, f * size : (f + 1) * size, :] for ref, size in zip(part_refs, (32, 16, 16))]
        out_ref[0, f * AREA : (f + 1) * AREA, :] = dot(select, jnp.concatenate(rows, axis=0)).astype(BF16)


def pack_kernel(place_ref, aspect_ref, x_ref, *send_refs):
    select = one_hot(send_source(aspect_ref[pl.program_id(0)], place_ref[0]), AREA)
    pack_rows(x_ref[0], select, send_refs)


def pack_grad_kernel(place_ref, aspect_ref, count_ref, ramp_ref, rec_ref, adv_ref, dy_ref, *send_refs):
    clip = pl.program_id(0)
    frame = lax.broadcasted_iota(jnp.int32, (rec_ref.shape[1], 1), 0) // AREA
    total = rec_ref[0].astype(F32) + ramp_ref[0] * adv_ref[0].astype(F32)
    dy_ref[0] = jnp.where(frame < count_ref[clip], total, 0.0).astype(BF16)
    select = one_hot(send_source(aspect_ref[clip], place_ref[0]), AREA)
    pack_rows(dy_ref[0], select, send_refs)


def join_kernel(place_ref, aspect_ref, own_ref, *refs):
    i = pl.program_id(0)
    source = raster_source(aspect_ref[i], place_ref[0])
    passes = len(refs) // 4
    count = pl.num_programs(0) // passes
    for n in range(passes):

        @pl.when(i // count == n)
        def _():
            join_parts(source, own_ref, refs[3 * n : 3 * n + 3], refs[3 * passes + n])


def send_shapes(x):
    clips, rows, width = x.shape
    return [shape((clips, rows // part, width)) for part in (2, 4, 4)]


def clip_specs(arrays, first=0, count=None):
    return [per_clip(a.shape, first, count) for a in arrays]


def whole_specs(arrays):
    return [whole(a.shape) for a in arrays]


def pack(place, aspect, x, after=()):
    outs = send_shapes(x)
    return run(
        pack_kernel, 0.01, x.shape[:1], (place, aspect, x), [SMEM, SMEM, per_clip(x.shape)], outs, clip_specs(outs), after=after
    )


def pack_grad(place, aspect, count, ramp, rec, adv, after=()):
    outs = [shape(rec.shape)] + send_shapes(rec)
    ins = (place, aspect, count, ramp, rec, adv)
    return run(
        pack_grad_kernel, 4, rec.shape[:1], ins, [SMEM] * 4 + clip_specs((rec, adv)), outs, clip_specs(outs), after=after
    )


def join_raster(place, aspect, own, parts, after=()):
    clips = parts[0][0].shape[0]

    def specs(arrays, n):
        return [pl.BlockSpec((1,) + a.shape[1:], lambda i: (jnp.clip(i - n * clips, 0, clips - 1), 0, 0)) for a in arrays]

    outs = [shape((clips,) + own.shape[1:])] * len(parts)
    ins = (place, aspect, own, *[p for group in parts for p in group])
    in_specs = [SMEM] * 2 + [per_clip(own.shape)] + [spec for n, group in enumerate(parts) for spec in specs(group, n)]
    out_specs = [spec for n, out in enumerate(outs) for spec in specs([out], n)]
    return run(join_kernel, 4 * len(parts), own.shape[:1], ins, in_specs, outs, out_specs, after=after)


def exchange(parts):
    return tuple(swap(part, "tensor", way) for way, part in zip((1, 2, 3), parts))


def swap(x, axis, way):
    return lax.ppermute(x, axis, [(i, i ^ way) for i in range(lax.axis_size(axis))])


def place_products(place_ref, block_ref, out_refs, cols):
    for k in range(8):
        rows = pl.ds(pl.multiple_of((place_ref[1] ^ k) * 64, 64), 64)
        for j in range(4):
            lanes = pl.ds(pl.multiple_of((place_ref[0] ^ j) * 128, 128), 128)
            out_refs[k % 2][k // 2, j, 0:64, cols] = block_ref[rows, lanes].astype(BF16)


def attention_products(place_ref, a_ref, dqkv_ref, low_ref, o_ref, turned_ref, block_ref, out_refs):
    def flat(ref, cols=slice(None)):
        values = ref[:, :, cols]
        return values.reshape(-1, values.shape[-1])

    turned_ref[...] = flat(a_ref).T
    for m in range(3):
        block_ref[...] = dot(turned_ref[...], flat(dqkv_ref, slice(m * 512, (m + 1) * 512)))
        place_products(place_ref, block_ref, out_refs, slice(m * 128, (m + 1) * 128))
    turned_ref[...] = flat(low_ref).T
    block_ref[...] = dot(turned_ref[...], flat(o_ref))
    place_products(place_ref, block_ref, out_refs, slice(384, 512))


def product_scratch(clips, rows, width):
    return [
        pltpu.VMEM((clips, rows, 3 * width), BF16),
        *[pltpu.VMEM((clips, rows, width), BF16)] * 3,
        pltpu.VMEM((width, clips * rows), BF16),
        pltpu.VMEM((width, width), F32),
    ]


def window_blocks(rows):
    return [(w, g) for w in range(rows // AREA) for g in range(2)]


def low_lanes():
    return lax.broadcasted_iota(jnp.int32, (64, 128), 1) < HEAD_DIM


def space_forward_kernel(parts, place_ref, aspect_ref, x_ref, *refs):
    part_refs = refs[:parts]
    gain_ref, bias_ref, w_ref, x1_ref, qkv_ref, p_ref, o_ref, xw_ref, a_ref = refs[parts:]
    rows = x_ref.shape[1]
    if parts:
        join_parts(window_source(aspect_ref[pl.program_id(0)], place_ref[0]), x_ref, part_refs, xw_ref)
    else:
        xw_ref[...] = x_ref[...]
    x = xw_ref[0].astype(F32)
    unit, _ = normalize(x)
    a_ref[...] = (unit * gain_ref[...] + bias_ref[...]).astype(BF16)
    for j in range(3):
        qkv_ref[0, :, j * 512 : (j + 1) * 512] = dot(a_ref[...], head_weight(w_ref, j)).astype(BF16)
    mask, low_lane = head_mask(BF16), low_lanes()

    def part(j, w, g):
        return qkv_ref[0, w * AREA : (w + 1) * AREA, j * 512 + g * 256 : j * 512 + (g + 1) * 256]

    blocks = window_blocks(rows)
    scores = [dot_nt(part(1, w, g), spread(part(0, w, g), mask)) * 0.125 for w, g in blocks]
    for s, (w, g) in zip(scores, blocks):
        e = jnp.exp(s - jnp.max(s, axis=0, keepdims=True))
        p_ref[0, 2 * w + g] = (e * (1.0 / jnp.sum(e, axis=0, keepdims=True))).astype(BF16)
    for w, g in blocks:
        attended = pair_product(p_ref[0, 2 * w + g], part(2, w, g), low_lane)
        o_ref[0, w * AREA : (w + 1) * AREA, g * 256 : (g + 1) * 256] = attended.astype(BF16)
    x1_ref[0] = x + dot(o_ref[0], out_weight(w_ref))


def space_forward(place, aspect, x, parts, gain, bias, w, total, bases=(), after=()):
    clips, rows, width = x.shape
    first = total - clips if bases else 0
    outs = [
        shape((total, rows, width), F32),
        shape((total, rows, 3 * width)),
        shape((total, 2 * rows // AREA, AREA, 256)),
        shape((total, rows, width)),
        shape((total, rows, width)),
    ]
    vectors = (gain, bias, w)
    return run(
        partial(space_forward_kernel, len(parts)), 10, (clips,), (place, aspect, x, *parts, *vectors),
        [SMEM] * 2 + clip_specs((x, *parts)) + whole_specs(vectors), outs, clip_specs(outs, first, clips),
        [pltpu.VMEM((rows, width), BF16)], after, bases,
    )


def space_backward_clip(dx1, x, gain, bias, w_ref, qkv_ref, p_ref, dqkv_ref, low_ref, a_ref, do_ref):
    low_ref[...] = dx1.astype(BF16)
    do_ref[...] = dot_nt(low_ref[...], out_weight(w_ref)).astype(BF16)
    mask, low_lane = head_mask(BF16), low_lanes()

    def part(j, w, g):
        return qkv_ref[0, w * AREA : (w + 1) * AREA, j * 512 + g * 256 : j * 512 + (g + 1) * 256]

    def grad(w, g):
        return spread(do_ref[w * AREA : (w + 1) * AREA, g * 256 : (g + 1) * 256], mask)

    def put(j, w, g, values):
        dqkv_ref[w * AREA : (w + 1) * AREA, j * 512 + g * 256 : j * 512 + (g + 1) * 256] = values.astype(BF16)

    blocks = window_blocks(low_ref.shape[0])
    grad_probs = [dot_nt(part(2, w, g), grad(w, g)) for w, g in blocks]
    for w, g in blocks:
        put(2, w, g, dot(p_ref[0, 2 * w + g], grad(w, g)))
    grad_scores = []
    for dp, (w, g) in zip(grad_probs, blocks):
        p = p_ref[0, 2 * w + g].astype(F32)
        weighted = p * dp
        grad_scores.append((weighted - p * jnp.sum(weighted, axis=0, keepdims=True)).astype(BF16))
    for ds, (w, g) in zip(grad_scores, blocks):
        put(1, w, g, dot(ds, spread(part(0, w, g), mask)) * 0.125)
    for ds, (w, g) in zip(grad_scores, blocks):
        put(0, w, g, pair_product(ds, part(1, w, g), low_lane) * 0.125)
    da = dot_nt(dqkv_ref[...], jnp.concatenate([head_weight(w_ref, j) for j in range(3)], axis=1))
    unit, scale = normalize(x)
    a_ref[...] = (unit * gain + bias).astype(BF16)
    return dx1 + norm_backward(unit, scale, gain, da), row_sums(da * unit), row_sums(da)


def space_backward_kernel(
    dx1_ref, x_ref, gain_ref, bias_ref, w_ref, qkv_ref, p_ref, dqkv_ref, low_ref, a_ref, dx0_ref, dg_ref, db_ref, *rest
):
    *send_refs, do_ref = rest

    @pl.when(pl.program_id(0) == 0)
    def _():
        dg_ref[...] = jnp.zeros_like(dg_ref)
        db_ref[...] = jnp.zeros_like(db_ref)

    dx0, dg, db = space_backward_clip(
        dx1_ref[0], x_ref[0].astype(F32), gain_ref[...], bias_ref[...], w_ref, qkv_ref, p_ref,
        dqkv_ref.at[0], low_ref.at[0], a_ref.at[0], do_ref,
    )
    dx0_ref[0] = dx0.astype(BF16)
    write_sends(dx0_ref[0], send_refs)
    dg_ref[...] += dg
    db_ref[...] += db


def space_backward(direct, dx1, x, gain, bias, w, qkv, p, bases=(), after=()):
    total, rows, width = x.shape
    clips = total // 2
    first = clips if bases else 0
    kept = [shape((total, rows, 3 * width))] + [shape(x.shape)] * 2
    outs = [shape((clips, rows, width))]
    sums = [shape((8, width), F32)] * 2
    sends = send_shapes(outs[0]) if direct else []
    return run(
        space_backward_kernel, 10, (clips,), (dx1, x, gain, bias, w, qkv, p),
        clip_specs((dx1, x), first, clips) + whole_specs((gain, bias, w)) + clip_specs((qkv, p), first, clips),
        kept + outs + sums + sends, clip_specs(kept, first, clips) + clip_specs(outs) + whole_specs(sums) + clip_specs(sends),
        [pltpu.VMEM((rows, width), BF16)], after, bases,
    )


def space_grad_kernel(place_ref, a_ref, dqkv_ref, low_ref, o_ref, *refs):
    norm_refs, (even_ref, odd_ref, turned_ref, block_ref) = refs[:-4], refs[-4:]
    i = pl.program_id(0)

    def place_block(m):
        place_products(place_ref, block_ref, (even_ref, odd_ref), slice(m * 128, (m + 1) * 128))

    @pl.when(i == 0)
    def _():
        turned_ref[...] = a_ref[...].T
        sums = [
            jnp.sum(left[...] + right[...], axis=0, keepdims=True) for left, right in zip(norm_refs[::2], norm_refs[1::2])
        ]
        sums = jnp.concatenate(sums + [jnp.zeros((16 - len(sums), 512), F32)], axis=0).astype(BF16)
        for ref in (even_ref, odd_ref):
            for k in range(4):
                for j in range(4):
                    ref[k, j, 64:80, :] = sums

    for m in range(3):

        @pl.when(i == m)
        def _():
            block_ref[...] = dot(turned_ref[...], dqkv_ref[...])
            place_block(m)

    @pl.when(i == 3)
    def _():
        turned_ref[...] = low_ref[...].T
        block_ref[...] = dot(turned_ref[...], o_ref[...])
        place_block(3)


def space_grad(place, a, dqkv, low, o, norms, after=()):
    a, dqkv, low, o = (v.reshape(-1, v.shape[-1]) for v in (a, dqkv, low, o))
    rows, width = a.shape
    outs = [shape((4, 4, 80, 512))] * 2
    column = pl.BlockSpec((rows, width), lambda i: (0, jnp.minimum(i, 2)))
    return run(
        space_grad_kernel, 6, (4,), (place, a, dqkv, low, o, *norms),
        [SMEM, whole(a.shape), column] + whole_specs((low, o, *norms)), outs, whole_specs(outs),
        [pltpu.VMEM((width, rows), BF16), pltpu.VMEM((width, width), F32)], after,
    )


def head_select(frame):
    rows = lax.broadcasted_iota(jnp.int32, (512, 128), 0) // HEAD_DIM
    cols = lax.broadcasted_iota(jnp.int32, (512, 128), 1) - 8 * frame
    return jnp.where(rows == cols, 1.0, 0.0).astype(BF16)


def head_expand(frame):
    rows = lax.broadcasted_iota(jnp.int32, (128, 512), 0) - 8 * frame
    cols = lax.broadcasted_iota(jnp.int32, (128, 512), 1) // HEAD_DIM
    return jnp.where(rows == cols, 1.0, 0.0).astype(BF16)


def head_sums(products, selector):
    high = products.astype(BF16)
    rest = (products - high.astype(F32)).astype(BF16)
    return dot(high, selector) + dot(rest, selector)


def time_scores(frames, left, right):
    totals = [None] * frames
    for t in range(frames):
        lhs = left(t).astype(F32)
        stacked = jnp.concatenate([lhs * right(f).astype(F32) for f in range(t + 1)], axis=0)
        sums = head_sums(stacked, head_select(t))
        for f in range(t + 1):
            part = sums[f * AREA : (f + 1) * AREA]
            totals[f] = part if totals[f] is None else totals[f] + part
    return totals


def time_forward_kernel(x_ref, gain_ref, bias_ref, w_ref, x2_ref, qkv_ref, p_ref, o_ref, a_ref):
    frames = x_ref.shape[1] // AREA
    x = x_ref[0]
    unit, _ = normalize(x)
    a_ref[...] = (unit * gain_ref[...] + bias_ref[...]).astype(BF16)
    for j in range(3):
        qkv_ref[0, :, j * 512 : (j + 1) * 512] = dot(a_ref[...], head_weight(w_ref, j)).astype(BF16)

    def part(j):
        return lambda f: qkv_ref[0, f * AREA : (f + 1) * AREA, j * 512 : (j + 1) * 512]

    scores = time_scores(frames, part(0), part(1))
    lane = lax.broadcasted_iota(jnp.int32, (AREA, 128), 1)
    scores = [jnp.where(lane >= 8 * f, s * 0.125, -1e30) for f, s in enumerate(scores)]
    top = scores[0]
    for s in scores[1:]:
        top = jnp.maximum(top, s)
    exps = [jnp.exp(s - top) for s in scores]
    inverse = 1.0 / sum(exps)
    probs = [e * inverse for e in exps]
    for f in range(frames):
        p_ref[0, f * AREA : (f + 1) * AREA, :] = probs[f]
    low = [p.astype(BF16) for p in probs]
    values = part(2)
    for t in range(frames):
        wide = dot(jnp.concatenate(low[: t + 1], axis=0), head_expand(t))
        total = None
        for f in range(t + 1):
            term = wide[f * AREA : (f + 1) * AREA] * values(f).astype(F32)
            total = term if total is None else total + term
        o_ref[0, t * AREA : (t + 1) * AREA, :] = total.astype(BF16)
    x2_ref[0] = x + dot(o_ref[0], out_weight(w_ref))


def time_forward(x, gain, bias, w, clips, bases=(), after=()):
    total, rows, width = x.shape
    first = total - clips if bases else 0
    outs = [
        shape((total, rows, width), F32),
        shape((total, rows, 3 * width)),
        shape((total, rows, 128), F32),
        shape((total, rows, width)),
    ]
    return run(
        time_forward_kernel, 10, (clips,), (x, gain, bias, w),
        clip_specs((x,), first, clips) + whole_specs((gain, bias)) + [whole(w.shape)],
        outs, clip_specs(outs, first, clips), [pltpu.VMEM((rows, width), BF16)], after, bases,
    )


def time_backward_clip(dx2, x, gain, bias, w_ref, qkv_ref, p_ref, dqkv_ref, low_ref, a_ref, do_ref):
    frames = low_ref.shape[0] // AREA
    low_ref[...] = dx2.astype(BF16)
    do_ref[...] = dot_nt(low_ref[...], out_weight(w_ref)).astype(BF16)

    def part(j):
        return lambda f: qkv_ref[0, f * AREA : (f + 1) * AREA, j * 512 : (j + 1) * 512]

    queries, key_rows, values = part(0), part(1), part(2)

    def grads(t):
        return do_ref[t * AREA : (t + 1) * AREA, :]

    dp = time_scores(frames, grads, values)
    probs = [p_ref[0, f * AREA : (f + 1) * AREA, :] for f in range(frames)]
    inner = sum(p * d for p, d in zip(probs, dp))
    ds = [(p * (d - inner)).astype(BF16) for p, d in zip(probs, dp)]
    low = [p.astype(BF16) for p in probs]
    dk = [None] * frames
    dv = [None] * frames
    for t in range(frames):
        wide = dot(jnp.concatenate(ds[: t + 1] + low[: t + 1], axis=0), head_expand(t))
        q, do = queries(t).astype(F32), grads(t).astype(F32)
        dq = None
        for f in range(t + 1):
            ds_wide = wide[f * AREA : (f + 1) * AREA]
            p_wide = wide[(t + 1 + f) * AREA : (t + 2 + f) * AREA]
            term = ds_wide * key_rows(f).astype(F32)
            dq = term if dq is None else dq + term
            dk[f] = ds_wide * q if dk[f] is None else dk[f] + ds_wide * q
            dv[f] = p_wide * do if dv[f] is None else dv[f] + p_wide * do
        dqkv_ref[t * AREA : (t + 1) * AREA, 0:512] = (dq * 0.125).astype(BF16)
    for f in range(frames):
        dqkv_ref[f * AREA : (f + 1) * AREA, 512:1024] = (dk[f] * 0.125).astype(BF16)
        dqkv_ref[f * AREA : (f + 1) * AREA, 1024:1536] = dv[f].astype(BF16)
    da = dot_nt(dqkv_ref[...], jnp.concatenate([head_weight(w_ref, j) for j in range(3)], axis=1))
    unit, scale = normalize(x)
    a_ref[...] = (unit * gain + bias).astype(BF16)
    return dx2 + norm_backward(unit, scale, gain, da), row_sums(da * unit), row_sums(da)


def time_backward_kernel(
    place_ref, dx2_ref, x_ref, gain_ref, bias_ref, w_ref, qkv_ref, p_ref, o_ref, dx1_ref, dg_ref, db_ref, *refs
):
    *out_refs, do_ref, dqkv_all, low_all, a_all, o_all, turned_ref, block_ref = refs
    i, count = pl.program_id(0), dqkv_all.shape[0]

    @pl.when(i == 0)
    def _():
        dg_ref[...] = jnp.zeros_like(dg_ref)
        db_ref[...] = jnp.zeros_like(db_ref)

    @pl.when(i < count)
    def _():
        o_all[i] = o_ref[0]
        dx1, dg, db = time_backward_clip(
            dx2_ref[0], x_ref[0], gain_ref[...], bias_ref[...], w_ref, qkv_ref, p_ref,
            dqkv_all.at[i], low_all.at[i], a_all.at[i], do_ref,
        )
        dx1_ref[0] = dx1
        dg_ref[...] += dg
        db_ref[...] += db

    @pl.when(i == count)
    def _():
        attention_products(place_ref, a_all, dqkv_all, low_all, o_all, turned_ref, block_ref, out_refs)


def time_backward(place, dx2, x, gain, bias, w, qkv, p, o, after=()):
    clips, rows, width = x.shape
    sums = [shape((8, width), F32)] * 2 + [shape((4, 4, 64, 512))] * 2
    ins = (place, dx2, x, gain, bias, w, qkv, p, o)
    return run(
        time_backward_kernel, COST[2], (clips + 1,), ins,
        [SMEM] + clip_specs((dx2, x)) + whole_specs((gain, bias)) + [whole(w.shape)] + clip_specs((qkv, p, o)),
        [shape(x.shape, F32)] + sums, [per_clip(x.shape)] + whole_specs(sums),
        [pltpu.VMEM((rows, width), BF16)] + product_scratch(clips, rows, width), after,
    )


def gelu_parts(h):
    e = jnp.exp2(h * h * (-0.5 * math.log2(math.e)) + math.log2(1.0 / math.sqrt(2.0 * math.pi)))
    t = pl.reciprocal(1.0 + (0.3275911 * math.sqrt(0.5)) * jnp.abs(h), approx=True)
    tail = t * (COEFS[0] + t * (COEFS[1] + t * (COEFS[2] + t * (COEFS[3] + t * COEFS[4])))) * e
    cdf = jnp.where(h >= 0, 1.0 - tail, tail)
    return h * cdf, cdf + h * e


def mlp_kernel(parts, sign_ref, count_ref, place_ref, aspect_ref, x_ref, gain_ref, bias_ref, w_ref, logit_ref, grad_ref, *rest):
    part_refs = rest[:parts]
    y_ref, dx_ref, out_ref, dg_ref, db_ref, *send_refs = rest[parts:-8]
    sends = len(send_refs) // 2
    slope_ref, dy_ref, c_all, gb_all, u_all, dh_all, turned_ref, block_ref = rest[-8:]
    i, (tiles, total, rows, span) = pl.program_id(0), u_all.shape
    passed = total // 2

    @pl.when(i == 0)
    def _():
        dg_ref[...] = jnp.zeros_like(dg_ref)
        db_ref[...] = jnp.zeros_like(db_ref)

    @pl.when(i < total)
    def _():
        x = x_ref[0]
        unit, scale = normalize(x)
        c_all[i] = (unit * gain_ref[...] + bias_ref[...]).astype(BF16)
        y = x
        for j in range(tiles):
            h = dot(c_all[i], hidden_weight(w_ref, j, 0))
            active, slope = gelu_parts(h)
            u_all[j, i] = active.astype(BF16)
            slope_ref[j] = slope.astype(BF16)
        y = x + dot(
            jnp.concatenate([u_all[j, i] for j in range(tiles)], axis=1),
            jnp.concatenate([hidden_weight(w_ref, j, 1) for j in range(tiles)], axis=0),
        )
        y_ref[0] = y.astype(BF16)
        dy_ref[...] = y

        @pl.when(i < passed)
        def _():
            write_sends(y_ref[0], send_refs[:sends])
            if parts:
                join_parts(window_source(aspect_ref[i], place_ref[0]), grad_ref, part_refs, gb_all.at[pl.ds(i, 1)])
            else:
                gb_all[i] = grad_ref[0]
            dy_ref[...] = gb_all[i].astype(F32)

        @pl.when(i >= passed)
        def _():
            write_sends(y_ref[0], send_refs[sends:])
            clip = i - passed
            sign = sign_ref[clip]
            frame = lax.broadcasted_iota(jnp.int32, (rows, 1), 0) // AREA
            live = jnp.where(frame < count_ref[clip], -sign, 0.0)
            signed = sign * logit_ref[...]
            dy = live * logit_ref[...] * jax.nn.sigmoid(1.0 - signed * dy_ref[...])
            gb_all[i] = dy.astype(BF16)
            dy_ref[...] = dy

        dc = None
        for j in range(tiles):
            du = dot_nt(gb_all[i], hidden_weight(w_ref, j, 1))
            dh_all[j, i] = (du * slope_ref[j].astype(F32)).astype(BF16)
        dc = dot_nt(
            jnp.concatenate([dh_all[j, i] for j in range(tiles)], axis=1),
            jnp.concatenate([hidden_weight(w_ref, j, 0) for j in range(tiles)], axis=1),
        )
        dg_ref[...] += row_sums(dc * unit)
        db_ref[...] += row_sums(dc)
        dx_ref[0] = dy_ref[...] + norm_backward(unit, scale, gain_ref[...], dc)

    @pl.when(i == total)
    def _():
        turned_ref[0] = c_all[...].reshape(-1, c_all.shape[2]).T
        turned_ref[1] = gb_all[...].reshape(-1, gb_all.shape[2]).T

    @pl.when(i >= total)
    def _():
        at = place_ref[0] ^ (i - total)
        for n, right in enumerate((dh_all, u_all)):
            block_ref[...] = dot(turned_ref[n], right[at].reshape(-1, span))
            for k in range(8):
                out_ref[k, 0, n * 64 : (n + 1) * 64, :] = block_ref[k * 64 : (k + 1) * 64, :].astype(BF16)


def mlp(direct, sign, count, place, aspect, x, gain, bias, w, logit, grad, parts=(), after=()):
    clips, rows, width = x.shape
    tiles, span = w.shape[1], w.shape[3]
    sends = send_shapes(x[: clips // 2]) if direct else []
    outs = [shape(x.shape), shape(x.shape, F32)]
    blocks = shape((8, tiles, 128, span))
    sums = [shape((8, width), F32)] * 2
    ins = (sign, count, place, aspect, x, gain, bias, w, logit, grad, *parts)
    return run(
        partial(mlp_kernel, len(parts)), COST[3], (clips + tiles,), ins,
        [SMEM] * 4 + [per_clip(x.shape)] + whole_specs((gain, bias)) + [whole(w.shape), whole(logit.shape)]
        + clip_specs((grad, *parts)),
        outs + [blocks] + sums + sends + sends,
        clip_specs(outs) + [pl.BlockSpec((8, 1, 128, span), lambda i: (0, jnp.clip(i - clips, 0, tiles - 1), 0, 0))]
        + whole_specs(sums) + clip_specs(sends) + [
            pl.BlockSpec((1,) + e.shape[1:], lambda i: (jnp.clip(i - clips // 2, 0, clips // 2 - 1), 0, 0)) for e in sends
        ],
        [
            pltpu.VMEM((tiles, rows, span), BF16),
            pltpu.VMEM((rows, width), F32),
            pltpu.VMEM((clips, rows, width), BF16),
            pltpu.VMEM((clips, rows, width), BF16),
            pltpu.VMEM((tiles, clips, rows, span), BF16),
            pltpu.VMEM((tiles, clips, rows, span), BF16),
            pltpu.VMEM((2, width, clips * rows), BF16),
            pltpu.VMEM((width, span), F32),
        ],
        after,
    )


def window_maps(aspect, tokens_frame):
    grid_side = math.isqrt(tokens_frame)
    grid_width = jnp.where(
        aspect == 1, 2 * grid_side, jnp.where(aspect == 2, grid_side // 2, grid_side)
    ).astype(jnp.int32)[:, None]
    across = grid_width // WIN
    places = jnp.arange(tokens_frame, dtype=jnp.int32)[None, :]
    window = places // AREA
    inside = places % AREA
    grid_row = window // across * WIN + inside // WIN
    grid_col = window % across * WIN + inside % WIN
    forward_order = grid_row * grid_width + grid_col
    raster_row = places // grid_width
    raster_col = places % grid_width
    back_order = (
        (raster_row // WIN * across + raster_col // WIN) * AREA + raster_row % WIN * WIN + raster_col % WIN
    )
    return (forward_order, back_order)


def reorder(values, order):
    return jax.vmap(partial(jnp.take, axis=1))(values, order)


def pad_clips(values, split):
    return jnp.pad(values, [(0, -values.shape[0] % split)] + [(0, 0)] * (values.ndim - 1))


def gather_window(x, aspect, split):
    whole_x = pad_clips(lax.all_gather(x, "tensor", axis=2, tiled=True), split)
    aspect = pad_clips(aspect, split)
    t = lax.axis_index("tensor")
    clips = aspect.shape[0] // split
    mine = lax.dynamic_slice_in_dim(whole_x, t % split * clips, clips, 0)
    kinds = lax.dynamic_slice_in_dim(aspect, t % split * clips, clips, 0)
    order, _ = window_maps(kinds, whole_x.shape[2])
    return reorder(mine, lax.dynamic_slice_in_dim(order, t // split * AREA, AREA, 1))


def gather_raster(y, aspect, split, patches):
    every = lax.all_gather(y, "tensor", axis=0)
    count, clips, frames, _, width = every.shape
    every = every.reshape(count // split, split, clips, frames, AREA, width)
    every = jnp.transpose(every, (1, 2, 3, 0, 4, 5)).reshape(split * clips, frames, -1, width)
    _, back = window_maps(aspect, every.shape[2])
    t = lax.axis_index("tensor")
    return reorder(every[: aspect.shape[0]], lax.dynamic_slice_in_dim(back, t * patches, patches, 1))


def attention_piece(d, w_ref, wo_ref):
    rows = w_ref.shape[1] // 8
    part = wo_ref.shape[0] // 8
    qkv = [w_ref[m, pl.ds(pl.multiple_of(d * rows, rows), rows), :] for m in range(3)]
    out = wo_ref[pl.ds(pl.multiple_of(d * part, part), part), :]
    squares = [out[:, c * 128 : (c + 1) * 128] for c in range(out.shape[1] // 128)]
    return jnp.concatenate(qkv + [jnp.concatenate(squares, axis=0)], axis=1)


def pack_weights_kernel(place_ref, sw_ref, swo_ref, tw_ref, two_ref, w_in_ref, w_out_ref, heads_ref, hidden_ref):
    d = place_ref[1]
    heads_ref[0:64, :] = attention_piece(d, sw_ref, swo_ref)
    heads_ref[64:128, :] = attention_piece(d, tw_ref, two_ref)
    rows = pl.ds(pl.multiple_of(d * 64, 64), 64)
    hidden_ref[0:64, :] = w_in_ref[rows, :]
    hidden_ref[64:128, :] = w_out_ref[rows, :]


def pack_weights(place, *weights):
    outs = [shape((128, 512))] * 2
    return run(pack_weights_kernel, 0.01, (1,), (place, *weights), [SMEM] + whole_specs(weights), outs, whole_specs(outs))


def stack_kernel(turn, place_ref, *refs):
    ins, outs = refs[:4], refs[4:]
    for j, ref in enumerate(ins):
        at = 0
        to = place_ref[0] ^ j if turn else j
        for out in outs:
            rows = out.shape[1]
            out[to] = ref[at : at + rows]
            at += rows


def stack_pieces(place, pieces, rows, after=()):
    outs = [shape((4, count) + pieces[0].shape[1:]) for count in rows]
    ins = (jnp.zeros(2, jnp.int32) if place is None else place, *pieces)
    return run(
        partial(stack_kernel, place is not None), 0.01, (1,), ins, [SMEM] + whole_specs(pieces), outs, whole_specs(outs), after=after
    )


def order_kernel(place_ref, even_ref, odd_ref, out_ref):
    for i in range(4):
        out_ref[place_ref[1] ^ (2 * i)] = even_ref[i]
        out_ref[place_ref[1] ^ (2 * i + 1)] = odd_ref[i]


def order_pieces(place, even, odd, after=()):
    ins = (place, even, odd)
    outs = [shape((8,) + even.shape[1:])]
    return run(order_kernel, 0.01, (1,), ins, [SMEM] + whole_specs(ins[1:]), outs, whole_specs(outs), after=after)[0]


def gather_shard(shard):
    rows = shard.shape[0] // lax.axis_size("dp")
    piece = lax.dynamic_slice_in_dim(shard, lax.axis_index("dp") * rows, rows, 0)
    whole_w = lax.all_gather(piece, ("tensor", "dp"), axis=0, tiled=True)
    return whole_w.reshape((-1,) + shard.shape)


def gather_attention(w, wo):
    width = wo.shape[1]
    heads = gather_shard(w.reshape(-1, w.shape[2])).reshape((-1,) + w.shape)
    heads = jnp.moveaxis(heads, 0, 2).reshape(3, width, 4, -1).transpose(2, 1, 0, 3).reshape(4, width, -1)
    out = gather_shard(wo).reshape(4, width // 4, 4, width // 4).transpose(0, 2, 1, 3).reshape(4, width, -1)
    return jnp.concatenate([heads, out], axis=2)[None]


def gather_hidden(w_in, w_out):
    columns = jnp.moveaxis(gather_shard(w_in), 0, 1).reshape(w_in.shape[0], 4, -1)
    rows = gather_shard(w_out).reshape(4, -1, w_out.shape[1])
    return jnp.concatenate([jnp.moveaxis(columns, 1, 0), rows], axis=1)[None]


def add_kernel(count, *refs):
    operands, outs = refs[:count], refs[count:]
    for i, out in enumerate(outs):
        total = operands[0][i].astype(F32)
        for operand in operands[1:]:
            total = total + operand[i].astype(F32)
        out[...] = total.astype(out.dtype)


def add_blocks(operands, dtype=BF16, after=()):
    outs = [shape(operands[0].shape[1:], dtype)] * operands[0].shape[0]
    return run(
        partial(add_kernel, len(operands)), 0.01, (1,), operands, whole_specs(operands), outs, whole_specs(outs), after=after
    )


def reduce_core(even, odd, after=()):
    return add_blocks([even, swap(odd, "dp", 1)], after=after)


def chips_kernel(*refs):
    ins, out_refs = refs[:8], refs[8:]
    for j, out in enumerate(out_refs):
        at = 0
        for group in (ins[:4], ins[4:]):
            rows = group[0].shape[1]
            out[at : at + rows] = sum(ref[j].astype(F32) for ref in group).astype(BF16)
            at += rows


def chip_parts(near):
    return [near[0]] + [swap(near[i], "dp", 2 * i) for i in (1, 2, 3)]


def reduce_chips(ours, others, after=()):
    outs = [shape((ours[0].shape[1] + others[0].shape[1], ours[0].shape[2]))] * 4
    ins = (*ours, *others)
    return run(chips_kernel, 0.01, (1,), ins, whole_specs(ins), outs, whole_specs(outs), after=after)


def reduce_tensor(mine, after=()):
    parts = [mine[0]] + [swap(mine[j], "tensor", j) for j in (1, 2, 3)]
    return add_blocks([p[None] for p in parts], F32, after)[0]


def scatter_grad(grads):
    flat = jnp.concatenate([g.astype(BF16).reshape(g.shape[0], -1) for g in grads], axis=1)
    flat = lax.psum_scatter(flat, "dp", scatter_dimension=0, tiled=True)
    pieces, offset = [], 0
    count = lax.axis_size("tensor")
    for g in grads:
        size = math.prod(g.shape[1:])
        piece = flat[:, offset : offset + size].reshape((flat.shape[0],) + g.shape[1:])
        pieces.append(jnp.moveaxis(piece, 2, 0).reshape(count, flat.shape[0], -1))
        offset += size
    mine = lax.psum_scatter(jnp.concatenate(pieces, axis=2), "tensor", scatter_dimension=0, tiled=True)[0]
    results, offset = [], 0
    for g in grads:
        size = g.shape[1] * g.shape[3]
        results.append(mine[:, offset : offset + size].reshape(-1, g.shape[1], g.shape[3]).astype(F32))
        offset += size
    return results


def in_order(even, odd):
    blocks = jnp.stack([even[:, :, :64], odd[:, :, :64]], axis=1).reshape(8, 4, 64, 4, 128)
    return jnp.transpose(blocks, (0, 2, 3, 1, 4)).reshape(512, 4, 512)


def shards(
    gen_tokens, rec_grad, adv_grad, gen_aspect, gen_frames, disc_tokens, disc_aspect, disc_frames, disc_labels,
    logit_gain, adv_weight, train_step, ln1_gain, ln1_bias, spatial_qkv, spatial_out, ln2_gain, ln2_bias,
    temporal_qkv, temporal_out, ln3_gain, ln3_bias, mlp_in, mlp_out,
):
    tensor = lax.axis_size("tensor")
    dp_at, tensor_at = lax.axis_index("dp"), lax.axis_index("tensor")
    local, frames, patches, width = gen_tokens.shape
    windows = patches * tensor // AREA
    direct = tensor == 4 and windows == 4 and lax.axis_size("dp") == 8
    split = max(tensor // windows, 1)
    clips = -(-local // split)
    place = jnp.stack([tensor_at, dp_at]).astype(jnp.int32)
    vectors = [v.reshape(1, -1) for v in (ln1_gain, ln1_bias, ln2_gain, ln2_bias, ln3_gain, ln3_bias, logit_gain)]
    g1, b1, g2, b2, g3, b3, logit = vectors

    step_value = train_step.astype(F32)
    ramp = adv_weight * step_value / (step_value + HALF)

    def mine(values):
        return lax.dynamic_slice_in_dim(pad_clips(values, split), tensor_at % split * clips, clips, 0)

    count = mine(disc_frames)
    sign = (2 * mine(disc_labels) - 1).astype(F32)
    aspects = (mine(gen_aspect), mine(disc_aspect))

    def flat(x):
        return x.reshape(x.shape[0], -1, width)

    if direct:
        x_gen, x_disc, rec, adv = (flat(v) for v in (gen_tokens, disc_tokens, rec_grad, adv_grad))
        heads, hidden = pack_weights(place, spatial_qkv, spatial_out, temporal_qkv, temporal_out, mlp_in, mlp_out)
        heads = [heads] + [swap(heads, "tensor", j) for j in (1, 2, 3)]
        space_piece, time_piece = stack_pieces(place, heads, (64, 64))
        time_w = lax.all_gather(time_piece, "dp", axis=0)
        gen_parts = exchange(pack(place, gen_aspect, x_gen, (space_piece,)))
        disc_parts = pack(place, disc_aspect, x_disc, (gen_parts[0],))
        even = stack_pieces(None, chip_parts([space_piece] * 4), (4,), (disc_parts[0], gen_parts[1]))[0]
        space_w = order_pieces(place, even, swap(even, "dp", 1), gen_parts)
        hidden = [hidden] + [swap(hidden, "tensor", j) for j in (1, 2, 3)]
        hidden = stack_pieces(place, hidden, (128,), (space_w,))[0]
        mlp_w = lax.all_gather(hidden, "dp", axis=0)
        disc_parts = exchange(disc_parts)
    else:
        place = jnp.zeros_like(place)
        space_w, time_w = gather_attention(spatial_qkv, spatial_out), gather_attention(temporal_qkv, temporal_out)
        mlp_w = gather_hidden(mlp_in, mlp_out)
        x_gen = flat(gather_window(gen_tokens, gen_aspect, split))
        x_disc = flat(gather_window(disc_tokens, disc_aspect, split))
        live = jnp.arange(frames, dtype=jnp.int32)[None, :] < gen_frames[:, None]
        total = rec_grad.astype(F32) + ramp[0] * adv_grad.astype(F32)
        dy = jnp.where(live[:, :, None, None], total, 0.0).astype(BF16)
        dy = flat(gather_window(dy, gen_aspect, split))
        gen_parts, disc_parts, dy_parts = (), (), ()

    sf = space_forward(place, aspects[0], x_gen, gen_parts, g1, b1, space_w, 2 * clips)
    tf = time_forward(sf[0], g2, b2, time_w, clips, (), (hidden,) if direct else ())
    if direct:
        dy, *dy_parts = pack_grad(place, gen_aspect, gen_frames, ramp, rec, adv, (tf[0],))
        dy_parts = exchange(dy_parts)
    sf = space_forward(place, aspects[1], x_disc, disc_parts, g1, b1, space_w, 2 * clips, sf, (tf[0], dy))
    x1, s_qkv, s_p, s_o, xw = sf
    x2, t_qkv, t_p, t_o = time_forward(x1, g2, b2, time_w, clips, tf)
    y, dx2, ff_blocks, ff_dg, ff_db, *y_sends = mlp(
        direct, sign, count, place, aspects[0], x2, g3, b3, mlp_w, logit, dy, dy_parts
    )
    y_gen, y_disc = (exchange(y_sends[:3]), exchange(y_sends[3:])) if direct else ((), ())
    if direct:
        ff_mine = lax.psum_scatter(ff_blocks, "dp", scatter_dimension=0)
    dx1, t_dg, t_db, t_even, t_odd = time_backward(place, dx2, x1, g2, b2, time_w, t_qkv, t_p, t_o)
    back = space_backward(direct, dx1, xw, g1, b1, space_w, s_qkv, s_p, (), y_gen)
    kept, (dx0_gen, s_dg, s_db, *gen_sends) = back[:3], back[3:]
    if direct:
        t_near = reduce_core(t_even, t_odd, (dx0_gen,))
        gen_parts = exchange(gen_sends)
        t_parts = chip_parts(t_near)
    back = space_backward(
        direct, dx1, xw, g1, b1, space_w, s_qkv, s_p, kept, (t_near[0], *y_disc) if direct else ()
    )
    kept, (dx0_disc, d_dg, d_db, *disc_sends) = back[:3], back[3:]
    disc_parts = exchange(disc_sends) if direct else ()
    dqkv, low, a = kept
    zero = jnp.zeros_like(t_dg)
    s_even, s_odd = space_grad(
        place, a, dqkv, low, s_o, (s_dg, d_dg, s_db, d_db, t_dg, zero, t_db, zero, ff_dg, zero, ff_db, zero),
        (dx0_disc, *t_parts, *gen_parts) if direct else (),
    )

    part = width // tensor
    if direct:
        near = reduce_core(s_even, s_odd, (ff_mine,))
        both = jnp.concatenate([gen_aspect, disc_aspect])
        outs = join_raster(place, both, y, (y_gen, y_disc), near[:1])
        dx_gen = join_raster(place, gen_aspect, dx0_gen, (gen_parts,), near[:1])
        ours = reduce_chips(chip_parts(near), t_parts, outs)
        dx_disc = join_raster(place, disc_aspect, dx0_disc, (disc_parts,), ours[:1])
        share = reduce_tensor(ours)
        ff_share = reduce_tensor(ff_mine)
        small = share[64:70]
        in_share, out_share = ff_share[:64], ff_share[64:]
        shares = []
        for block in (share[:64], share[80:]):
            shares += [jnp.moveaxis(block[:, : 3 * part].reshape(-1, 3, part), 1, 0), block[:, 3 * part :].T]
        y_gen, y_disc, dx_gen, dx_disc = (v.reshape(gen_tokens.shape) for v in (*outs, *dx_gen, *dx_disc))
    else:
        y_gen, y_disc, dx_gen, dx_disc = (
            gather_raster(v.reshape(clips, frames, AREA, width), aspect, split, patches)
            for v, aspect in ((y[:clips], gen_aspect), (y[clips:], disc_aspect), (dx0_gen, gen_aspect), (dx0_disc, disc_aspect))
        )
        ff = jnp.transpose(ff_blocks.reshape(8, 4, 2, 64, 512), (0, 3, 2, 1, 4)).reshape(width, 2, tensor, -1)
        ff_share = scatter_grad([ff])[0]
        in_share, out_share = ff_share[:, 0], ff_share[:, 1]
        shares = []
        for even, odd in ((s_even, s_odd), (t_even, t_odd)):
            block = scatter_grad([in_order(even, odd).reshape(width, 4, tensor, part)])[0]
            shares += [jnp.moveaxis(block[:, :3], 1, 0), block[:, 3].T]
        small = lax.psum(s_even[0, 0, 64:70].astype(F32), ("dp", "tensor"))
    piece = width // lax.axis_size("dp")
    small = lax.dynamic_slice_in_dim(small, dp_at * piece, piece, 1)

    return (
        y_gen, dx_gen, y_disc, dx_disc,
        small[0], small[1], shares[0], shares[1], small[2], small[3], shares[2], shares[3],
        small[4], small[5], in_share, out_share.T,
    )


def solution(mesh):
    tokens = P("dp", None, "tensor", None)
    vector, clip = P(), P("dp")
    qkv, rows, cols = P(None, None, "tensor"), P("tensor", None), P(None, "tensor")
    in_specs = (
        (tokens,) * 3 + (clip,) * 2 + (tokens,) + (clip,) * 3 + (vector,) * 5
        + (qkv, rows, vector, vector, qkv, rows, vector, vector, cols, rows)
    )
    block = (clip, clip, P(None, "dp", "tensor"), P("tensor", "dp"))
    out_specs = (tokens,) * 4 + block * 2 + (clip, clip, P("dp", "tensor"), P("tensor", "dp"))
    return jax.shard_map(shards, mesh=mesh, in_specs=in_specs, out_specs=out_specs, check_vma=False)
```

```python
from functools import partial
import math

import jax
import jax.numpy as jnp
from jax import lax
from jax.experimental import pallas as pl
from jax.experimental.pallas import tpu as pltpu
from jax.sharding import PartitionSpec as P

HEAD_DIM = 64
WIN = 8
AREA = WIN * WIN
HALF = 5000
EPS = 1e-05
F32 = jnp.float32
BF16 = jnp.bfloat16
VMEM_LIMIT = 58 * 1024 * 1024
JOIN = 3
COEFS = tuple(math.sqrt(math.pi / 2.0) * a for a in (0.254829592, -0.284496736, 1.421413741, -1.453152027, 1.061405429))

NT = (((1,), (1,)), ((), ()))
TN = (((0,), (0,)), ((), ()))


def dot(lhs, rhs):
    return jnp.dot(lhs, rhs, preferred_element_type=F32)


def dot_nt(lhs, rhs):
    return lax.dot_general(lhs, rhs, NT, preferred_element_type=F32)


def dot_tn(lhs, rhs):
    return lax.dot_general(lhs, rhs, TN, preferred_element_type=F32)


def normalize(value):
    average = jnp.mean(value, axis=-1, keepdims=True)
    centred = value - average
    variance = jnp.mean(centred * centred, axis=-1, keepdims=True)
    scale = lax.rsqrt(variance + EPS)
    return centred * scale, scale


def norm_backward(unit, scale, gain, grad):
    scaled = grad * gain
    inner = scaled - jnp.mean(scaled, axis=-1, keepdims=True)
    return scale * (inner - unit * jnp.mean(scaled * unit, axis=-1, keepdims=True))


def row_sums(values):
    return jnp.sum(values.reshape(-1, 8, values.shape[-1]), axis=0)


ANY = pl.BlockSpec(memory_space=pl.ANY)
SMEM = pl.BlockSpec(memory_space=pltpu.SMEM)


def run(kernel, microseconds, grid, ins, in_specs, outs, out_specs, scratch=(), after=(), bases=()):
    ins, after, bases = tuple(ins), tuple(after), tuple(bases)
    count, extra = len(ins), len(after) + len(bases)

    def body(*refs):
        kernel(*refs[:count], *refs[count + extra :])

    return pl.pallas_call(
        body,
        grid=grid,
        in_specs=list(in_specs) + [ANY] * extra,
        out_specs=list(out_specs),
        out_shape=list(outs),
        scratch_shapes=list(scratch),
        input_output_aliases={count + len(after) + i: i for i in range(len(bases))},
        cost_estimate=pl.CostEstimate(flops=int(microseconds * 2.5e9), bytes_accessed=0, transcendentals=0),
        compiler_params=pltpu.CompilerParams(
            dimension_semantics=("arbitrary",) * len(grid), vmem_limit_bytes=VMEM_LIMIT
        ),
    )(*ins, *after, *bases)


def shape(dims, dtype=BF16):
    return jax.ShapeDtypeStruct(tuple(dims), dtype)


def whole(dims):
    zeros = (0,) * len(dims)
    return pl.BlockSpec(tuple(dims), lambda i: zeros)


def per_clip(dims, first=0, count=None):
    zeros = (0,) * (len(dims) - 1)
    count = count or dims[0]
    return pl.BlockSpec((1,) + tuple(dims[1:]), lambda i: (first + jnp.clip(i, 0, count - 1),) + zeros)


def join_rows(w_ref, part):
    return jnp.concatenate(
        [
            jnp.concatenate([part(w_ref, i, j) for j in range(w_ref.shape[1])], axis=1)
            for i in range(w_ref.shape[0])
        ],
        axis=0,
    )


def head_weight(w_ref, m):
    return join_rows(w_ref, lambda ref, i, j: ref[i, j, :, m * 128 : (m + 1) * 128])


def out_weight(w_ref):
    part = w_ref.shape[2] // 4
    return jnp.concatenate(
        [
            jnp.concatenate([w_ref[i, j, c * part : (c + 1) * part, 384:512] for c in range(4)], axis=1)
            for j in range(w_ref.shape[1])
            for i in range(w_ref.shape[0])
        ],
        axis=0,
    )


def hidden_weight(w_ref, j, n):
    part = w_ref.shape[2] // 2
    return jnp.concatenate([w_ref[i, j, n * part : (n + 1) * part, :] for i in range(w_ref.shape[0])], axis=0)


def head_mask(dtype):
    rows = lax.broadcasted_iota(jnp.int32, (256, 256), 0) // HEAD_DIM
    cols = lax.broadcasted_iota(jnp.int32, (256, 256), 1) // HEAD_DIM
    return jnp.where(rows == cols, 1.0, 0.0).astype(dtype)


def spread(values, mask):
    return jnp.concatenate([values] * 4, axis=0) * mask


def pair_product(scores, values, low_lane):
    parts = []
    for c in range(2):
        full = dot_tn(scores[:, c * 128 : (c + 1) * 128], values[:, c * 128 : (c + 1) * 128])
        parts.append(jnp.where(low_lane, full[:64], full[64:]))
    return jnp.concatenate(parts, axis=1)


def one_hot(source, count):
    rows = source.shape[0]
    inside = lax.broadcasted_iota(jnp.int32, (rows, count), 0) % 8
    cols = lax.broadcasted_iota(jnp.int32, (rows, count), 1)
    return jnp.where((source >= 0) & (cols == source * 8 + inside), 1.0, 0.0).astype(BF16)


def chunk_ids():
    return lax.broadcasted_iota(jnp.int32, (AREA, 1), 0) // 8


def send_source(aspect, t):
    c = chunk_ids()
    square = jnp.where(c < 4, 2 * c + 1 - t % 2, -1)
    wide = jnp.where(
        c < 2, 4 * c + (t ^ 1), jnp.where(c < 4, -1, jnp.where(c < 6, 4 * (c - 4) + (t ^ 2), 4 * (c - 6) + (t ^ 3)))
    )
    return jnp.where(aspect == 0, square, jnp.where(aspect == 1, wide, -1))


def window_source(aspect, t):
    c = chunk_ids()
    square = jnp.where(c < 4, 2 * c + t % 2, c + 4)
    wide = jnp.where(c < 2, 4 * c + t, jnp.where(c < 4, c + 10, jnp.where(c < 6, c + 4, c + 8)))
    return jnp.where(aspect == 0, square, jnp.where(aspect == 1, wide, c))


def raster_source(aspect, t):
    c = chunk_ids()
    square = c // 2 + jnp.where(c % 2 == t % 2, 0, 8)
    way = (c % 4) ^ t
    wide = c // 4 + jnp.where(way == 0, 0, jnp.where(way == 1, 8, jnp.where(way == 2, 12, 14)))
    return jnp.where(aspect == 0, square, jnp.where(aspect == 1, wide, c))


def write_sends(values, refs):
    if not refs:
        return
    for f in range(values.shape[0] // AREA):
        base = f * AREA
        refs[0][0, f * 32 : (f + 1) * 32, :] = values[base + 32 : base + 64]
        refs[1][0, f * 16 : (f + 1) * 16, :] = values[base + 16 : base + 32]
        refs[2][0, f * 16 : (f + 1) * 16, :] = values[base + 48 : base + 64]


def pack_rows(values, select, refs):
    for f in range(values.shape[0] // AREA):
        moved = dot(select, values[f * AREA : (f + 1) * AREA]).astype(BF16)
        refs[0][0, f * 32 : (f + 1) * 32, :] = moved[:32]
        refs[1][0, f * 16 : (f + 1) * 16, :] = moved[32:48]
        refs[2][0, f * 16 : (f + 1) * 16, :] = moved[48:]


def join_parts(source, own_ref, part_refs, out_ref):
    select = one_hot(source, 2 * AREA)
    for f in range(out_ref.shape[1] // AREA):
        rows = [own_ref[0, f * AREA : (f + 1) * AREA, :]]
        rows += [ref[0, f * size : (f + 1) * size, :] for ref, size in zip(part_refs, (32, 16, 16))]
        out_ref[0, f * AREA : (f + 1) * AREA, :] = dot(select, jnp.concatenate(rows, axis=0)).astype(BF16)


def pack_kernel(place_ref, aspect_ref, x_ref, *send_refs):
    select = one_hot(send_source(aspect_ref[pl.program_id(0)], place_ref[0]), AREA)
    pack_rows(x_ref[0], select, send_refs)


def pack_grad_kernel(place_ref, aspect_ref, count_ref, ramp_ref, rec_ref, adv_ref, dy_ref, *send_refs):
    clip = pl.program_id(0)
    frame = lax.broadcasted_iota(jnp.int32, (rec_ref.shape[1], 1), 0) // AREA
    total = rec_ref[0].astype(F32) + ramp_ref[0] * adv_ref[0].astype(F32)
    dy_ref[0] = jnp.where(frame < count_ref[clip], total, 0.0).astype(BF16)
    select = one_hot(send_source(aspect_ref[clip], place_ref[0]), AREA)
    pack_rows(dy_ref[0], select, send_refs)


def join_kernel(place_ref, aspect_ref, own_ref, *refs):
    i = pl.program_id(0)
    source = raster_source(aspect_ref[i], place_ref[0])
    passes = len(refs) // 4
    count = pl.num_programs(0) // passes
    for n in range(passes):

        @pl.when(i // count == n)
        def _():
            join_parts(source, own_ref, refs[3 * n : 3 * n + 3], refs[3 * passes + n])


def send_shapes(x):
    clips, rows, width = x.shape
    return [shape((clips, rows // part, width)) for part in (2, 4, 4)]


def head_spec(w, n):
    if w.shape[2] != 128:
        return whole(w.shape)
    return pl.BlockSpec(w.shape[:2] + (64, w.shape[3]), lambda i: (0, 0, n, 0))


def clip_specs(arrays, first=0, count=None):
    return [per_clip(a.shape, first, count) for a in arrays]


def whole_specs(arrays):
    return [whole(a.shape) for a in arrays]


def pack(place, aspect, x, after=()):
    outs = send_shapes(x)
    return run(
        pack_kernel, 0.01, x.shape[:1], (place, aspect, x), [SMEM, SMEM, per_clip(x.shape)], outs, clip_specs(outs), after=after
    )


def pack_grad(place, aspect, count, ramp, rec, adv, after=()):
    outs = [shape(rec.shape)] + send_shapes(rec)
    ins = (place, aspect, count, ramp, rec, adv)
    return run(
        pack_grad_kernel, 4, rec.shape[:1], ins, [SMEM] * 4 + clip_specs((rec, adv)), outs, clip_specs(outs), after=after
    )


def join_raster(place, aspect, own, parts, after=()):
    clips = parts[0][0].shape[0]

    def specs(arrays, n):
        return [pl.BlockSpec((1,) + a.shape[1:], lambda i: (jnp.clip(i - n * clips, 0, clips - 1), 0, 0)) for a in arrays]

    outs = [shape((clips,) + own.shape[1:])] * len(parts)
    ins = (place, aspect, own, *[p for group in parts for p in group])
    in_specs = [SMEM] * 2 + [per_clip(own.shape)] + [spec for n, group in enumerate(parts) for spec in specs(group, n)]
    out_specs = [spec for n, out in enumerate(outs) for spec in specs([out], n)]
    return run(join_kernel, JOIN * len(parts), own.shape[:1], ins, in_specs, outs, out_specs, after=after)


def exchange(parts):
    return tuple(swap(part, "tensor", way) for way, part in zip((1, 2, 3), parts))


def swap(x, axis, way):
    return lax.ppermute(x, axis, [(i, i ^ way) for i in range(lax.axis_size(axis))])


def place_products(place_ref, block_ref, out_refs, cols):
    for k in range(8):
        rows = pl.ds(pl.multiple_of((place_ref[1] ^ k) * 64, 64), 64)
        for j in range(4):
            lanes = pl.ds(pl.multiple_of((place_ref[0] ^ j) * 128, 128), 128)
            out_refs[k % 2][k // 2, j, 0:64, cols] = block_ref[rows, lanes].astype(BF16)


def attention_products(place_ref, a_ref, dqkv_ref, low_ref, o_ref, turned_ref, block_ref, out_refs):
    def flat(ref, cols=slice(None)):
        values = ref[:, :, cols]
        return values.reshape(-1, values.shape[-1])

    turned_ref[...] = flat(a_ref).T
    for m in range(3):
        block_ref[...] = dot(turned_ref[...], flat(dqkv_ref, slice(m * 512, (m + 1) * 512)))
        place_products(place_ref, block_ref, out_refs, slice(m * 128, (m + 1) * 128))
    turned_ref[...] = flat(low_ref).T
    block_ref[...] = dot(turned_ref[...], flat(o_ref))
    place_products(place_ref, block_ref, out_refs, slice(384, 512))


def product_scratch(clips, rows, width):
    return [
        pltpu.VMEM((clips, rows, 3 * width), BF16),
        *[pltpu.VMEM((clips, rows, width), BF16)] * 3,
        pltpu.VMEM((width, clips * rows), BF16),
        pltpu.VMEM((width, width), F32),
    ]


def window_blocks(rows):
    return [(w, g) for w in range(rows // AREA) for g in range(2)]


def low_lanes():
    return lax.broadcasted_iota(jnp.int32, (64, 128), 1) < HEAD_DIM


def space_forward_kernel(parts, place_ref, aspect_ref, x_ref, *refs):
    part_refs = refs[:parts]
    gain_ref, bias_ref, w_ref, x1_ref, qkv_ref, p_ref, o_ref, xw_ref, a_ref = refs[parts:]
    rows = x_ref.shape[1]
    if parts:
        join_parts(window_source(aspect_ref[pl.program_id(0)], place_ref[0]), x_ref, part_refs, xw_ref)
    else:
        xw_ref[...] = x_ref[...]
    x = xw_ref[0].astype(F32)
    unit, _ = normalize(x)
    a_ref[...] = (unit * gain_ref[...] + bias_ref[...]).astype(BF16)
    for j in range(3):
        qkv_ref[0, :, j * 512 : (j + 1) * 512] = dot(a_ref[...], head_weight(w_ref, j)).astype(BF16)
    mask, low_lane = head_mask(BF16), low_lanes()

    def part(j, w, g):
        return qkv_ref[0, w * AREA : (w + 1) * AREA, j * 512 + g * 256 : j * 512 + (g + 1) * 256]

    blocks = window_blocks(rows)
    scores = [dot_nt(part(1, w, g), spread(part(0, w, g), mask)) * 0.125 for w, g in blocks]
    for s, (w, g) in zip(scores, blocks):
        e = jnp.exp(s - jnp.max(s, axis=0, keepdims=True))
        p_ref[0, 2 * w + g] = (e * (1.0 / jnp.sum(e, axis=0, keepdims=True))).astype(BF16)
    for w, g in blocks:
        attended = pair_product(p_ref[0, 2 * w + g], part(2, w, g), low_lane)
        o_ref[0, w * AREA : (w + 1) * AREA, g * 256 : (g + 1) * 256] = attended.astype(BF16)
    x1_ref[0] = x + dot(o_ref[0], out_weight(w_ref))


def space_forward(place, aspect, x, parts, gain, bias, w, total, bases=(), after=()):
    clips, rows, width = x.shape
    first = total - clips if bases else 0
    outs = [
        shape((total, rows, width), F32),
        shape((total, rows, 3 * width)),
        shape((total, 2 * rows // AREA, AREA, 256)),
        shape((total, rows, width)),
        shape((total, rows, width)),
    ]
    return run(
        partial(space_forward_kernel, len(parts)), 10, (clips,), (place, aspect, x, *parts, gain, bias, w),
        [SMEM] * 2 + clip_specs((x, *parts)) + whole_specs((gain, bias)) + [head_spec(w, 0)], outs, clip_specs(outs, first, clips),
        [pltpu.VMEM((rows, width), BF16)], after, bases,
    )


def space_backward_clip(dx1, x, gain, bias, w_ref, qkv_ref, p_ref, dqkv_ref, low_ref, a_ref, do_ref):
    low_ref[...] = dx1.astype(BF16)
    do_ref[...] = dot_nt(low_ref[...], out_weight(w_ref)).astype(BF16)
    mask, low_lane = head_mask(BF16), low_lanes()

    def part(j, w, g):
        return qkv_ref[0, w * AREA : (w + 1) * AREA, j * 512 + g * 256 : j * 512 + (g + 1) * 256]

    def grad(w, g):
        return spread(do_ref[w * AREA : (w + 1) * AREA, g * 256 : (g + 1) * 256], mask)

    def put(j, w, g, values):
        dqkv_ref[w * AREA : (w + 1) * AREA, j * 512 + g * 256 : j * 512 + (g + 1) * 256] = values.astype(BF16)

    blocks = window_blocks(low_ref.shape[0])
    grad_probs = [dot_nt(part(2, w, g), grad(w, g)) for w, g in blocks]
    for w, g in blocks:
        put(2, w, g, dot(p_ref[0, 2 * w + g], grad(w, g)))
    grad_scores = []
    for dp, (w, g) in zip(grad_probs, blocks):
        p = p_ref[0, 2 * w + g].astype(F32)
        weighted = p * dp
        grad_scores.append((weighted - p * jnp.sum(weighted, axis=0, keepdims=True)).astype(BF16))
    for ds, (w, g) in zip(grad_scores, blocks):
        put(1, w, g, dot(ds, spread(part(0, w, g), mask)) * 0.125)
    for ds, (w, g) in zip(grad_scores, blocks):
        put(0, w, g, pair_product(ds, part(1, w, g), low_lane) * 0.125)
    da = dot_nt(dqkv_ref[...], jnp.concatenate([head_weight(w_ref, j) for j in range(3)], axis=1))
    unit, scale = normalize(x)
    a_ref[...] = (unit * gain + bias).astype(BF16)
    return dx1 + norm_backward(unit, scale, gain, da), row_sums(da * unit), row_sums(da)


def space_backward_kernel(
    dx1_ref, x_ref, gain_ref, bias_ref, w_ref, qkv_ref, p_ref, dqkv_ref, low_ref, a_ref, dx0_ref, dg_ref, db_ref, *rest
):
    *send_refs, do_ref = rest

    @pl.when(pl.program_id(0) == 0)
    def _():
        dg_ref[...] = jnp.zeros_like(dg_ref)
        db_ref[...] = jnp.zeros_like(db_ref)

    dx0, dg, db = space_backward_clip(
        dx1_ref[0], x_ref[0].astype(F32), gain_ref[...], bias_ref[...], w_ref, qkv_ref, p_ref,
        dqkv_ref.at[0], low_ref.at[0], a_ref.at[0], do_ref,
    )
    dx0_ref[0] = dx0.astype(BF16)
    write_sends(dx0_ref[0], send_refs)
    dg_ref[...] += dg
    db_ref[...] += db


def space_backward(direct, dx1, x, gain, bias, w, qkv, p, bases=(), after=()):
    total, rows, width = x.shape
    clips = total // 2
    first = clips if bases else 0
    kept = [shape((total, rows, 3 * width))] + [shape(x.shape)] * 2
    outs = [shape((clips, rows, width))]
    sums = [shape((8, width), F32)] * 2
    sends = send_shapes(outs[0]) if direct else []
    return run(
        space_backward_kernel, 10, (clips,), (dx1, x, gain, bias, w, qkv, p),
        clip_specs((dx1, x), first, clips) + whole_specs((gain, bias)) + [head_spec(w, 0)] + clip_specs((qkv, p), first, clips),
        kept + outs + sums + sends, clip_specs(kept, first, clips) + clip_specs(outs) + whole_specs(sums) + clip_specs(sends),
        [pltpu.VMEM((rows, width), BF16)], after, bases,
    )


def space_grad_kernel(place_ref, a_ref, dqkv_ref, low_ref, o_ref, *refs):
    norm_refs, (even_ref, odd_ref, turned_ref, block_ref) = refs[:-4], refs[-4:]
    i = pl.program_id(0)

    def place_block(m):
        place_products(place_ref, block_ref, (even_ref, odd_ref), slice(m * 128, (m + 1) * 128))

    @pl.when(i == 0)
    def _():
        turned_ref[...] = a_ref[...].T
        sums = [
            jnp.sum(left[...] + right[...], axis=0, keepdims=True) for left, right in zip(norm_refs[::2], norm_refs[1::2])
        ]
        sums = jnp.concatenate(sums + [jnp.zeros((16 - len(sums), 512), F32)], axis=0).astype(BF16)
        for ref in (even_ref, odd_ref):
            for k in range(4):
                for j in range(4):
                    ref[k, j, 64:80, :] = sums

    for m in range(3):

        @pl.when(i == m)
        def _():
            block_ref[...] = dot(turned_ref[...], dqkv_ref[...])
            place_block(m)

    @pl.when(i == 3)
    def _():
        turned_ref[...] = low_ref[...].T
        block_ref[...] = dot(turned_ref[...], o_ref[...])
        place_block(3)


def space_grad(place, a, dqkv, low, o, norms, after=()):
    a, dqkv, low, o = (v.reshape(-1, v.shape[-1]) for v in (a, dqkv, low, o))
    rows, width = a.shape
    outs = [shape((4, 4, 80, 512))] * 2
    column = pl.BlockSpec((rows, width), lambda i: (0, jnp.minimum(i, 2)))
    return run(
        space_grad_kernel, 6, (4,), (place, a, dqkv, low, o, *norms),
        [SMEM, whole(a.shape), column] + whole_specs((low, o, *norms)), outs, whole_specs(outs),
        [pltpu.VMEM((width, rows), BF16), pltpu.VMEM((width, width), F32)], after,
    )


def head_select(frame):
    rows = lax.broadcasted_iota(jnp.int32, (512, 128), 0) // HEAD_DIM
    cols = lax.broadcasted_iota(jnp.int32, (512, 128), 1) - 8 * frame
    return jnp.where(rows == cols, 1.0, 0.0).astype(BF16)


def head_expand(frame):
    rows = lax.broadcasted_iota(jnp.int32, (128, 512), 0) - 8 * frame
    cols = lax.broadcasted_iota(jnp.int32, (128, 512), 1) // HEAD_DIM
    return jnp.where(rows == cols, 1.0, 0.0).astype(BF16)


def head_sums(products, selector):
    high = products.astype(BF16)
    rest = (products - high.astype(F32)).astype(BF16)
    return dot(high, selector) + dot(rest, selector)


def time_scores(frames, left, right):
    totals = [None] * frames
    for t in range(frames):
        lhs = left(t).astype(F32)
        stacked = jnp.concatenate([lhs * right(f).astype(F32) for f in range(t + 1)], axis=0)
        sums = head_sums(stacked, head_select(t))
        for f in range(t + 1):
            part = sums[f * AREA : (f + 1) * AREA]
            totals[f] = part if totals[f] is None else totals[f] + part
    return totals


def time_forward_kernel(x_ref, gain_ref, bias_ref, w_ref, x2_ref, qkv_ref, p_ref, o_ref, a_ref):
    frames = x_ref.shape[1] // AREA
    x = x_ref[0]
    unit, _ = normalize(x)
    a_ref[...] = (unit * gain_ref[...] + bias_ref[...]).astype(BF16)
    for j in range(3):
        qkv_ref[0, :, j * 512 : (j + 1) * 512] = dot(a_ref[...], head_weight(w_ref, j)).astype(BF16)

    def part(j):
        return lambda f: qkv_ref[0, f * AREA : (f + 1) * AREA, j * 512 : (j + 1) * 512]

    scores = time_scores(frames, part(0), part(1))
    lane = lax.broadcasted_iota(jnp.int32, (AREA, 128), 1)
    scores = [jnp.where(lane >= 8 * f, s * 0.125, -1e30) for f, s in enumerate(scores)]
    top = scores[0]
    for s in scores[1:]:
        top = jnp.maximum(top, s)
    exps = [jnp.exp(s - top) for s in scores]
    inverse = 1.0 / sum(exps)
    probs = [e * inverse for e in exps]
    for f in range(frames):
        p_ref[0, f * AREA : (f + 1) * AREA, :] = probs[f]
    low = [p.astype(BF16) for p in probs]
    values = part(2)
    for t in range(frames):
        wide = dot(jnp.concatenate(low[: t + 1], axis=0), head_expand(t))
        total = None
        for f in range(t + 1):
            term = wide[f * AREA : (f + 1) * AREA] * values(f).astype(F32)
            total = term if total is None else total + term
        o_ref[0, t * AREA : (t + 1) * AREA, :] = total.astype(BF16)
    x2_ref[0] = x + dot(o_ref[0], out_weight(w_ref))


def time_forward(x, gain, bias, w, clips, bases=(), after=()):
    total, rows, width = x.shape
    first = total - clips if bases else 0
    outs = [
        shape((total, rows, width), F32),
        shape((total, rows, 3 * width)),
        shape((total, rows, 128), F32),
        shape((total, rows, width)),
    ]
    return run(
        time_forward_kernel, 10, (clips,), (x, gain, bias, w),
        clip_specs((x,), first, clips) + whole_specs((gain, bias)) + [head_spec(w, 1)],
        outs, clip_specs(outs, first, clips), [pltpu.VMEM((rows, width), BF16)], after, bases,
    )


def time_backward_clip(dx2, x, gain, bias, w_ref, qkv_ref, p_ref, dqkv_ref, low_ref, a_ref, do_ref):
    frames = low_ref.shape[0] // AREA
    low_ref[...] = dx2.astype(BF16)
    do_ref[...] = dot_nt(low_ref[...], out_weight(w_ref)).astype(BF16)

    def part(j):
        return lambda f: qkv_ref[0, f * AREA : (f + 1) * AREA, j * 512 : (j + 1) * 512]

    queries, key_rows, values = part(0), part(1), part(2)

    def grads(t):
        return do_ref[t * AREA : (t + 1) * AREA, :]

    dp = time_scores(frames, grads, values)
    probs = [p_ref[0, f * AREA : (f + 1) * AREA, :] for f in range(frames)]
    inner = sum(p * d for p, d in zip(probs, dp))
    ds = [(p * (d - inner)).astype(BF16) for p, d in zip(probs, dp)]
    low = [p.astype(BF16) for p in probs]
    dk = [None] * frames
    dv = [None] * frames
    for t in range(frames):
        wide = dot(jnp.concatenate(ds[: t + 1] + low[: t + 1], axis=0), head_expand(t))
        q, do = queries(t).astype(F32), grads(t).astype(F32)
        dq = None
        for f in range(t + 1):
            ds_wide = wide[f * AREA : (f + 1) * AREA]
            p_wide = wide[(t + 1 + f) * AREA : (t + 2 + f) * AREA]
            term = ds_wide * key_rows(f).astype(F32)
            dq = term if dq is None else dq + term
            dk[f] = ds_wide * q if dk[f] is None else dk[f] + ds_wide * q
            dv[f] = p_wide * do if dv[f] is None else dv[f] + p_wide * do
        dqkv_ref[t * AREA : (t + 1) * AREA, 0:512] = (dq * 0.125).astype(BF16)
    for f in range(frames):
        dqkv_ref[f * AREA : (f + 1) * AREA, 512:1024] = (dk[f] * 0.125).astype(BF16)
        dqkv_ref[f * AREA : (f + 1) * AREA, 1024:1536] = dv[f].astype(BF16)
    da = dot_nt(dqkv_ref[...], jnp.concatenate([head_weight(w_ref, j) for j in range(3)], axis=1))
    unit, scale = normalize(x)
    a_ref[...] = (unit * gain + bias).astype(BF16)
    return dx2 + norm_backward(unit, scale, gain, da), row_sums(da * unit), row_sums(da)


def time_backward_kernel(
    place_ref, dx2_ref, x_ref, gain_ref, bias_ref, w_ref, qkv_ref, p_ref, o_ref, dx1_ref, dg_ref, db_ref, *refs
):
    *out_refs, do_ref, dqkv_all, low_all, a_all, o_all, turned_ref, block_ref = refs
    i, count = pl.program_id(0), dqkv_all.shape[0]

    @pl.when(i == 0)
    def _():
        dg_ref[...] = jnp.zeros_like(dg_ref)
        db_ref[...] = jnp.zeros_like(db_ref)

    @pl.when(i < count)
    def _():
        o_all[i] = o_ref[0]
        dx1, dg, db = time_backward_clip(
            dx2_ref[0], x_ref[0], gain_ref[...], bias_ref[...], w_ref, qkv_ref, p_ref,
            dqkv_all.at[i], low_all.at[i], a_all.at[i], do_ref,
        )
        dx1_ref[0] = dx1
        dg_ref[...] += dg
        db_ref[...] += db

    @pl.when(i == count)
    def _():
        attention_products(place_ref, a_all, dqkv_all, low_all, o_all, turned_ref, block_ref, out_refs)


def time_backward(place, dx2, x, gain, bias, w, qkv, p, o, after=()):
    clips, rows, width = x.shape
    sums = [shape((8, width), F32)] * 2 + [shape((4, 4, 64, 512))] * 2
    ins = (place, dx2, x, gain, bias, w, qkv, p, o)
    return run(
        time_backward_kernel, 26, (clips + 1,), ins,
        [SMEM] + clip_specs((dx2, x)) + whole_specs((gain, bias)) + [head_spec(w, 1)] + clip_specs((qkv, p, o)),
        [shape(x.shape, F32)] + sums, [per_clip(x.shape)] + whole_specs(sums),
        [pltpu.VMEM((rows, width), BF16)] + product_scratch(clips, rows, width), after,
    )


def gelu_parts(h):
    e = jnp.exp2(h * h * (-0.5 * math.log2(math.e)) + math.log2(1.0 / math.sqrt(2.0 * math.pi)))
    t = pl.reciprocal(1.0 + (0.3275911 * math.sqrt(0.5)) * jnp.abs(h), approx=True)
    tail = t * (COEFS[0] + t * (COEFS[1] + t * (COEFS[2] + t * (COEFS[3] + t * COEFS[4])))) * e
    cdf = jnp.where(h >= 0, 1.0 - tail, tail)
    return h * cdf, cdf + h * e


def mlp_clip(x, gain, bias, w_ref, c_ref, gb_ref, u_ref, dh_ref, slope_ref, y_ref, send_refs, grad_of):
    tiles = w_ref.shape[1]
    unit, scale = normalize(x)
    c_ref[...] = (unit * gain + bias).astype(BF16)
    for j in range(tiles):
        active, slope = gelu_parts(dot(c_ref[...], hidden_weight(w_ref, j, 0)))
        u_ref[j] = active.astype(BF16)
        slope_ref[j] = slope.astype(BF16)
    y = x + dot(
        jnp.concatenate([u_ref[j] for j in range(tiles)], axis=1),
        jnp.concatenate([hidden_weight(w_ref, j, 1) for j in range(tiles)], axis=0),
    )
    y_ref[...] = y.astype(BF16)
    write_sends(y_ref[...], send_refs)
    dy = grad_of(y)
    for j in range(tiles):
        du = dot_nt(gb_ref[...], hidden_weight(w_ref, j, 1))
        dh_ref[j] = (du * slope_ref[j].astype(F32)).astype(BF16)
    dc = dot_nt(
        jnp.concatenate([dh_ref[j] for j in range(tiles)], axis=1),
        jnp.concatenate([hidden_weight(w_ref, j, 0) for j in range(tiles)], axis=1),
    )
    return dy + norm_backward(unit, scale, gain, dc), row_sums(dc * unit), row_sums(dc)


def mlp_gen_kernel(parts, place_ref, aspect_ref, x_ref, gain_ref, bias_ref, w_ref, grad_ref, *rest):
    part_refs = rest[:parts]
    y_ref, dx_ref, c_ref, gb_ref, u_ref, dh_ref, dg_ref, db_ref, *send_refs, slope_ref = rest[parts:]
    i = pl.program_id(0)

    @pl.when(i == 0)
    def _():
        dg_ref[...] = jnp.zeros_like(dg_ref)
        db_ref[...] = jnp.zeros_like(db_ref)

    if parts:
        join_parts(window_source(aspect_ref[i], place_ref[0]), grad_ref, part_refs, gb_ref)
    else:
        gb_ref[...] = grad_ref[...]
    dx, dg, db = mlp_clip(
        x_ref[0], gain_ref[...], bias_ref[...], w_ref, c_ref.at[0], gb_ref.at[0], u_ref.at[:, 0], dh_ref.at[:, 0], slope_ref,
        y_ref.at[0], send_refs, lambda y: gb_ref[0].astype(F32),
    )
    dx_ref[0] = dx
    dg_ref[...] += dg
    db_ref[...] += db


def tile_block(dims, count):
    return pl.BlockSpec((dims[0], 1) + tuple(dims[2:]), lambda i: (0, jnp.minimum(i, count - 1), 0, 0))


def mlp_gen(direct, place, aspect, x, gain, bias, w, grad, parts=(), after=()):
    total, rows, width = x.shape
    clips, tiles, span = total // 2, w.shape[1], w.shape[3]
    both = [shape(x.shape), shape(x.shape, F32)]
    kept = [shape((clips, rows, width))] * 2
    hidden = [shape((tiles, clips, rows, span))] * 2
    sums = [shape((8, width), F32)] * 2
    sends = send_shapes(kept[0]) if direct else []
    return run(
        partial(mlp_gen_kernel, len(parts)), 20, (clips,), (place, aspect, x, gain, bias, w, grad, *parts),
        [SMEM] * 2 + clip_specs((x,), 0, clips) + whole_specs((gain, bias, w)) + clip_specs((grad, *parts)),
        both + kept + hidden + sums + sends,
        clip_specs(both, 0, clips) + clip_specs(kept) + [tile_block(h.shape, clips) for h in hidden] + whole_specs(sums) + clip_specs(sends),
        [pltpu.VMEM((tiles, rows, span), BF16)], after,
    )


def mlp_disc_kernel(
    sign_ref, count_ref, place_ref, x_ref, gain_ref, bias_ref, w_ref, logit_ref, c_gen, gb_gen, u_gen, dh_gen, dg_gen, db_gen,
    y_ref, dx_ref, out_ref, dg_ref, db_ref, *rest,
):
    send_refs, (slope_ref, c_all, gb_all, u_all, dh_all, turned_ref, block_ref) = rest[:-7], rest[-7:]
    i, (tiles, total, rows, span) = pl.program_id(0), u_all.shape
    count = total // 2

    @pl.when(i == 0)
    def _():
        dg_ref[...] = dg_gen[...]
        db_ref[...] = db_gen[...]

    @pl.when(i < count)
    def _():
        at = count + i
        c_all[i] = c_gen[0]
        gb_all[i] = gb_gen[0]
        u_all[:, i] = u_gen[:, 0]
        dh_all[:, i] = dh_gen[:, 0]

        def grad_of(y):
            sign = sign_ref[i]
            frame = lax.broadcasted_iota(jnp.int32, (rows, 1), 0) // AREA
            live = jnp.where(frame < count_ref[i], -sign, 0.0)
            dy = live * logit_ref[...] * jax.nn.sigmoid(1.0 - sign * logit_ref[...] * y)
            gb_all[at] = dy.astype(BF16)
            return dy

        dx, dg, db = mlp_clip(
            x_ref[0], gain_ref[...], bias_ref[...], w_ref, c_all.at[at], gb_all.at[at], u_all.at[:, at], dh_all.at[:, at],
            slope_ref, y_ref.at[0], send_refs, grad_of,
        )
        dx_ref[0] = dx
        dg_ref[...] += dg
        db_ref[...] += db

    @pl.when(i == count)
    def _():
        turned_ref[0] = c_all[...].reshape(-1, c_all.shape[2]).T
        turned_ref[1] = gb_all[...].reshape(-1, gb_all.shape[2]).T

    @pl.when(i >= count)
    def _():
        at = place_ref[0] ^ (i - count)
        for n, right in enumerate((dh_all, u_all)):
            block_ref[...] = dot(turned_ref[n], right[at].reshape(-1, span))
            for k in range(8):
                out_ref[k, 0, n * 64 : (n + 1) * 64, :] = block_ref[k * 64 : (k + 1) * 64, :].astype(BF16)


def mlp_disc(direct, sign, count, place, x, gain, bias, w, logit, kept, hidden, sums, bases, after=()):
    total, rows, width = x.shape
    clips, tiles, span = total // 2, w.shape[1], w.shape[3]
    outs = [shape(x.shape), shape(x.shape, F32)]
    blocks = shape((8, tiles, 128, span))
    sends = send_shapes(kept[0]) if direct else []
    ins = (sign, count, place, x, gain, bias, w, logit, *kept, *hidden, *sums)
    return run(
        mlp_disc_kernel, 30, (clips + tiles,), ins,
        [SMEM] * 3 + clip_specs((x,), clips, clips) + whole_specs((gain, bias, w, logit)) + clip_specs(kept)
        + [tile_block(h.shape, clips) for h in hidden] + whole_specs(sums),
        outs + [blocks] + [shape(v.shape, F32) for v in sums] + sends,
        clip_specs(outs, clips, clips) + [pl.BlockSpec((8, 1, 128, span), lambda i: (0, jnp.clip(i - clips, 0, tiles - 1), 0, 0))]
        + whole_specs(sums) + clip_specs(sends),
        [
            pltpu.VMEM((tiles, rows, span), BF16),
            pltpu.VMEM((total, rows, width), BF16),
            pltpu.VMEM((total, rows, width), BF16),
            pltpu.VMEM((tiles, total, rows, span), BF16),
            pltpu.VMEM((tiles, total, rows, span), BF16),
            pltpu.VMEM((2, width, total * rows), BF16),
            pltpu.VMEM((width, span), F32),
        ],
        after, bases,
    )


def window_maps(aspect, tokens_frame):
    grid_side = math.isqrt(tokens_frame)
    grid_width = jnp.where(
        aspect == 1, 2 * grid_side, jnp.where(aspect == 2, grid_side // 2, grid_side)
    ).astype(jnp.int32)[:, None]
    across = grid_width // WIN
    places = jnp.arange(tokens_frame, dtype=jnp.int32)[None, :]
    window = places // AREA
    inside = places % AREA
    grid_row = window // across * WIN + inside // WIN
    grid_col = window % across * WIN + inside % WIN
    forward_order = grid_row * grid_width + grid_col
    raster_row = places // grid_width
    raster_col = places % grid_width
    back_order = (
        (raster_row // WIN * across + raster_col // WIN) * AREA + raster_row % WIN * WIN + raster_col % WIN
    )
    return (forward_order, back_order)


def reorder(values, order):
    return jax.vmap(partial(jnp.take, axis=1))(values, order)


def pad_clips(values, split):
    return jnp.pad(values, [(0, -values.shape[0] % split)] + [(0, 0)] * (values.ndim - 1))


def gather_window(x, aspect, split):
    whole_x = pad_clips(lax.all_gather(x, "tensor", axis=2, tiled=True), split)
    aspect = pad_clips(aspect, split)
    t = lax.axis_index("tensor")
    clips = aspect.shape[0] // split
    mine = lax.dynamic_slice_in_dim(whole_x, t % split * clips, clips, 0)
    kinds = lax.dynamic_slice_in_dim(aspect, t % split * clips, clips, 0)
    order, _ = window_maps(kinds, whole_x.shape[2])
    return reorder(mine, lax.dynamic_slice_in_dim(order, t // split * AREA, AREA, 1))


def gather_raster(y, aspect, split, patches):
    every = lax.all_gather(y, "tensor", axis=0)
    count, clips, frames, _, width = every.shape
    every = every.reshape(count // split, split, clips, frames, AREA, width)
    every = jnp.transpose(every, (1, 2, 3, 0, 4, 5)).reshape(split * clips, frames, -1, width)
    _, back = window_maps(aspect, every.shape[2])
    t = lax.axis_index("tensor")
    return reorder(every[: aspect.shape[0]], lax.dynamic_slice_in_dim(back, t * patches, patches, 1))


def attention_piece(d, w_ref, wo_ref):
    rows = w_ref.shape[1] // 8
    part = wo_ref.shape[0] // 8
    qkv = [w_ref[m, pl.ds(pl.multiple_of(d * rows, rows), rows), :] for m in range(3)]
    out = wo_ref[pl.ds(pl.multiple_of(d * part, part), part), :]
    squares = [out[:, c * 128 : (c + 1) * 128] for c in range(out.shape[1] // 128)]
    return jnp.concatenate(qkv + [jnp.concatenate(squares, axis=0)], axis=1)


def pack_weights_kernel(place_ref, sw_ref, swo_ref, tw_ref, two_ref, w_in_ref, w_out_ref, heads_ref, hidden_ref):
    d = place_ref[1]
    heads_ref[0:64, :] = attention_piece(d, sw_ref, swo_ref)
    heads_ref[64:128, :] = attention_piece(d, tw_ref, two_ref)
    rows = pl.ds(pl.multiple_of(d * 64, 64), 64)
    hidden_ref[0:64, :] = w_in_ref[rows, :]
    hidden_ref[64:128, :] = w_out_ref[rows, :]


def pack_weights(place, *weights):
    outs = [shape((128, 512))] * 2
    return run(pack_weights_kernel, 0.01, (1,), (place, *weights), [SMEM] + whole_specs(weights), outs, whole_specs(outs))


def stack_kernel(place_ref, *refs):
    for j in range(4):
        refs[4][place_ref[0] ^ j] = refs[j][...]


def stack_pieces(place, pieces, after=()):
    outs = [shape((4,) + pieces[0].shape)]
    ins = (place, *pieces)
    return run(stack_kernel, 0.01, (1,), ins, [SMEM] + whole_specs(pieces), outs, whole_specs(outs), after=after)[0]


def gather_shard(shard):
    rows = shard.shape[0] // lax.axis_size("dp")
    piece = lax.dynamic_slice_in_dim(shard, lax.axis_index("dp") * rows, rows, 0)
    whole_w = lax.all_gather(piece, ("tensor", "dp"), axis=0, tiled=True)
    return whole_w.reshape((-1,) + shard.shape)


def gather_attention(w, wo):
    width = wo.shape[1]
    heads = gather_shard(w.reshape(-1, w.shape[2])).reshape((-1,) + w.shape)
    heads = jnp.moveaxis(heads, 0, 2).reshape(3, width, 4, -1).transpose(2, 1, 0, 3).reshape(4, width, -1)
    out = gather_shard(wo).reshape(4, width // 4, 4, width // 4).transpose(0, 2, 1, 3).reshape(4, width, -1)
    return jnp.concatenate([heads, out], axis=2)[None]


def gather_hidden(w_in, w_out):
    columns = jnp.moveaxis(gather_shard(w_in), 0, 1).reshape(w_in.shape[0], 4, -1)
    rows = gather_shard(w_out).reshape(4, -1, w_out.shape[1])
    return jnp.concatenate([jnp.moveaxis(columns, 1, 0), rows], axis=1)[None]


def add_kernel(count, *refs):
    operands, outs = refs[:count], refs[count:]
    for i, out in enumerate(outs):
        total = operands[0][i].astype(F32)
        for operand in operands[1:]:
            total = total + operand[i].astype(F32)
        out[...] = total.astype(out.dtype)


def add_blocks(operands, dtype=BF16, after=()):
    outs = [shape(operands[0].shape[1:], dtype)] * operands[0].shape[0]
    return run(
        partial(add_kernel, len(operands)), 0.01, (1,), operands, whole_specs(operands), outs, whole_specs(outs), after=after
    )


def reduce_core(even, odd, after=()):
    return add_blocks([even, swap(odd, "dp", 1)], after=after)


def chips_kernel(*refs):
    ins, out_refs = refs[:8], refs[8:]
    for j, out in enumerate(out_refs):
        at = 0
        for group in (ins[:4], ins[4:]):
            rows = group[0].shape[1]
            out[at : at + rows] = sum(ref[j].astype(F32) for ref in group).astype(BF16)
            at += rows


def chip_parts(near):
    return [near[0]] + [swap(near[i], "dp", 2 * i) for i in (1, 2, 3)]


def reduce_chips(ours, others, after=()):
    outs = [shape((ours[0].shape[1] + others[0].shape[1], ours[0].shape[2]))] * 4
    ins = (*ours, *others)
    return run(chips_kernel, 0.01, (1,), ins, whole_specs(ins), outs, whole_specs(outs), after=after)


def reduce_tensor(mine, after=()):
    parts = [mine[0]] + [swap(mine[j], "tensor", j) for j in (1, 2, 3)]
    return add_blocks([p[None] for p in parts], F32, after)[0]


def scatter_grad(grads):
    flat = jnp.concatenate([g.astype(BF16).reshape(g.shape[0], -1) for g in grads], axis=1)
    flat = lax.psum_scatter(flat, "dp", scatter_dimension=0, tiled=True)
    pieces, offset = [], 0
    count = lax.axis_size("tensor")
    for g in grads:
        size = math.prod(g.shape[1:])
        piece = flat[:, offset : offset + size].reshape((flat.shape[0],) + g.shape[1:])
        pieces.append(jnp.moveaxis(piece, 2, 0).reshape(count, flat.shape[0], -1))
        offset += size
    mine = lax.psum_scatter(jnp.concatenate(pieces, axis=2), "tensor", scatter_dimension=0, tiled=True)[0]
    results, offset = [], 0
    for g in grads:
        size = g.shape[1] * g.shape[3]
        results.append(mine[:, offset : offset + size].reshape(-1, g.shape[1], g.shape[3]).astype(F32))
        offset += size
    return results


def in_order(even, odd):
    blocks = jnp.stack([even[:, :, :64], odd[:, :, :64]], axis=1).reshape(8, 4, 64, 4, 128)
    return jnp.transpose(blocks, (0, 2, 3, 1, 4)).reshape(512, 4, 512)


def shards(
    gen_tokens, rec_grad, adv_grad, gen_aspect, gen_frames, disc_tokens, disc_aspect, disc_frames, disc_labels,
    logit_gain, adv_weight, train_step, ln1_gain, ln1_bias, spatial_qkv, spatial_out, ln2_gain, ln2_bias,
    temporal_qkv, temporal_out, ln3_gain, ln3_bias, mlp_in, mlp_out,
):
    tensor = lax.axis_size("tensor")
    dp_at, tensor_at = lax.axis_index("dp"), lax.axis_index("tensor")
    local, frames, patches, width = gen_tokens.shape
    windows = patches * tensor // AREA
    direct = tensor == 4 and windows == 4 and lax.axis_size("dp") == 8
    split = max(tensor // windows, 1)
    clips = -(-local // split)
    place = jnp.stack([tensor_at, dp_at]).astype(jnp.int32)
    vectors = [v.reshape(1, -1) for v in (ln1_gain, ln1_bias, ln2_gain, ln2_bias, ln3_gain, ln3_bias, logit_gain)]
    g1, b1, g2, b2, g3, b3, logit = vectors

    step_value = train_step.astype(F32)
    ramp = adv_weight * step_value / (step_value + HALF)

    def mine(values):
        return lax.dynamic_slice_in_dim(pad_clips(values, split), tensor_at % split * clips, clips, 0)

    count = mine(disc_frames)
    sign = (2 * mine(disc_labels) - 1).astype(F32)
    aspects = (mine(gen_aspect), mine(disc_aspect))

    def flat(x):
        return x.reshape(x.shape[0], -1, width)

    if direct:
        x_gen, x_disc, rec, adv = (flat(v) for v in (gen_tokens, disc_tokens, rec_grad, adv_grad))
        heads, hidden = pack_weights(place, spatial_qkv, spatial_out, temporal_qkv, temporal_out, mlp_in, mlp_out)
        gen_parts = pack(place, gen_aspect, x_gen, (heads,))
        disc_parts = pack(place, disc_aspect, x_disc, gen_parts)
        dy, *dy_parts = pack_grad(place, gen_aspect, gen_frames, ramp, rec, adv, disc_parts)
        heads = [heads] + [swap(heads, "tensor", j) for j in (1, 2, 3)]
        heads = stack_pieces(place, heads, (dy,))
        space_w = time_w = lax.all_gather(heads, "dp", axis=0)
        gen_parts = exchange(gen_parts)
        hidden = [hidden] + [swap(hidden, "tensor", j) for j in (1, 2, 3)]
        hidden = stack_pieces(place, hidden, (heads, *gen_parts))
        mlp_w = lax.all_gather(hidden, "dp", axis=0)
        disc_parts, dy_parts = exchange(disc_parts), exchange(dy_parts)
    else:
        place = jnp.zeros_like(place)
        space_w, time_w = gather_attention(spatial_qkv, spatial_out), gather_attention(temporal_qkv, temporal_out)
        mlp_w = gather_hidden(mlp_in, mlp_out)
        x_gen = flat(gather_window(gen_tokens, gen_aspect, split))
        x_disc = flat(gather_window(disc_tokens, disc_aspect, split))
        live = jnp.arange(frames, dtype=jnp.int32)[None, :] < gen_frames[:, None]
        total = rec_grad.astype(F32) + ramp[0] * adv_grad.astype(F32)
        dy = jnp.where(live[:, :, None, None], total, 0.0).astype(BF16)
        dy = flat(gather_window(dy, gen_aspect, split))
        gen_parts, disc_parts, dy_parts = (), (), ()

    sf = space_forward(place, aspects[0], x_gen, gen_parts, g1, b1, space_w, 2 * clips, (), (hidden,) if direct else ())
    tf = time_forward(sf[0], g2, b2, time_w, clips)
    sf = space_forward(place, aspects[1], x_disc, disc_parts, g1, b1, space_w, 2 * clips, sf, tf[:1])
    x1, s_qkv, s_p, s_o, xw = sf
    x2, t_qkv, t_p, t_o = time_forward(x1, g2, b2, time_w, clips, tf)
    gen = mlp_gen(direct, place, aspects[0], x2, g3, b3, mlp_w, dy, dy_parts)
    y_gen = exchange(gen[8:]) if direct else ()
    y, dx2, ff_blocks, ff_dg, ff_db, *y_sends = mlp_disc(
        direct, sign, count, place, x2, g3, b3, mlp_w, logit, gen[2:4], gen[4:6], gen[6:8], gen[:2]
    )
    y_disc = exchange(y_sends) if direct else ()
    if direct:
        ff_mine = lax.psum_scatter(ff_blocks, "dp", scatter_dimension=0)
    dx1, t_dg, t_db, t_even, t_odd = time_backward(place, dx2, x1, g2, b2, time_w, t_qkv, t_p, t_o, y_gen)
    back = space_backward(direct, dx1, xw, g1, b1, space_w, s_qkv, s_p, (), y_disc)
    kept, (dx0_gen, s_dg, s_db, *gen_sends) = back[:3], back[3:]
    if direct:
        t_near = reduce_core(t_even, t_odd, (dx0_gen,))
        gen_parts = exchange(gen_sends)
        t_parts = chip_parts(t_near)
    back = space_backward(
        direct, dx1, xw, g1, b1, space_w, s_qkv, s_p, kept, (t_near[0],) if direct else ()
    )
    kept, (dx0_disc, d_dg, d_db, *disc_sends) = back[:3], back[3:]
    disc_parts = exchange(disc_sends) if direct else ()
    dqkv, low, a = kept
    zero = jnp.zeros_like(t_dg)
    s_even, s_odd = space_grad(
        place, a, dqkv, low, s_o, (s_dg, d_dg, s_db, d_db, t_dg, zero, t_db, zero, ff_dg, zero, ff_db, zero),
        (dx0_disc, ff_mine, *t_parts) if direct else (),
    )

    part = width // tensor
    if direct:
        ff_share = reduce_tensor(ff_mine)
        both = jnp.concatenate([gen_aspect, disc_aspect])
        outs = join_raster(place, both, y, (y_gen, y_disc), (s_even, ff_share))
        near = reduce_core(s_even, s_odd, (*gen_parts, *outs))
        dx_gen = join_raster(place, gen_aspect, dx0_gen, (gen_parts,), near[:1])
        ours = reduce_chips(chip_parts(near), t_parts, dx_gen)
        dx_disc = join_raster(place, disc_aspect, dx0_disc, (disc_parts,), ours[:1])
        share = reduce_tensor(ours)
        small = share[64:70]
        in_share, out_share = ff_share[:64], ff_share[64:]
        shares = []
        for block in (share[:64], share[80:]):
            shares += [jnp.moveaxis(block[:, : 3 * part].reshape(-1, 3, part), 1, 0), block[:, 3 * part :].T]
        y_gen, y_disc, dx_gen, dx_disc = (v.reshape(gen_tokens.shape) for v in (*outs, *dx_gen, *dx_disc))
    else:
        y_gen, y_disc, dx_gen, dx_disc = (
            gather_raster(v.reshape(clips, frames, AREA, width), aspect, split, patches)
            for v, aspect in ((y[:clips], gen_aspect), (y[clips:], disc_aspect), (dx0_gen, gen_aspect), (dx0_disc, disc_aspect))
        )
        ff = jnp.transpose(ff_blocks.reshape(8, 4, 2, 64, 512), (0, 3, 2, 1, 4)).reshape(width, 2, tensor, -1)
        ff_share = scatter_grad([ff])[0]
        in_share, out_share = ff_share[:, 0], ff_share[:, 1]
        shares = []
        for even, odd in ((s_even, s_odd), (t_even, t_odd)):
            block = scatter_grad([in_order(even, odd).reshape(width, 4, tensor, part)])[0]
            shares += [jnp.moveaxis(block[:, :3], 1, 0), block[:, 3].T]
        small = lax.psum(s_even[0, 0, 64:70].astype(F32), ("dp", "tensor"))
    piece = width // lax.axis_size("dp")
    small = lax.dynamic_slice_in_dim(small, dp_at * piece, piece, 1)

    return (
        y_gen, dx_gen, y_disc, dx_disc,
        small[0], small[1], shares[0], shares[1], small[2], small[3], shares[2], shares[3],
        small[4], small[5], in_share, out_share.T,
    )


def solution(mesh):
    tokens = P("dp", None, "tensor", None)
    vector, clip = P(), P("dp")
    qkv, rows, cols = P(None, None, "tensor"), P("tensor", None), P(None, "tensor")
    in_specs = (
        (tokens,) * 3 + (clip,) * 2 + (tokens,) + (clip,) * 3 + (vector,) * 5
        + (qkv, rows, vector, vector, qkv, rows, vector, vector, cols, rows)
    )
    block = (clip, clip, P(None, "dp", "tensor"), P("tensor", "dp"))
    out_specs = (tokens,) * 4 + block * 2 + (clip, clip, P("dp", "tensor"), P("tensor", "dp"))
    return jax.shard_map(shards, mesh=mesh, in_specs=in_specs, out_specs=out_specs, check_vma=False)
```

```python
from functools import partial
import math

import jax
import jax.numpy as jnp
from jax import lax
from jax.experimental import pallas as pl
from jax.experimental.pallas import tpu as pltpu
from jax.sharding import PartitionSpec as P

HEAD_DIM = 64
WIN = 8
AREA = WIN * WIN
HALF = 5000
EPS = 1e-05
F32 = jnp.float32
BF16 = jnp.bfloat16
VMEM_LIMIT = 58 * 1024 * 1024
JOIN = 0.01
COEFS = tuple(math.sqrt(math.pi / 2.0) * a for a in (0.254829592, -0.284496736, 1.421413741, -1.453152027, 1.061405429))

NT = (((1,), (1,)), ((), ()))
TN = (((0,), (0,)), ((), ()))


def dot(lhs, rhs):
    return jnp.dot(lhs, rhs, preferred_element_type=F32)


def dot_nt(lhs, rhs):
    return lax.dot_general(lhs, rhs, NT, preferred_element_type=F32)


def dot_tn(lhs, rhs):
    return lax.dot_general(lhs, rhs, TN, preferred_element_type=F32)


def normalize(value):
    average = jnp.mean(value, axis=-1, keepdims=True)
    centred = value - average
    variance = jnp.mean(centred * centred, axis=-1, keepdims=True)
    scale = lax.rsqrt(variance + EPS)
    return centred * scale, scale


def norm_backward(unit, scale, gain, grad):
    scaled = grad * gain
    inner = scaled - jnp.mean(scaled, axis=-1, keepdims=True)
    return scale * (inner - unit * jnp.mean(scaled * unit, axis=-1, keepdims=True))


def row_sums(values):
    return jnp.sum(values.reshape(-1, 8, values.shape[-1]), axis=0)


ANY = pl.BlockSpec(memory_space=pl.ANY)
SMEM = pl.BlockSpec(memory_space=pltpu.SMEM)


def run(kernel, microseconds, grid, ins, in_specs, outs, out_specs, scratch=(), after=(), bases=()):
    ins, after, bases = tuple(ins), tuple(after), tuple(bases)
    count, extra = len(ins), len(after) + len(bases)

    def body(*refs):
        kernel(*refs[:count], *refs[count + extra :])

    return pl.pallas_call(
        body,
        grid=grid,
        in_specs=list(in_specs) + [ANY] * extra,
        out_specs=list(out_specs),
        out_shape=list(outs),
        scratch_shapes=list(scratch),
        input_output_aliases={count + len(after) + i: i for i in range(len(bases))},
        cost_estimate=pl.CostEstimate(flops=int(microseconds * 2.5e9), bytes_accessed=0, transcendentals=0),
        compiler_params=pltpu.CompilerParams(
            dimension_semantics=("arbitrary",) * len(grid), vmem_limit_bytes=VMEM_LIMIT
        ),
    )(*ins, *after, *bases)


def shape(dims, dtype=BF16):
    return jax.ShapeDtypeStruct(tuple(dims), dtype)


def whole(dims):
    zeros = (0,) * len(dims)
    return pl.BlockSpec(tuple(dims), lambda i: zeros)


def per_clip(dims, first=0, count=None):
    zeros = (0,) * (len(dims) - 1)
    count = count or dims[0]
    return pl.BlockSpec((1,) + tuple(dims[1:]), lambda i: (first + jnp.clip(i, 0, count - 1),) + zeros)


def join_rows(w_ref, part):
    return jnp.concatenate(
        [
            jnp.concatenate([part(w_ref, i, j) for j in range(w_ref.shape[1])], axis=1)
            for i in range(w_ref.shape[0])
        ],
        axis=0,
    )


def head_weight(w_ref, m):
    return join_rows(w_ref, lambda ref, i, j: ref[i, j, :, m * 128 : (m + 1) * 128])


def out_weight(w_ref):
    part = w_ref.shape[2] // 4
    return jnp.concatenate(
        [
            jnp.concatenate([w_ref[i, j, c * part : (c + 1) * part, 384:512] for c in range(4)], axis=1)
            for j in range(w_ref.shape[1])
            for i in range(w_ref.shape[0])
        ],
        axis=0,
    )


def hidden_weight(w_ref, j, n):
    part = w_ref.shape[2] // 2
    return jnp.concatenate([w_ref[i, j, n * part : (n + 1) * part, :] for i in range(w_ref.shape[0])], axis=0)


def head_mask(dtype):
    rows = lax.broadcasted_iota(jnp.int32, (256, 256), 0) // HEAD_DIM
    cols = lax.broadcasted_iota(jnp.int32, (256, 256), 1) // HEAD_DIM
    return jnp.where(rows == cols, 1.0, 0.0).astype(dtype)


def spread(values, mask):
    return jnp.concatenate([values] * 4, axis=0) * mask


def pair_product(scores, values, low_lane):
    parts = []
    for c in range(2):
        full = dot_tn(scores[:, c * 128 : (c + 1) * 128], values[:, c * 128 : (c + 1) * 128])
        parts.append(jnp.where(low_lane, full[:64], full[64:]))
    return jnp.concatenate(parts, axis=1)


def one_hot(source, count):
    rows = source.shape[0]
    inside = lax.broadcasted_iota(jnp.int32, (rows, count), 0) % 8
    cols = lax.broadcasted_iota(jnp.int32, (rows, count), 1)
    return jnp.where((source >= 0) & (cols == source * 8 + inside), 1.0, 0.0).astype(BF16)


def chunk_ids():
    return lax.broadcasted_iota(jnp.int32, (AREA, 1), 0) // 8


def send_source(aspect, t):
    c = chunk_ids()
    square = jnp.where(c < 4, 2 * c + 1 - t % 2, -1)
    wide = jnp.where(
        c < 2, 4 * c + (t ^ 1), jnp.where(c < 4, -1, jnp.where(c < 6, 4 * (c - 4) + (t ^ 2), 4 * (c - 6) + (t ^ 3)))
    )
    return jnp.where(aspect == 0, square, jnp.where(aspect == 1, wide, -1))


def window_source(aspect, t):
    c = chunk_ids()
    square = jnp.where(c < 4, 2 * c + t % 2, c + 4)
    wide = jnp.where(c < 2, 4 * c + t, jnp.where(c < 4, c + 10, jnp.where(c < 6, c + 4, c + 8)))
    return jnp.where(aspect == 0, square, jnp.where(aspect == 1, wide, c))


def raster_source(aspect, t):
    c = chunk_ids()
    square = c // 2 + jnp.where(c % 2 == t % 2, 0, 8)
    way = (c % 4) ^ t
    wide = c // 4 + jnp.where(way == 0, 0, jnp.where(way == 1, 8, jnp.where(way == 2, 12, 14)))
    return jnp.where(aspect == 0, square, jnp.where(aspect == 1, wide, c))


def write_sends(values, refs):
    if not refs:
        return
    for f in range(values.shape[0] // AREA):
        base = f * AREA
        refs[0][0, f * 32 : (f + 1) * 32, :] = values[base + 32 : base + 64]
        refs[1][0, f * 16 : (f + 1) * 16, :] = values[base + 16 : base + 32]
        refs[2][0, f * 16 : (f + 1) * 16, :] = values[base + 48 : base + 64]


def pack_rows(values, select, refs):
    for f in range(values.shape[0] // AREA):
        moved = dot(select, values[f * AREA : (f + 1) * AREA]).astype(BF16)
        refs[0][0, f * 32 : (f + 1) * 32, :] = moved[:32]
        refs[1][0, f * 16 : (f + 1) * 16, :] = moved[32:48]
        refs[2][0, f * 16 : (f + 1) * 16, :] = moved[48:]


def join_parts(source, own_ref, part_refs, out_ref):
    select = one_hot(source, 2 * AREA)
    for f in range(out_ref.shape[1] // AREA):
        rows = [own_ref[0, f * AREA : (f + 1) * AREA, :]]
        rows += [ref[0, f * size : (f + 1) * size, :] for ref, size in zip(part_refs, (32, 16, 16))]
        out_ref[0, f * AREA : (f + 1) * AREA, :] = dot(select, jnp.concatenate(rows, axis=0)).astype(BF16)


def pack_kernel(place_ref, aspect_ref, x_ref, *send_refs):
    select = one_hot(send_source(aspect_ref[pl.program_id(0)], place_ref[0]), AREA)
    pack_rows(x_ref[0], select, send_refs)


def pack_grad_kernel(place_ref, aspect_ref, count_ref, ramp_ref, rec_ref, adv_ref, dy_ref, *send_refs):
    clip = pl.program_id(0)
    frame = lax.broadcasted_iota(jnp.int32, (rec_ref.shape[1], 1), 0) // AREA
    total = rec_ref[0].astype(F32) + ramp_ref[0] * adv_ref[0].astype(F32)
    dy_ref[0] = jnp.where(frame < count_ref[clip], total, 0.0).astype(BF16)
    select = one_hot(send_source(aspect_ref[clip], place_ref[0]), AREA)
    pack_rows(dy_ref[0], select, send_refs)


def join_kernel(place_ref, aspect_ref, own_ref, r1_ref, r2_ref, r3_ref, out_ref):
    source = raster_source(aspect_ref[pl.program_id(0)], place_ref[0])
    join_parts(source, own_ref, (r1_ref, r2_ref, r3_ref), out_ref)


def send_shapes(x):
    clips, rows, width = x.shape
    return [shape((clips, rows // part, width)) for part in (2, 4, 4)]


def head_spec(w, n):
    if w.shape[2] != 128:
        return whole(w.shape)
    return pl.BlockSpec(w.shape[:2] + (64, w.shape[3]), lambda i: (0, 0, n, 0))


def clip_specs(arrays, first=0, count=None):
    return [per_clip(a.shape, first, count) for a in arrays]


def whole_specs(arrays):
    return [whole(a.shape) for a in arrays]


def pack(place, aspect, x, after=()):
    outs = send_shapes(x)
    return run(
        pack_kernel, 0.01, x.shape[:1], (place, aspect, x), [SMEM, SMEM, per_clip(x.shape)], outs, clip_specs(outs), after=after
    )


def pack_grad(place, aspect, count, ramp, rec, adv, after=()):
    outs = [shape(rec.shape)] + send_shapes(rec)
    ins = (place, aspect, count, ramp, rec, adv)
    return run(
        pack_grad_kernel, 4, rec.shape[:1], ins, [SMEM] * 4 + clip_specs((rec, adv)), outs, clip_specs(outs), after=after
    )


def join_raster(place, aspect, own, parts, first, microseconds, after=()):
    clips = parts[0][0].shape[0]
    outs = [shape((clips,) + own.shape[1:])]
    ins = (place, aspect, own, *parts[0])
    in_specs = [SMEM] * 2 + clip_specs((own,), first, clips) + clip_specs(parts[0])
    return run(join_kernel, microseconds, (clips,), ins, in_specs, outs, clip_specs(outs), after=after)


def exchange(parts):
    return tuple(swap(part, "tensor", way) for way, part in zip((1, 2, 3), parts))


def swap(x, axis, way):
    return lax.ppermute(x, axis, [(i, i ^ way) for i in range(lax.axis_size(axis))])


def place_products(place_ref, block_ref, out_refs, cols):
    for k in range(8):
        rows = pl.ds(pl.multiple_of((place_ref[1] ^ k) * 64, 64), 64)
        for j in range(4):
            lanes = pl.ds(pl.multiple_of((place_ref[0] ^ j) * 128, 128), 128)
            out_refs[k % 2][k // 2, j, 0:64, cols] = block_ref[rows, lanes].astype(BF16)


def attention_products(place_ref, a_ref, dqkv_ref, low_ref, o_ref, turned_ref, block_ref, out_refs):
    def flat(ref, cols=slice(None)):
        values = ref[:, :, cols]
        return values.reshape(-1, values.shape[-1])

    turned_ref[...] = flat(a_ref).T
    for m in range(3):
        block_ref[...] = dot(turned_ref[...], flat(dqkv_ref, slice(m * 512, (m + 1) * 512)))
        place_products(place_ref, block_ref, out_refs, slice(m * 128, (m + 1) * 128))
    turned_ref[...] = flat(low_ref).T
    block_ref[...] = dot(turned_ref[...], flat(o_ref))
    place_products(place_ref, block_ref, out_refs, slice(384, 512))


def product_scratch(clips, rows, width):
    return [
        pltpu.VMEM((clips, rows, 3 * width), BF16),
        *[pltpu.VMEM((clips, rows, width), BF16)] * 3,
        pltpu.VMEM((width, clips * rows), BF16),
        pltpu.VMEM((width, width), F32),
    ]


def window_blocks(rows):
    return [(w, g) for w in range(rows // AREA) for g in range(2)]


def low_lanes():
    return lax.broadcasted_iota(jnp.int32, (64, 128), 1) < HEAD_DIM


def space_forward_kernel(parts, place_ref, aspect_ref, x_ref, *refs):
    part_refs = refs[:parts]
    gain_ref, bias_ref, w_ref, x1_ref, qkv_ref, p_ref, o_ref, xw_ref, a_ref = refs[parts:]
    rows = x_ref.shape[1]
    if parts:
        join_parts(window_source(aspect_ref[pl.program_id(0)], place_ref[0]), x_ref, part_refs, xw_ref)
    else:
        xw_ref[...] = x_ref[...]
    x = xw_ref[0].astype(F32)
    unit, _ = normalize(x)
    a_ref[...] = (unit * gain_ref[...] + bias_ref[...]).astype(BF16)
    for j in range(3):
        qkv_ref[0, :, j * 512 : (j + 1) * 512] = dot(a_ref[...], head_weight(w_ref, j)).astype(BF16)
    mask, low_lane = head_mask(BF16), low_lanes()

    def part(j, w, g):
        return qkv_ref[0, w * AREA : (w + 1) * AREA, j * 512 + g * 256 : j * 512 + (g + 1) * 256]

    blocks = window_blocks(rows)
    scores = [dot_nt(part(1, w, g), spread(part(0, w, g), mask)) * 0.125 for w, g in blocks]
    for s, (w, g) in zip(scores, blocks):
        e = jnp.exp(s - jnp.max(s, axis=0, keepdims=True))
        p_ref[0, 2 * w + g] = (e * (1.0 / jnp.sum(e, axis=0, keepdims=True))).astype(BF16)
    for w, g in blocks:
        attended = pair_product(p_ref[0, 2 * w + g], part(2, w, g), low_lane)
        o_ref[0, w * AREA : (w + 1) * AREA, g * 256 : (g + 1) * 256] = attended.astype(BF16)
    x1_ref[0] = x + dot(o_ref[0], out_weight(w_ref))


def space_forward(place, aspect, x, parts, gain, bias, w, total, bases=(), after=()):
    clips, rows, width = x.shape
    first = total - clips if bases else 0
    outs = [
        shape((total, rows, width), F32),
        shape((total, rows, 3 * width)),
        shape((total, 2 * rows // AREA, AREA, 256)),
        shape((total, rows, width)),
        shape((total, rows, width)),
    ]
    return run(
        partial(space_forward_kernel, len(parts)), 10, (clips,), (place, aspect, x, *parts, gain, bias, w),
        [SMEM] * 2 + clip_specs((x, *parts)) + whole_specs((gain, bias)) + [head_spec(w, 0)], outs, clip_specs(outs, first, clips),
        [pltpu.VMEM((rows, width), BF16)], after, bases,
    )


def space_backward_clip(dx1, x, gain, bias, w_ref, qkv_ref, p_ref, dqkv_ref, low_ref, a_ref, do_ref):
    low_ref[...] = dx1.astype(BF16)
    do_ref[...] = dot_nt(low_ref[...], out_weight(w_ref)).astype(BF16)
    mask, low_lane = head_mask(BF16), low_lanes()

    def part(j, w, g):
        return qkv_ref[0, w * AREA : (w + 1) * AREA, j * 512 + g * 256 : j * 512 + (g + 1) * 256]

    def grad(w, g):
        return spread(do_ref[w * AREA : (w + 1) * AREA, g * 256 : (g + 1) * 256], mask)

    def put(j, w, g, values):
        dqkv_ref[w * AREA : (w + 1) * AREA, j * 512 + g * 256 : j * 512 + (g + 1) * 256] = values.astype(BF16)

    blocks = window_blocks(low_ref.shape[0])
    grad_probs = [dot_nt(part(2, w, g), grad(w, g)) for w, g in blocks]
    for w, g in blocks:
        put(2, w, g, dot(p_ref[0, 2 * w + g], grad(w, g)))
    grad_scores = []
    for dp, (w, g) in zip(grad_probs, blocks):
        p = p_ref[0, 2 * w + g].astype(F32)
        weighted = p * dp
        grad_scores.append((weighted - p * jnp.sum(weighted, axis=0, keepdims=True)).astype(BF16))
    for ds, (w, g) in zip(grad_scores, blocks):
        put(1, w, g, dot(ds, spread(part(0, w, g), mask)) * 0.125)
    for ds, (w, g) in zip(grad_scores, blocks):
        put(0, w, g, pair_product(ds, part(1, w, g), low_lane) * 0.125)
    da = dot_nt(dqkv_ref[...], jnp.concatenate([head_weight(w_ref, j) for j in range(3)], axis=1))
    unit, scale = normalize(x)
    a_ref[...] = (unit * gain + bias).astype(BF16)
    return dx1 + norm_backward(unit, scale, gain, da), row_sums(da * unit), row_sums(da)


def space_backward_kernel(
    dx1_ref, x_ref, gain_ref, bias_ref, w_ref, qkv_ref, p_ref, dqkv_ref, low_ref, a_ref, dx0_ref, dg_ref, db_ref, *rest
):
    *send_refs, do_ref = rest

    @pl.when(pl.program_id(0) == 0)
    def _():
        dg_ref[...] = jnp.zeros_like(dg_ref)
        db_ref[...] = jnp.zeros_like(db_ref)

    dx0, dg, db = space_backward_clip(
        dx1_ref[0], x_ref[0].astype(F32), gain_ref[...], bias_ref[...], w_ref, qkv_ref, p_ref,
        dqkv_ref.at[0], low_ref.at[0], a_ref.at[0], do_ref,
    )
    dx0_ref[0] = dx0.astype(BF16)
    write_sends(dx0_ref[0], send_refs)
    dg_ref[...] += dg
    db_ref[...] += db


def space_backward(direct, dx1, x, gain, bias, w, qkv, p, bases=(), after=()):
    total, rows, width = x.shape
    clips = total // 2
    first = clips if bases else 0
    kept = [shape((total, rows, 3 * width))] + [shape(x.shape)] * 2
    outs = [shape((clips, rows, width))]
    sums = [shape((8, width), F32)] * 2
    sends = send_shapes(outs[0]) if direct else []
    return run(
        space_backward_kernel, 10, (clips,), (dx1, x, gain, bias, w, qkv, p),
        clip_specs((dx1, x), first, clips) + whole_specs((gain, bias)) + [head_spec(w, 0)] + clip_specs((qkv, p), first, clips),
        kept + outs + sums + sends, clip_specs(kept, first, clips) + clip_specs(outs) + whole_specs(sums) + clip_specs(sends),
        [pltpu.VMEM((rows, width), BF16)], after, bases,
    )


def space_grad_kernel(place_ref, a_ref, dqkv_ref, low_ref, o_ref, *refs):
    norm_refs, (even_ref, odd_ref, turned_ref, block_ref) = refs[:-4], refs[-4:]
    i = pl.program_id(0)

    def place_block(m):
        place_products(place_ref, block_ref, (even_ref, odd_ref), slice(m * 128, (m + 1) * 128))

    @pl.when(i == 0)
    def _():
        turned_ref[...] = a_ref[...].T
        sums = [
            jnp.sum(left[...] + right[...], axis=0, keepdims=True) for left, right in zip(norm_refs[::2], norm_refs[1::2])
        ]
        sums = jnp.concatenate(sums + [jnp.zeros((16 - len(sums), 512), F32)], axis=0).astype(BF16)
        for ref in (even_ref, odd_ref):
            for k in range(4):
                for j in range(4):
                    ref[k, j, 64:80, :] = sums

    for m in range(3):

        @pl.when(i == m)
        def _():
            block_ref[...] = dot(turned_ref[...], dqkv_ref[...])
            place_block(m)

    @pl.when(i == 3)
    def _():
        turned_ref[...] = low_ref[...].T
        block_ref[...] = dot(turned_ref[...], o_ref[...])
        place_block(3)


def space_grad(place, a, dqkv, low, o, norms, after=()):
    a, dqkv, low, o = (v.reshape(-1, v.shape[-1]) for v in (a, dqkv, low, o))
    rows, width = a.shape
    outs = [shape((4, 4, 80, 512))] * 2
    column = pl.BlockSpec((rows, width), lambda i: (0, jnp.minimum(i, 2)))
    return run(
        space_grad_kernel, 6, (4,), (place, a, dqkv, low, o, *norms),
        [SMEM, whole(a.shape), column] + whole_specs((low, o, *norms)), outs, whole_specs(outs),
        [pltpu.VMEM((width, rows), BF16), pltpu.VMEM((width, width), F32)], after,
    )


def head_select(frame):
    rows = lax.broadcasted_iota(jnp.int32, (512, 128), 0) // HEAD_DIM
    cols = lax.broadcasted_iota(jnp.int32, (512, 128), 1) - 8 * frame
    return jnp.where(rows == cols, 1.0, 0.0).astype(BF16)


def head_expand(frame):
    rows = lax.broadcasted_iota(jnp.int32, (128, 512), 0) - 8 * frame
    cols = lax.broadcasted_iota(jnp.int32, (128, 512), 1) // HEAD_DIM
    return jnp.where(rows == cols, 1.0, 0.0).astype(BF16)


def head_sums(products, selector):
    high = products.astype(BF16)
    rest = (products - high.astype(F32)).astype(BF16)
    return dot(high, selector) + dot(rest, selector)


def time_scores(frames, left, right):
    totals = [None] * frames
    for t in range(frames):
        lhs = left(t).astype(F32)
        stacked = jnp.concatenate([lhs * right(f).astype(F32) for f in range(t + 1)], axis=0)
        sums = head_sums(stacked, head_select(t))
        for f in range(t + 1):
            part = sums[f * AREA : (f + 1) * AREA]
            totals[f] = part if totals[f] is None else totals[f] + part
    return totals


def time_forward_kernel(x_ref, gain_ref, bias_ref, w_ref, x2_ref, qkv_ref, p_ref, o_ref, a_ref):
    frames = x_ref.shape[1] // AREA
    x = x_ref[0]
    unit, _ = normalize(x)
    a_ref[...] = (unit * gain_ref[...] + bias_ref[...]).astype(BF16)
    for j in range(3):
        qkv_ref[0, :, j * 512 : (j + 1) * 512] = dot(a_ref[...], head_weight(w_ref, j)).astype(BF16)

    def part(j):
        return lambda f: qkv_ref[0, f * AREA : (f + 1) * AREA, j * 512 : (j + 1) * 512]

    scores = time_scores(frames, part(0), part(1))
    lane = lax.broadcasted_iota(jnp.int32, (AREA, 128), 1)
    scores = [jnp.where(lane >= 8 * f, s * 0.125, -1e30) for f, s in enumerate(scores)]
    top = scores[0]
    for s in scores[1:]:
        top = jnp.maximum(top, s)
    exps = [jnp.exp(s - top) for s in scores]
    inverse = 1.0 / sum(exps)
    probs = [e * inverse for e in exps]
    for f in range(frames):
        p_ref[0, f * AREA : (f + 1) * AREA, :] = probs[f]
    low = [p.astype(BF16) for p in probs]
    values = part(2)
    for t in range(frames):
        wide = dot(jnp.concatenate(low[: t + 1], axis=0), head_expand(t))
        total = None
        for f in range(t + 1):
            term = wide[f * AREA : (f + 1) * AREA] * values(f).astype(F32)
            total = term if total is None else total + term
        o_ref[0, t * AREA : (t + 1) * AREA, :] = total.astype(BF16)
    x2_ref[0] = x + dot(o_ref[0], out_weight(w_ref))


def time_forward(x, gain, bias, w, clips, bases=(), after=()):
    total, rows, width = x.shape
    first = total - clips if bases else 0
    outs = [
        shape((total, rows, width), F32),
        shape((total, rows, 3 * width)),
        shape((total, rows, 128), F32),
        shape((total, rows, width)),
    ]
    return run(
        time_forward_kernel, 10, (clips,), (x, gain, bias, w),
        clip_specs((x,), first, clips) + whole_specs((gain, bias)) + [head_spec(w, 1)],
        outs, clip_specs(outs, first, clips), [pltpu.VMEM((rows, width), BF16)], after, bases,
    )


def time_backward_clip(dx2, x, gain, bias, w_ref, qkv_ref, p_ref, dqkv_ref, low_ref, a_ref, do_ref):
    frames = low_ref.shape[0] // AREA
    low_ref[...] = dx2.astype(BF16)
    do_ref[...] = dot_nt(low_ref[...], out_weight(w_ref)).astype(BF16)

    def part(j):
        return lambda f: qkv_ref[0, f * AREA : (f + 1) * AREA, j * 512 : (j + 1) * 512]

    queries, key_rows, values = part(0), part(1), part(2)

    def grads(t):
        return do_ref[t * AREA : (t + 1) * AREA, :]

    dp = time_scores(frames, grads, values)
    probs = [p_ref[0, f * AREA : (f + 1) * AREA, :] for f in range(frames)]
    inner = sum(p * d for p, d in zip(probs, dp))
    ds = [(p * (d - inner)).astype(BF16) for p, d in zip(probs, dp)]
    low = [p.astype(BF16) for p in probs]
    dk = [None] * frames
    dv = [None] * frames
    for t in range(frames):
        wide = dot(jnp.concatenate(ds[: t + 1] + low[: t + 1], axis=0), head_expand(t))
        q, do = queries(t).astype(F32), grads(t).astype(F32)
        dq = None
        for f in range(t + 1):
            ds_wide = wide[f * AREA : (f + 1) * AREA]
            p_wide = wide[(t + 1 + f) * AREA : (t + 2 + f) * AREA]
            term = ds_wide * key_rows(f).astype(F32)
            dq = term if dq is None else dq + term
            dk[f] = ds_wide * q if dk[f] is None else dk[f] + ds_wide * q
            dv[f] = p_wide * do if dv[f] is None else dv[f] + p_wide * do
        dqkv_ref[t * AREA : (t + 1) * AREA, 0:512] = (dq * 0.125).astype(BF16)
    for f in range(frames):
        dqkv_ref[f * AREA : (f + 1) * AREA, 512:1024] = (dk[f] * 0.125).astype(BF16)
        dqkv_ref[f * AREA : (f + 1) * AREA, 1024:1536] = dv[f].astype(BF16)
    da = dot_nt(dqkv_ref[...], jnp.concatenate([head_weight(w_ref, j) for j in range(3)], axis=1))
    unit, scale = normalize(x)
    a_ref[...] = (unit * gain + bias).astype(BF16)
    return dx2 + norm_backward(unit, scale, gain, da), row_sums(da * unit), row_sums(da)


def time_backward_kernel(
    place_ref, dx2_ref, x_ref, gain_ref, bias_ref, w_ref, qkv_ref, p_ref, o_ref, dx1_ref, dg_ref, db_ref, *refs
):
    *out_refs, do_ref, dqkv_all, low_all, a_all, o_all, turned_ref, block_ref = refs
    i, count = pl.program_id(0), dqkv_all.shape[0]

    @pl.when(i == 0)
    def _():
        dg_ref[...] = jnp.zeros_like(dg_ref)
        db_ref[...] = jnp.zeros_like(db_ref)

    @pl.when(i < count)
    def _():
        o_all[i] = o_ref[0]
        dx1, dg, db = time_backward_clip(
            dx2_ref[0], x_ref[0], gain_ref[...], bias_ref[...], w_ref, qkv_ref, p_ref,
            dqkv_all.at[i], low_all.at[i], a_all.at[i], do_ref,
        )
        dx1_ref[0] = dx1
        dg_ref[...] += dg
        db_ref[...] += db

    @pl.when(i == count)
    def _():
        attention_products(place_ref, a_all, dqkv_all, low_all, o_all, turned_ref, block_ref, out_refs)


def time_backward(place, dx2, x, gain, bias, w, qkv, p, o, after=()):
    clips, rows, width = x.shape
    sums = [shape((8, width), F32)] * 2 + [shape((4, 4, 64, 512))] * 2
    ins = (place, dx2, x, gain, bias, w, qkv, p, o)
    return run(
        time_backward_kernel, 26, (clips + 1,), ins,
        [SMEM] + clip_specs((dx2, x)) + whole_specs((gain, bias)) + [head_spec(w, 1)] + clip_specs((qkv, p, o)),
        [shape(x.shape, F32)] + sums, [per_clip(x.shape)] + whole_specs(sums),
        [pltpu.VMEM((rows, width), BF16)] + product_scratch(clips, rows, width), after,
    )


def gelu_parts(h):
    e = jnp.exp2(h * h * (-0.5 * math.log2(math.e)) + math.log2(1.0 / math.sqrt(2.0 * math.pi)))
    t = pl.reciprocal(1.0 + (0.3275911 * math.sqrt(0.5)) * jnp.abs(h), approx=True)
    tail = t * (COEFS[0] + t * (COEFS[1] + t * (COEFS[2] + t * (COEFS[3] + t * COEFS[4])))) * e
    cdf = jnp.where(h >= 0, 1.0 - tail, tail)
    return h * cdf, cdf + h * e


def mlp_clip(x, gain, bias, w_ref, c_ref, gb_ref, u_ref, dh_ref, slope_ref, y_ref, send_refs, grad_of):
    tiles = w_ref.shape[1]
    unit, scale = normalize(x)
    c_ref[...] = (unit * gain + bias).astype(BF16)
    for j in range(tiles):
        active, slope = gelu_parts(dot(c_ref[...], hidden_weight(w_ref, j, 0)))
        u_ref[j] = active.astype(BF16)
        slope_ref[j] = slope.astype(BF16)
    y = x + dot(
        jnp.concatenate([u_ref[j] for j in range(tiles)], axis=1),
        jnp.concatenate([hidden_weight(w_ref, j, 1) for j in range(tiles)], axis=0),
    )
    y_ref[...] = y.astype(BF16)
    write_sends(y_ref[...], send_refs)
    dy = grad_of(y)
    for j in range(tiles):
        du = dot_nt(gb_ref[...], hidden_weight(w_ref, j, 1))
        dh_ref[j] = (du * slope_ref[j].astype(F32)).astype(BF16)
    dc = dot_nt(
        jnp.concatenate([dh_ref[j] for j in range(tiles)], axis=1),
        jnp.concatenate([hidden_weight(w_ref, j, 0) for j in range(tiles)], axis=1),
    )
    return dy + norm_backward(unit, scale, gain, dc), row_sums(dc * unit), row_sums(dc)


def mlp_gen_kernel(parts, place_ref, aspect_ref, x_ref, gain_ref, bias_ref, w_ref, grad_ref, *rest):
    part_refs = rest[:parts]
    y_ref, dx_ref, c_ref, gb_ref, u_ref, dh_ref, dg_ref, db_ref, *send_refs, slope_ref = rest[parts:]
    i = pl.program_id(0)

    @pl.when(i == 0)
    def _():
        dg_ref[...] = jnp.zeros_like(dg_ref)
        db_ref[...] = jnp.zeros_like(db_ref)

    if parts:
        join_parts(window_source(aspect_ref[i], place_ref[0]), grad_ref, part_refs, gb_ref)
    else:
        gb_ref[...] = grad_ref[...]
    dx, dg, db = mlp_clip(
        x_ref[0], gain_ref[...], bias_ref[...], w_ref, c_ref.at[0], gb_ref.at[0], u_ref.at[:, 0], dh_ref.at[:, 0], slope_ref,
        y_ref.at[0], send_refs, lambda y: gb_ref[0].astype(F32),
    )
    dx_ref[0] = dx
    dg_ref[...] += dg
    db_ref[...] += db


def tile_block(dims, count):
    return pl.BlockSpec((dims[0], 1) + tuple(dims[2:]), lambda i: (0, jnp.minimum(i, count - 1), 0, 0))


def mlp_gen(direct, place, aspect, x, gain, bias, w, grad, parts=(), after=()):
    total, rows, width = x.shape
    clips, tiles, span = total // 2, w.shape[1], w.shape[3]
    both = [shape(x.shape), shape(x.shape, F32)]
    kept = [shape((clips, rows, width))] * 2
    hidden = [shape((tiles, clips, rows, span))] * 2
    sums = [shape((8, width), F32)] * 2
    sends = send_shapes(kept[0]) if direct else []
    return run(
        partial(mlp_gen_kernel, len(parts)), 20, (clips,), (place, aspect, x, gain, bias, w, grad, *parts),
        [SMEM] * 2 + clip_specs((x,), 0, clips) + whole_specs((gain, bias, w)) + clip_specs((grad, *parts)),
        both + kept + hidden + sums + sends,
        clip_specs(both, 0, clips) + clip_specs(kept) + [tile_block(h.shape, clips) for h in hidden] + whole_specs(sums) + clip_specs(sends),
        [pltpu.VMEM((tiles, rows, span), BF16)], after,
    )


def mlp_disc_kernel(
    sign_ref, count_ref, place_ref, x_ref, gain_ref, bias_ref, w_ref, logit_ref, c_gen, gb_gen, u_gen, dh_gen, dg_gen, db_gen,
    y_ref, dx_ref, out_ref, dg_ref, db_ref, *rest,
):
    send_refs, (slope_ref, c_all, gb_all, u_all, dh_all, turned_ref, block_ref) = rest[:-7], rest[-7:]
    i, (tiles, total, rows, span) = pl.program_id(0), u_all.shape
    count = total // 2

    @pl.when(i == 0)
    def _():
        dg_ref[...] = dg_gen[...]
        db_ref[...] = db_gen[...]

    @pl.when(i < count)
    def _():
        at = count + i
        c_all[i] = c_gen[0]
        gb_all[i] = gb_gen[0]
        u_all[:, i] = u_gen[:, 0]
        dh_all[:, i] = dh_gen[:, 0]

        def grad_of(y):
            sign = sign_ref[i]
            frame = lax.broadcasted_iota(jnp.int32, (rows, 1), 0) // AREA
            live = jnp.where(frame < count_ref[i], -sign, 0.0)
            dy = live * logit_ref[...] * jax.nn.sigmoid(1.0 - sign * logit_ref[...] * y)
            gb_all[at] = dy.astype(BF16)
            return dy

        dx, dg, db = mlp_clip(
            x_ref[0], gain_ref[...], bias_ref[...], w_ref, c_all.at[at], gb_all.at[at], u_all.at[:, at], dh_all.at[:, at],
            slope_ref, y_ref.at[0], send_refs, grad_of,
        )
        dx_ref[0] = dx
        dg_ref[...] += dg
        db_ref[...] += db

    @pl.when(i == count)
    def _():
        turned_ref[0] = c_all[...].reshape(-1, c_all.shape[2]).T
        turned_ref[1] = gb_all[...].reshape(-1, gb_all.shape[2]).T

    @pl.when(i >= count)
    def _():
        at = i - count
        for n, right in enumerate((dh_all, u_all)):
            block_ref[...] = dot(turned_ref[n], right[at].reshape(-1, span))
            for k in range(8):
                out_ref[k, 0, n * 64 : (n + 1) * 64, :] = block_ref[k * 64 : (k + 1) * 64, :].astype(BF16)


def mlp_disc(direct, sign, count, place, x, gain, bias, w, logit, kept, hidden, sums, bases, after=()):
    total, rows, width = x.shape
    clips, tiles, span = total // 2, w.shape[1], w.shape[3]
    outs = [shape(x.shape), shape(x.shape, F32)]
    blocks = shape((8, tiles, 128, span))
    sends = send_shapes(kept[0]) if direct else []
    ins = (sign, count, place, x, gain, bias, w, logit, *kept, *hidden, *sums)
    return run(
        mlp_disc_kernel, 30, (clips + tiles,), ins,
        [SMEM] * 3 + clip_specs((x,), clips, clips) + whole_specs((gain, bias, w, logit)) + clip_specs(kept)
        + [tile_block(h.shape, clips) for h in hidden] + whole_specs(sums),
        outs + [blocks] + [shape(v.shape, F32) for v in sums] + sends,
        clip_specs(outs, clips, clips) + [pl.BlockSpec((8, 1, 128, span), lambda i: (0, jnp.clip(i - clips, 0, tiles - 1), 0, 0))]
        + whole_specs(sums) + clip_specs(sends),
        [
            pltpu.VMEM((tiles, rows, span), BF16),
            pltpu.VMEM((total, rows, width), BF16),
            pltpu.VMEM((total, rows, width), BF16),
            pltpu.VMEM((tiles, total, rows, span), BF16),
            pltpu.VMEM((tiles, total, rows, span), BF16),
            pltpu.VMEM((2, width, total * rows), BF16),
            pltpu.VMEM((width, span), F32),
        ],
        after, bases,
    )


def window_maps(aspect, tokens_frame):
    grid_side = math.isqrt(tokens_frame)
    grid_width = jnp.where(
        aspect == 1, 2 * grid_side, jnp.where(aspect == 2, grid_side // 2, grid_side)
    ).astype(jnp.int32)[:, None]
    across = grid_width // WIN
    places = jnp.arange(tokens_frame, dtype=jnp.int32)[None, :]
    window = places // AREA
    inside = places % AREA
    grid_row = window // across * WIN + inside // WIN
    grid_col = window % across * WIN + inside % WIN
    forward_order = grid_row * grid_width + grid_col
    raster_row = places // grid_width
    raster_col = places % grid_width
    back_order = (
        (raster_row // WIN * across + raster_col // WIN) * AREA + raster_row % WIN * WIN + raster_col % WIN
    )
    return (forward_order, back_order)


def reorder(values, order):
    return jax.vmap(partial(jnp.take, axis=1))(values, order)


def pad_clips(values, split):
    return jnp.pad(values, [(0, -values.shape[0] % split)] + [(0, 0)] * (values.ndim - 1))


def gather_window(x, aspect, split):
    whole_x = pad_clips(lax.all_gather(x, "tensor", axis=2, tiled=True), split)
    aspect = pad_clips(aspect, split)
    t = lax.axis_index("tensor")
    clips = aspect.shape[0] // split
    mine = lax.dynamic_slice_in_dim(whole_x, t % split * clips, clips, 0)
    kinds = lax.dynamic_slice_in_dim(aspect, t % split * clips, clips, 0)
    order, _ = window_maps(kinds, whole_x.shape[2])
    return reorder(mine, lax.dynamic_slice_in_dim(order, t // split * AREA, AREA, 1))


def gather_raster(y, aspect, split, patches):
    every = lax.all_gather(y, "tensor", axis=0)
    count, clips, frames, _, width = every.shape
    every = every.reshape(count // split, split, clips, frames, AREA, width)
    every = jnp.transpose(every, (1, 2, 3, 0, 4, 5)).reshape(split * clips, frames, -1, width)
    _, back = window_maps(aspect, every.shape[2])
    t = lax.axis_index("tensor")
    return reorder(every[: aspect.shape[0]], lax.dynamic_slice_in_dim(back, t * patches, patches, 1))


def attention_piece(d, w_ref, wo_ref):
    rows = w_ref.shape[1] // 8
    part = wo_ref.shape[0] // 8
    qkv = [w_ref[m, pl.ds(pl.multiple_of(d * rows, rows), rows), :] for m in range(3)]
    out = wo_ref[pl.ds(pl.multiple_of(d * part, part), part), :]
    squares = [out[:, c * 128 : (c + 1) * 128] for c in range(out.shape[1] // 128)]
    return jnp.concatenate(qkv + [jnp.concatenate(squares, axis=0)], axis=1)


def pack_weights_kernel(place_ref, sw_ref, swo_ref, tw_ref, two_ref, w_in_ref, w_out_ref, heads_ref, hidden_ref):
    d = place_ref[1]
    heads_ref[0:64, :] = attention_piece(d, sw_ref, swo_ref)
    heads_ref[64:128, :] = attention_piece(d, tw_ref, two_ref)
    rows = pl.ds(pl.multiple_of(d * 64, 64), 64)
    hidden_ref[0:64, :] = w_in_ref[rows, :]
    hidden_ref[64:128, :] = w_out_ref[rows, :]


def pack_weights(place, *weights):
    outs = [shape((128, 512))] * 2
    return run(pack_weights_kernel, 0.01, (1,), (place, *weights), [SMEM] + whole_specs(weights), outs, whole_specs(outs))


def stack_kernel(place_ref, *refs):
    for j in range(4):
        refs[4][place_ref[0] ^ j] = refs[j][...]


def stack_pieces(place, pieces, after=()):
    outs = [shape((4,) + pieces[0].shape)]
    ins = (place, *pieces)
    return run(stack_kernel, 0.01, (1,), ins, [SMEM] + whole_specs(pieces), outs, whole_specs(outs), after=after)[0]


def gather_shard(shard):
    rows = shard.shape[0] // lax.axis_size("dp")
    piece = lax.dynamic_slice_in_dim(shard, lax.axis_index("dp") * rows, rows, 0)
    whole_w = lax.all_gather(piece, ("tensor", "dp"), axis=0, tiled=True)
    return whole_w.reshape((-1,) + shard.shape)


def gather_attention(w, wo):
    width = wo.shape[1]
    heads = gather_shard(w.reshape(-1, w.shape[2])).reshape((-1,) + w.shape)
    heads = jnp.moveaxis(heads, 0, 2).reshape(3, width, 4, -1).transpose(2, 1, 0, 3).reshape(4, width, -1)
    out = gather_shard(wo).reshape(4, width // 4, 4, width // 4).transpose(0, 2, 1, 3).reshape(4, width, -1)
    return jnp.concatenate([heads, out], axis=2)[None]


def gather_hidden(w_in, w_out):
    columns = jnp.moveaxis(gather_shard(w_in), 0, 1).reshape(w_in.shape[0], 4, -1)
    rows = gather_shard(w_out).reshape(4, -1, w_out.shape[1])
    return jnp.concatenate([jnp.moveaxis(columns, 1, 0), rows], axis=1)[None]


def add_kernel(count, *refs):
    operands, outs = refs[:count], refs[count:]
    for i, out in enumerate(outs):
        total = operands[0][i].astype(F32)
        for operand in operands[1:]:
            total = total + operand[i].astype(F32)
        out[...] = total.astype(out.dtype)


def add_blocks(operands, dtype=BF16, after=()):
    outs = [shape(operands[0].shape[1:], dtype)] * operands[0].shape[0]
    return run(
        partial(add_kernel, len(operands)), 0.01, (1,), operands, whole_specs(operands), outs, whole_specs(outs), after=after
    )


def reduce_core(even, odd, after=()):
    return add_blocks([even, swap(odd, "dp", 1)], after=after)


def chips_kernel(*refs):
    ins, out_refs = refs[:8], refs[8:]
    for j, out in enumerate(out_refs):
        at = 0
        for group in (ins[:4], ins[4:]):
            rows = group[0].shape[1]
            out[at : at + rows] = sum(ref[j].astype(F32) for ref in group).astype(BF16)
            at += rows


def chip_parts(near):
    return [near[0]] + [swap(near[i], "dp", 2 * i) for i in (1, 2, 3)]


def reduce_chips(ours, others, after=()):
    outs = [shape((ours[0].shape[1] + others[0].shape[1], ours[0].shape[2]))] * 4
    ins = (*ours, *others)
    return run(chips_kernel, 0.01, (1,), ins, whole_specs(ins), outs, whole_specs(outs), after=after)


def finish_kernel(place_ref, *refs):
    parts, (s_qkv, s_out, t_qkv, t_out, *norms) = refs[:4], refs[4:-1]
    sums_ref = refs[-1]
    total = sum(part[...].astype(F32) for part in parts)
    for block, qkv_ref, out_ref in ((total[0:64], s_qkv, s_out), (total[80:144], t_qkv, t_out)):
        for m in range(3):
            qkv_ref[m] = block[:, m * 128 : (m + 1) * 128]
        out_ref[...] = block[:, 384:512]
    sums_ref[...] = total[64:72]
    d = place_ref[1]
    pair = sums_ref[:, pl.ds(pl.multiple_of(d // 2 * 128, 128), 128)]
    mine = jnp.where(d % 2 == 0, pair[:, 0:64], pair[:, 64:128])
    for n, ref in enumerate(norms):
        ref[...] = mine[n : n + 1]


def finish(place, mine):
    ins = [place, mine[0]] + [swap(mine[j], "tensor", j) for j in (1, 2, 3)]
    outs = [shape((3, 64, 128), F32), shape((64, 128), F32)] * 2 + [shape((1, 64), F32)] * 6
    return run(
        finish_kernel, 0.01, (1,), ins, [SMEM] + whole_specs(ins[1:]), outs, whole_specs(outs), [pltpu.VMEM((8, 512), F32)]
    )


def scatter_grad(grads):
    flat = jnp.concatenate([g.astype(BF16).reshape(g.shape[0], -1) for g in grads], axis=1)
    flat = lax.psum_scatter(flat, "dp", scatter_dimension=0, tiled=True)
    pieces, offset = [], 0
    count = lax.axis_size("tensor")
    for g in grads:
        size = math.prod(g.shape[1:])
        piece = flat[:, offset : offset + size].reshape((flat.shape[0],) + g.shape[1:])
        pieces.append(jnp.moveaxis(piece, 2, 0).reshape(count, flat.shape[0], -1))
        offset += size
    mine = lax.psum_scatter(jnp.concatenate(pieces, axis=2), "tensor", scatter_dimension=0, tiled=True)[0]
    results, offset = [], 0
    for g in grads:
        size = g.shape[1] * g.shape[3]
        results.append(mine[:, offset : offset + size].reshape(-1, g.shape[1], g.shape[3]).astype(F32))
        offset += size
    return results


def in_order(even, odd):
    blocks = jnp.stack([even[:, :, :64], odd[:, :, :64]], axis=1).reshape(8, 4, 64, 4, 128)
    return jnp.transpose(blocks, (0, 2, 3, 1, 4)).reshape(512, 4, 512)


def shards(
    gen_tokens, rec_grad, adv_grad, gen_aspect, gen_frames, disc_tokens, disc_aspect, disc_frames, disc_labels,
    logit_gain, adv_weight, train_step, ln1_gain, ln1_bias, spatial_qkv, spatial_out, ln2_gain, ln2_bias,
    temporal_qkv, temporal_out, ln3_gain, ln3_bias, mlp_in, mlp_out,
):
    tensor = lax.axis_size("tensor")
    dp_at, tensor_at = lax.axis_index("dp"), lax.axis_index("tensor")
    local, frames, patches, width = gen_tokens.shape
    windows = patches * tensor // AREA
    direct = tensor == 4 and windows == 4 and lax.axis_size("dp") == 8
    split = max(tensor // windows, 1)
    clips = -(-local // split)
    place = jnp.stack([tensor_at, dp_at]).astype(jnp.int32)
    vectors = [v.reshape(1, -1) for v in (ln1_gain, ln1_bias, ln2_gain, ln2_bias, ln3_gain, ln3_bias, logit_gain)]
    g1, b1, g2, b2, g3, b3, logit = vectors

    step_value = train_step.astype(F32)
    ramp = adv_weight * step_value / (step_value + HALF)

    def mine(values):
        return lax.dynamic_slice_in_dim(pad_clips(values, split), tensor_at % split * clips, clips, 0)

    count = mine(disc_frames)
    sign = (2 * mine(disc_labels) - 1).astype(F32)
    aspects = (mine(gen_aspect), mine(disc_aspect))

    def flat(x):
        return x.reshape(x.shape[0], -1, width)

    if direct:
        x_gen, x_disc, rec, adv = (flat(v) for v in (gen_tokens, disc_tokens, rec_grad, adv_grad))
        heads, hidden = pack_weights(place, spatial_qkv, spatial_out, temporal_qkv, temporal_out, mlp_in, mlp_out)
        gen_parts = pack(place, gen_aspect, x_gen, (heads,))
        disc_parts = pack(place, disc_aspect, x_disc, gen_parts)
        dy, *dy_parts = pack_grad(place, gen_aspect, gen_frames, ramp, rec, adv, disc_parts)
        heads = [heads] + [swap(heads, "tensor", j) for j in (1, 2, 3)]
        heads = stack_pieces(place, heads, (dy,))
        space_w = time_w = lax.all_gather(heads, "dp", axis=0)
        gen_parts = exchange(gen_parts)
        hidden = [hidden] + [swap(hidden, "tensor", j) for j in (1, 2, 3)]
        hidden = stack_pieces(place, hidden, (heads, *gen_parts))
        mlp_w = lax.all_gather(hidden, "dp", axis=0)
        disc_parts, dy_parts = exchange(disc_parts), exchange(dy_parts)
    else:
        place = jnp.zeros_like(place)
        space_w, time_w = gather_attention(spatial_qkv, spatial_out), gather_attention(temporal_qkv, temporal_out)
        mlp_w = gather_hidden(mlp_in, mlp_out)
        x_gen = flat(gather_window(gen_tokens, gen_aspect, split))
        x_disc = flat(gather_window(disc_tokens, disc_aspect, split))
        live = jnp.arange(frames, dtype=jnp.int32)[None, :] < gen_frames[:, None]
        total = rec_grad.astype(F32) + ramp[0] * adv_grad.astype(F32)
        dy = jnp.where(live[:, :, None, None], total, 0.0).astype(BF16)
        dy = flat(gather_window(dy, gen_aspect, split))
        gen_parts, disc_parts, dy_parts = (), (), ()

    sf = space_forward(place, aspects[0], x_gen, gen_parts, g1, b1, space_w, 2 * clips, (), (hidden,) if direct else ())
    tf = time_forward(sf[0], g2, b2, time_w, clips)
    sf = space_forward(place, aspects[1], x_disc, disc_parts, g1, b1, space_w, 2 * clips, sf, tf[:1])
    x1, s_qkv, s_p, s_o, xw = sf
    x2, t_qkv, t_p, t_o = time_forward(x1, g2, b2, time_w, clips, tf)
    gen = mlp_gen(direct, place, aspects[0], x2, g3, b3, mlp_w, dy, dy_parts)
    y_gen = exchange(gen[8:]) if direct else ()
    y, dx2, ff_blocks, ff_dg, ff_db, *y_sends = mlp_disc(
        direct, sign, count, place, x2, g3, b3, mlp_w, logit, gen[2:4], gen[4:6], gen[6:8], gen[:2]
    )
    y_disc = exchange(y_sends) if direct else ()
    if direct:
        ff_mine = lax.psum_scatter(ff_blocks, "dp", scatter_dimension=0)
    dx1, t_dg, t_db, t_even, t_odd = time_backward(place, dx2, x1, g2, b2, time_w, t_qkv, t_p, t_o, y_gen)
    back = space_backward(direct, dx1, xw, g1, b1, space_w, s_qkv, s_p, (), y_disc)
    kept, (dx0_gen, s_dg, s_db, *gen_sends) = back[:3], back[3:]
    if direct:
        t_near = reduce_core(t_even, t_odd, (dx0_gen,))
        gen_parts = exchange(gen_sends)
        t_parts = chip_parts(t_near)
    back = space_backward(
        direct, dx1, xw, g1, b1, space_w, s_qkv, s_p, kept, (t_near[0],) if direct else ()
    )
    kept, (dx0_disc, d_dg, d_db, *disc_sends) = back[:3], back[3:]
    disc_parts = exchange(disc_sends) if direct else ()
    dqkv, low, a = kept
    zero = jnp.zeros_like(t_dg)
    s_even, s_odd = space_grad(
        place, a, dqkv, low, s_o, (s_dg, d_dg, s_db, d_db, t_dg, zero, t_db, zero, ff_dg, zero, ff_db, zero),
        (dx0_disc, *t_parts) if direct else (),
    )

    part = width // tensor
    if direct:
        ff_share = lax.psum_scatter(ff_mine, "tensor", scatter_dimension=0).astype(F32)
        y_gen = join_raster(place, gen_aspect, y, (y_gen,), 0, 6, (s_even,))
        near = reduce_core(s_even, s_odd, (*gen_parts, *y_gen, disc_parts[0]))
        dx_gen = join_raster(place, gen_aspect, dx0_gen, (gen_parts,), 0, JOIN, near[:1])
        y_disc = join_raster(place, disc_aspect, y, (y_disc,), clips, JOIN, near[:1])
        ours = reduce_chips(chip_parts(near), t_parts, (*dx_gen, *y_disc, ff_share))
        dx_disc = join_raster(place, disc_aspect, dx0_disc, (disc_parts,), 0, JOIN, ours[:1])
        s_qkv, s_out, t_qkv, t_out, *small = finish(place, ours)
        shares = (s_qkv, s_out.T, t_qkv, t_out.T)
        small = [n[0] for n in small]
        in_share, out_share = ff_share[:64], ff_share[64:]
        y_gen, y_disc, dx_gen, dx_disc = (v.reshape(gen_tokens.shape) for v in (*y_gen, *y_disc, *dx_gen, *dx_disc))
    else:
        y_gen, y_disc, dx_gen, dx_disc = (
            gather_raster(v.reshape(clips, frames, AREA, width), aspect, split, patches)
            for v, aspect in ((y[:clips], gen_aspect), (y[clips:], disc_aspect), (dx0_gen, gen_aspect), (dx0_disc, disc_aspect))
        )
        ff = jnp.transpose(ff_blocks.reshape(8, 4, 2, 64, 512), (0, 3, 2, 1, 4)).reshape(width, 2, tensor, -1)
        ff_share = scatter_grad([ff])[0]
        in_share, out_share = ff_share[:, 0], ff_share[:, 1]
        shares = []
        for even, odd in ((s_even, s_odd), (t_even, t_odd)):
            block = scatter_grad([in_order(even, odd).reshape(width, 4, tensor, part)])[0]
            shares += [jnp.moveaxis(block[:, :3], 1, 0), block[:, 3].T]
        small = lax.psum(s_even[0, 0, 64:70].astype(F32), ("dp", "tensor"))
        piece = width // lax.axis_size("dp")
        small = lax.dynamic_slice_in_dim(small, dp_at * piece, piece, 1)

    return (
        y_gen, dx_gen, y_disc, dx_disc,
        small[0], small[1], shares[0], shares[1], small[2], small[3], shares[2], shares[3],
        small[4], small[5], in_share, out_share.T,
    )


def solution(mesh):
    tokens = P("dp", None, "tensor", None)
    vector, clip = P(), P("dp")
    qkv, rows, cols = P(None, None, "tensor"), P("tensor", None), P(None, "tensor")
    in_specs = (
        (tokens,) * 3 + (clip,) * 2 + (tokens,) + (clip,) * 3 + (vector,) * 5
        + (qkv, rows, vector, vector, qkv, rows, vector, vector, cols, rows)
    )
    block = (clip, clip, P(None, "dp", "tensor"), P("tensor", "dp"))
    out_specs = (tokens,) * 4 + block * 2 + (clip, clip, P("dp", "tensor"), P("tensor", "dp"))
    return jax.shard_map(shards, mesh=mesh, in_specs=in_specs, out_specs=out_specs, check_vma=False)
```

```python
from functools import partial
import math

import jax
import jax.numpy as jnp
from jax import lax
from jax.experimental import pallas as pl
from jax.experimental.pallas import tpu as pltpu
from jax.sharding import PartitionSpec as P

HEAD_DIM = 64
WIN = 8
AREA = WIN * WIN
HALF = 5000
EPS = 1e-05
F32 = jnp.float32
BF16 = jnp.bfloat16
VMEM_LIMIT = 58 * 1024 * 1024
JOIN = 0.01
COEFS = tuple(math.sqrt(math.pi / 2.0) * a for a in (0.254829592, -0.284496736, 1.421413741, -1.453152027, 1.061405429))

NT = (((1,), (1,)), ((), ()))
TN = (((0,), (0,)), ((), ()))


def dot(lhs, rhs):
    return jnp.dot(lhs, rhs, preferred_element_type=F32)


def dot_nt(lhs, rhs):
    return lax.dot_general(lhs, rhs, NT, preferred_element_type=F32)


def dot_tn(lhs, rhs):
    return lax.dot_general(lhs, rhs, TN, preferred_element_type=F32)


def normalize(value):
    average = jnp.mean(value, axis=-1, keepdims=True)
    centred = value - average
    variance = jnp.mean(centred * centred, axis=-1, keepdims=True)
    scale = lax.rsqrt(variance + EPS)
    return centred * scale, scale


def norm_backward(unit, scale, gain, grad):
    scaled = grad * gain
    inner = scaled - jnp.mean(scaled, axis=-1, keepdims=True)
    return scale * (inner - unit * jnp.mean(scaled * unit, axis=-1, keepdims=True))


def row_sums(values):
    return jnp.sum(values.reshape(-1, 8, values.shape[-1]), axis=0)


HBM = pl.BlockSpec(memory_space=pltpu.HBM)
SMEM = pl.BlockSpec(memory_space=pltpu.SMEM)


def run(kernel, microseconds, grid, ins, in_specs, outs, out_specs, scratch=(), after=(), bases=()):
    ins, after, bases = tuple(ins), tuple(after), tuple(bases)
    count, extra = len(ins), len(after) + len(bases)

    def body(*refs):
        kernel(*refs[:count], *refs[count + extra :])

    return pl.pallas_call(
        body,
        grid=grid,
        in_specs=list(in_specs) + [HBM] * extra,
        out_specs=list(out_specs),
        out_shape=list(outs),
        scratch_shapes=list(scratch),
        input_output_aliases={count + len(after) + i: i for i in range(len(bases))},
        cost_estimate=pl.CostEstimate(flops=int(microseconds * 2.5e9), bytes_accessed=0, transcendentals=0),
        compiler_params=pltpu.CompilerParams(
            dimension_semantics=("arbitrary",) * len(grid), vmem_limit_bytes=VMEM_LIMIT
        ),
    )(*ins, *after, *bases)


def shape(dims, dtype=BF16):
    return jax.ShapeDtypeStruct(tuple(dims), dtype)


def whole(dims):
    zeros = (0,) * len(dims)
    return pl.BlockSpec(tuple(dims), lambda i: zeros)


def per_clip(dims, first=0, count=None):
    zeros = (0,) * (len(dims) - 1)
    count = count or dims[0]
    return pl.BlockSpec((1,) + tuple(dims[1:]), lambda i: (first + jnp.clip(i, 0, count - 1),) + zeros)


def join_rows(w_ref, part):
    return jnp.concatenate(
        [
            jnp.concatenate([part(w_ref, i, j) for j in range(w_ref.shape[1])], axis=1)
            for i in range(w_ref.shape[0])
        ],
        axis=0,
    )


def head_weight(w_ref, m):
    return join_rows(w_ref, lambda ref, i, j: ref[i, j, :, m * 128 : (m + 1) * 128])


def out_weight(w_ref):
    part = w_ref.shape[2] // 4
    return jnp.concatenate(
        [
            jnp.concatenate([w_ref[i, j, c * part : (c + 1) * part, 384:512] for c in range(4)], axis=1)
            for j in range(w_ref.shape[1])
            for i in range(w_ref.shape[0])
        ],
        axis=0,
    )


def hidden_weight(w_ref, j, n):
    part = w_ref.shape[2] // 2
    return jnp.concatenate([w_ref[i, j, n * part : (n + 1) * part, :] for i in range(w_ref.shape[0])], axis=0)


def head_mask(dtype):
    rows = lax.broadcasted_iota(jnp.int32, (256, 256), 0) // HEAD_DIM
    cols = lax.broadcasted_iota(jnp.int32, (256, 256), 1) // HEAD_DIM
    return jnp.where(rows == cols, 1.0, 0.0).astype(dtype)


def spread(values, mask):
    return jnp.concatenate([values] * 4, axis=0) * mask


def pair_product(scores, values, low_lane):
    parts = []
    for c in range(2):
        full = dot_tn(scores[:, c * 128 : (c + 1) * 128], values[:, c * 128 : (c + 1) * 128])
        parts.append(jnp.where(low_lane, full[:64], full[64:]))
    return jnp.concatenate(parts, axis=1)


def one_hot(source, count):
    rows = source.shape[0]
    inside = lax.broadcasted_iota(jnp.int32, (rows, count), 0) % 8
    cols = lax.broadcasted_iota(jnp.int32, (rows, count), 1)
    return jnp.where((source >= 0) & (cols == source * 8 + inside), 1.0, 0.0).astype(BF16)


def chunk_ids():
    return lax.broadcasted_iota(jnp.int32, (AREA, 1), 0) // 8


def send_source(aspect, t):
    c = chunk_ids()
    square = jnp.where(c < 4, 2 * c + 1 - t % 2, -1)
    wide = jnp.where(
        c < 2, 4 * c + (t ^ 1), jnp.where(c < 4, -1, jnp.where(c < 6, 4 * (c - 4) + (t ^ 2), 4 * (c - 6) + (t ^ 3)))
    )
    return jnp.where(aspect == 0, square, jnp.where(aspect == 1, wide, -1))


def window_source(aspect, t):
    c = chunk_ids()
    square = jnp.where(c < 4, 2 * c + t % 2, c + 4)
    wide = jnp.where(c < 2, 4 * c + t, jnp.where(c < 4, c + 10, jnp.where(c < 6, c + 4, c + 8)))
    return jnp.where(aspect == 0, square, jnp.where(aspect == 1, wide, c))


def raster_source(aspect, t):
    c = chunk_ids()
    square = c // 2 + jnp.where(c % 2 == t % 2, 0, 8)
    way = (c % 4) ^ t
    wide = c // 4 + jnp.where(way == 0, 0, jnp.where(way == 1, 8, jnp.where(way == 2, 12, 14)))
    return jnp.where(aspect == 0, square, jnp.where(aspect == 1, wide, c))


def write_sends(values, refs):
    if not refs:
        return
    for f in range(values.shape[0] // AREA):
        base = f * AREA
        refs[0][0, f * 32 : (f + 1) * 32, :] = values[base + 32 : base + 64]
        refs[1][0, f * 16 : (f + 1) * 16, :] = values[base + 16 : base + 32]
        refs[2][0, f * 16 : (f + 1) * 16, :] = values[base + 48 : base + 64]


def pack_rows(values, select, refs):
    for f in range(values.shape[0] // AREA):
        moved = dot(select, values[f * AREA : (f + 1) * AREA]).astype(BF16)
        refs[0][0, f * 32 : (f + 1) * 32, :] = moved[:32]
        refs[1][0, f * 16 : (f + 1) * 16, :] = moved[32:48]
        refs[2][0, f * 16 : (f + 1) * 16, :] = moved[48:]


def join_parts(source, own_ref, part_refs, out_ref):
    select = one_hot(source, 2 * AREA)
    for f in range(out_ref.shape[1] // AREA):
        rows = [own_ref[0, f * AREA : (f + 1) * AREA, :]]
        rows += [ref[0, f * size : (f + 1) * size, :] for ref, size in zip(part_refs, (32, 16, 16))]
        out_ref[0, f * AREA : (f + 1) * AREA, :] = dot(select, jnp.concatenate(rows, axis=0)).astype(BF16)


def pack_kernel(place_ref, aspect_ref, x_ref, *send_refs):
    select = one_hot(send_source(aspect_ref[pl.program_id(0)], place_ref[0]), AREA)
    pack_rows(x_ref[0], select, send_refs)


def pack_grad_kernel(place_ref, aspect_ref, count_ref, ramp_ref, rec_ref, adv_ref, dy_ref, *send_refs):
    clip = pl.program_id(0)
    frame = lax.broadcasted_iota(jnp.int32, (rec_ref.shape[1], 1), 0) // AREA
    total = rec_ref[0].astype(F32) + ramp_ref[0] * adv_ref[0].astype(F32)
    dy_ref[0] = jnp.where(frame < count_ref[clip], total, 0.0).astype(BF16)
    select = one_hot(send_source(aspect_ref[clip], place_ref[0]), AREA)
    pack_rows(dy_ref[0], select, send_refs)


def join_kernel(place_ref, aspect_ref, own_ref, r1_ref, r2_ref, r3_ref, out_ref):
    source = raster_source(aspect_ref[pl.program_id(0)], place_ref[0])
    join_parts(source, own_ref, (r1_ref, r2_ref, r3_ref), out_ref)


def send_shapes(x):
    clips, rows, width = x.shape
    return [shape((clips, rows // part, width)) for part in (2, 4, 4)]


def head_spec(w, n):
    if w.shape[2] != 128:
        return whole(w.shape)
    return pl.BlockSpec(w.shape[:2] + (64, w.shape[3]), lambda i: (0, 0, n, 0))


def clip_specs(arrays, first=0, count=None):
    return [per_clip(a.shape, first, count) for a in arrays]


def whole_specs(arrays):
    return [whole(a.shape) for a in arrays]


def pack(place, aspect, x, after=()):
    outs = send_shapes(x)
    return run(
        pack_kernel, 0.01, x.shape[:1], (place, aspect, x), [SMEM, SMEM, per_clip(x.shape)], outs, clip_specs(outs), after=after
    )


def pack_grad(place, aspect, count, ramp, rec, adv, after=()):
    outs = [shape(rec.shape)] + send_shapes(rec)
    ins = (place, aspect, count, ramp, rec, adv)
    return run(
        pack_grad_kernel, 4, rec.shape[:1], ins, [SMEM] * 4 + clip_specs((rec, adv)), outs, clip_specs(outs), after=after
    )


def join_raster(place, aspect, own, parts, first, microseconds, after=()):
    clips = parts[0][0].shape[0]
    outs = [shape((clips,) + own.shape[1:])]
    ins = (place, aspect, own, *parts[0])
    in_specs = [SMEM] * 2 + clip_specs((own,), first, clips) + clip_specs(parts[0])
    return run(join_kernel, microseconds, (clips,), ins, in_specs, outs, clip_specs(outs), after=after)


def exchange(parts):
    return tuple(swap(part, "tensor", way) for way, part in zip((1, 2, 3), parts))


def swap(x, axis, way):
    return lax.ppermute(x, axis, [(i, i ^ way) for i in range(lax.axis_size(axis))])


def place_products(place_ref, block_ref, out_refs, cols):
    for k in range(8):
        rows = pl.ds(pl.multiple_of((place_ref[1] ^ k) * 64, 64), 64)
        for j in range(4):
            lanes = pl.ds(pl.multiple_of((place_ref[0] ^ j) * 128, 128), 128)
            out_refs[k % 2][k // 2, j, 0:64, cols] = block_ref[rows, lanes].astype(BF16)


def attention_products(place_ref, a_ref, dqkv_ref, low_ref, o_ref, turned_ref, block_ref, out_refs):
    def flat(ref, cols=slice(None)):
        values = ref[:, :, cols]
        return values.reshape(-1, values.shape[-1])

    turned_ref[...] = flat(a_ref).T
    for m in range(3):
        block_ref[...] = dot(turned_ref[...], flat(dqkv_ref, slice(m * 512, (m + 1) * 512)))
        place_products(place_ref, block_ref, out_refs, slice(m * 128, (m + 1) * 128))
    turned_ref[...] = flat(low_ref).T
    block_ref[...] = dot(turned_ref[...], flat(o_ref))
    place_products(place_ref, block_ref, out_refs, slice(384, 512))


def product_scratch(clips, rows, width):
    return [
        pltpu.VMEM((clips, rows, 3 * width), BF16),
        *[pltpu.VMEM((clips, rows, width), BF16)] * 3,
        pltpu.VMEM((width, clips * rows), BF16),
        pltpu.VMEM((width, width), F32),
    ]


def window_blocks(rows):
    return [(w, g) for w in range(rows // AREA) for g in range(2)]


def low_lanes():
    return lax.broadcasted_iota(jnp.int32, (64, 128), 1) < HEAD_DIM


def space_forward_kernel(parts, place_ref, aspect_ref, x_ref, *refs):
    part_refs = refs[:parts]
    gain_ref, bias_ref, w_ref, x1_ref, qkv_ref, p_ref, o_ref, xw_ref, a_ref = refs[parts:]
    rows = x_ref.shape[1]
    if parts:
        join_parts(window_source(aspect_ref[pl.program_id(0)], place_ref[0]), x_ref, part_refs, xw_ref)
    else:
        xw_ref[...] = x_ref[...]
    x = xw_ref[0].astype(F32)
    unit, _ = normalize(x)
    a_ref[...] = (unit * gain_ref[...] + bias_ref[...]).astype(BF16)
    for j in range(3):
        qkv_ref[0, :, j * 512 : (j + 1) * 512] = dot(a_ref[...], head_weight(w_ref, j)).astype(BF16)
    mask, low_lane = head_mask(BF16), low_lanes()

    def part(j, w, g):
        return qkv_ref[0, w * AREA : (w + 1) * AREA, j * 512 + g * 256 : j * 512 + (g + 1) * 256]

    blocks = window_blocks(rows)
    scores = [dot_nt(part(1, w, g), spread(part(0, w, g), mask)) * 0.125 for w, g in blocks]
    for s, (w, g) in zip(scores, blocks):
        e = jnp.exp(s - jnp.max(s, axis=0, keepdims=True))
        p_ref[0, 2 * w + g] = (e * (1.0 / jnp.sum(e, axis=0, keepdims=True))).astype(BF16)
    for w, g in blocks:
        attended = pair_product(p_ref[0, 2 * w + g], part(2, w, g), low_lane)
        o_ref[0, w * AREA : (w + 1) * AREA, g * 256 : (g + 1) * 256] = attended.astype(BF16)
    x1_ref[0] = x + dot(o_ref[0], out_weight(w_ref))


def space_forward(place, aspect, x, parts, gain, bias, w, total, bases=(), after=()):
    clips, rows, width = x.shape
    first = total - clips if bases else 0
    outs = [
        shape((total, rows, width), F32),
        shape((total, rows, 3 * width)),
        shape((total, 2 * rows // AREA, AREA, 256)),
        shape((total, rows, width)),
        shape((total, rows, width)),
    ]
    return run(
        partial(space_forward_kernel, len(parts)), 10, (clips,), (place, aspect, x, *parts, gain, bias, w),
        [SMEM] * 2 + clip_specs((x, *parts)) + whole_specs((gain, bias)) + [head_spec(w, 0)], outs, clip_specs(outs, first, clips),
        [pltpu.VMEM((rows, width), BF16)], after, bases,
    )


def space_backward_clip(dx1, x, gain, bias, w_ref, qkv_ref, p_ref, dqkv_ref, low_ref, a_ref, do_ref):
    low_ref[...] = dx1.astype(BF16)
    do_ref[...] = dot_nt(low_ref[...], out_weight(w_ref)).astype(BF16)
    mask, low_lane = head_mask(BF16), low_lanes()

    def part(j, w, g):
        return qkv_ref[0, w * AREA : (w + 1) * AREA, j * 512 + g * 256 : j * 512 + (g + 1) * 256]

    def grad(w, g):
        return spread(do_ref[w * AREA : (w + 1) * AREA, g * 256 : (g + 1) * 256], mask)

    def put(j, w, g, values):
        dqkv_ref[w * AREA : (w + 1) * AREA, j * 512 + g * 256 : j * 512 + (g + 1) * 256] = values.astype(BF16)

    blocks = window_blocks(low_ref.shape[0])
    grad_probs = [dot_nt(part(2, w, g), grad(w, g)) for w, g in blocks]
    for w, g in blocks:
        put(2, w, g, dot(p_ref[0, 2 * w + g], grad(w, g)))
    grad_scores = []
    for dp, (w, g) in zip(grad_probs, blocks):
        p = p_ref[0, 2 * w + g].astype(F32)
        weighted = p * dp
        grad_scores.append((weighted - p * jnp.sum(weighted, axis=0, keepdims=True)).astype(BF16))
    for ds, (w, g) in zip(grad_scores, blocks):
        put(1, w, g, dot(ds, spread(part(0, w, g), mask)) * 0.125)
    for ds, (w, g) in zip(grad_scores, blocks):
        put(0, w, g, pair_product(ds, part(1, w, g), low_lane) * 0.125)
    da = dot_nt(dqkv_ref[...], jnp.concatenate([head_weight(w_ref, j) for j in range(3)], axis=1))
    unit, scale = normalize(x)
    a_ref[...] = (unit * gain + bias).astype(BF16)
    return dx1 + norm_backward(unit, scale, gain, da), row_sums(da * unit), row_sums(da)


def space_backward_kernel(
    dx1_ref, x_ref, gain_ref, bias_ref, w_ref, qkv_ref, p_ref, dqkv_ref, low_ref, a_ref, dx0_ref, dg_ref, db_ref, *rest
):
    *send_refs, do_ref = rest

    @pl.when(pl.program_id(0) == 0)
    def _():
        dg_ref[...] = jnp.zeros_like(dg_ref)
        db_ref[...] = jnp.zeros_like(db_ref)

    dx0, dg, db = space_backward_clip(
        dx1_ref[0], x_ref[0].astype(F32), gain_ref[...], bias_ref[...], w_ref, qkv_ref, p_ref,
        dqkv_ref.at[0], low_ref.at[0], a_ref.at[0], do_ref,
    )
    dx0_ref[0] = dx0.astype(BF16)
    write_sends(dx0_ref[0], send_refs)
    dg_ref[...] += dg
    db_ref[...] += db


def space_backward(direct, dx1, x, gain, bias, w, qkv, p, bases=(), after=()):
    total, rows, width = x.shape
    clips = total // 2
    first = clips if bases else 0
    kept = [shape((total, rows, 3 * width))] + [shape(x.shape)] * 2
    outs = [shape((clips, rows, width))]
    sums = [shape((8, width), F32)] * 2
    sends = send_shapes(outs[0]) if direct else []
    return run(
        space_backward_kernel, 10, (clips,), (dx1, x, gain, bias, w, qkv, p),
        clip_specs((dx1, x), first, clips) + whole_specs((gain, bias)) + [head_spec(w, 0)] + clip_specs((qkv, p), first, clips),
        kept + outs + sums + sends, clip_specs(kept, first, clips) + clip_specs(outs) + whole_specs(sums) + clip_specs(sends),
        [pltpu.VMEM((rows, width), BF16)], after, bases,
    )


def space_grad_kernel(place_ref, a_ref, dqkv_ref, low_ref, o_ref, *refs):
    norm_refs, (even_ref, odd_ref, turned_ref, block_ref) = refs[:-4], refs[-4:]
    i = pl.program_id(0)

    def place_block(m):
        place_products(place_ref, block_ref, (even_ref, odd_ref), slice(m * 128, (m + 1) * 128))

    @pl.when(i == 0)
    def _():
        turned_ref[...] = a_ref[...].T
        sums = [
            jnp.sum(left[...] + right[...], axis=0, keepdims=True) for left, right in zip(norm_refs[::2], norm_refs[1::2])
        ]
        sums = jnp.concatenate(sums + [jnp.zeros((16 - len(sums), 512), F32)], axis=0).astype(BF16)
        for ref in (even_ref, odd_ref):
            for k in range(4):
                for j in range(4):
                    ref[k, j, 64:80, :] = sums

    for m in range(3):

        @pl.when(i == m)
        def _():
            block_ref[...] = dot(turned_ref[...], dqkv_ref[...])
            place_block(m)

    @pl.when(i == 3)
    def _():
        turned_ref[...] = low_ref[...].T
        block_ref[...] = dot(turned_ref[...], o_ref[...])
        place_block(3)


def space_grad(place, a, dqkv, low, o, norms, after=()):
    a, dqkv, low, o = (v.reshape(-1, v.shape[-1]) for v in (a, dqkv, low, o))
    rows, width = a.shape
    outs = [shape((4, 4, 80, 512))] * 2
    column = pl.BlockSpec((rows, width), lambda i: (0, jnp.minimum(i, 2)))
    return run(
        space_grad_kernel, 6, (4,), (place, a, dqkv, low, o, *norms),
        [SMEM, whole(a.shape), column] + whole_specs((low, o, *norms)), outs, whole_specs(outs),
        [pltpu.VMEM((width, rows), BF16), pltpu.VMEM((width, width), F32)], after,
    )


def head_select(frame):
    rows = lax.broadcasted_iota(jnp.int32, (512, 128), 0) // HEAD_DIM
    cols = lax.broadcasted_iota(jnp.int32, (512, 128), 1) - 8 * frame
    return jnp.where(rows == cols, 1.0, 0.0).astype(BF16)


def head_expand(frame):
    rows = lax.broadcasted_iota(jnp.int32, (128, 512), 0) - 8 * frame
    cols = lax.broadcasted_iota(jnp.int32, (128, 512), 1) // HEAD_DIM
    return jnp.where(rows == cols, 1.0, 0.0).astype(BF16)


def head_sums(products, selector, exact):
    high = products.astype(BF16)
    if not exact:
        return dot(high, selector)
    rest = (products - high.astype(F32)).astype(BF16)
    return dot(high, selector) + dot(rest, selector)


def time_scores(frames, left, right, exact=True):
    totals = [None] * frames
    for t in range(frames):
        lhs = left(t).astype(F32)
        stacked = jnp.concatenate([lhs * right(f).astype(F32) for f in range(t + 1)], axis=0)
        sums = head_sums(stacked, head_select(t), exact)
        for f in range(t + 1):
            part = sums[f * AREA : (f + 1) * AREA]
            totals[f] = part if totals[f] is None else totals[f] + part
    return totals


def time_forward_kernel(x_ref, gain_ref, bias_ref, w_ref, x2_ref, qkv_ref, p_ref, o_ref, a_ref):
    frames = x_ref.shape[1] // AREA
    x = x_ref[0]
    unit, _ = normalize(x)
    a_ref[...] = (unit * gain_ref[...] + bias_ref[...]).astype(BF16)
    for j in range(3):
        qkv_ref[0, :, j * 512 : (j + 1) * 512] = dot(a_ref[...], head_weight(w_ref, j)).astype(BF16)

    def part(j):
        return lambda f: qkv_ref[0, f * AREA : (f + 1) * AREA, j * 512 : (j + 1) * 512]

    scores = time_scores(frames, part(0), part(1))
    lane = lax.broadcasted_iota(jnp.int32, (AREA, 128), 1)
    scores = [jnp.where(lane >= 8 * f, s * 0.125, -1e30) for f, s in enumerate(scores)]
    top = scores[0]
    for s in scores[1:]:
        top = jnp.maximum(top, s)
    exps = [jnp.exp(s - top) for s in scores]
    inverse = 1.0 / sum(exps)
    probs = [e * inverse for e in exps]
    for f in range(frames):
        p_ref[0, f * AREA : (f + 1) * AREA, :] = probs[f]
    low = [p.astype(BF16) for p in probs]
    values = part(2)
    for t in range(frames):
        wide = dot(jnp.concatenate(low[: t + 1], axis=0), head_expand(t))
        total = None
        for f in range(t + 1):
            term = wide[f * AREA : (f + 1) * AREA] * values(f).astype(F32)
            total = term if total is None else total + term
        o_ref[0, t * AREA : (t + 1) * AREA, :] = total.astype(BF16)
    x2_ref[0] = x + dot(o_ref[0], out_weight(w_ref))


def time_forward(x, gain, bias, w, clips, bases=(), after=()):
    total, rows, width = x.shape
    first = total - clips if bases else 0
    outs = [
        shape((total, rows, width), F32),
        shape((total, rows, 3 * width)),
        shape((total, rows, 128), F32),
        shape((total, rows, width)),
    ]
    return run(
        time_forward_kernel, 10, (clips,), (x, gain, bias, w),
        clip_specs((x,), first, clips) + whole_specs((gain, bias)) + [head_spec(w, 1)],
        outs, clip_specs(outs, first, clips), [pltpu.VMEM((rows, width), BF16)], after, bases,
    )


def time_backward_clip(dx2, x, gain, bias, w_ref, qkv_ref, p_ref, dqkv_ref, low_ref, a_ref, do_ref):
    frames = low_ref.shape[0] // AREA
    low_ref[...] = dx2.astype(BF16)
    do_ref[...] = dot_nt(low_ref[...], out_weight(w_ref)).astype(BF16)

    def part(j):
        return lambda f: qkv_ref[0, f * AREA : (f + 1) * AREA, j * 512 : (j + 1) * 512]

    queries, key_rows, values = part(0), part(1), part(2)

    def grads(t):
        return do_ref[t * AREA : (t + 1) * AREA, :]

    dp = time_scores(frames, grads, values, False)
    probs = [p_ref[0, f * AREA : (f + 1) * AREA, :] for f in range(frames)]
    inner = sum(p * d for p, d in zip(probs, dp))
    ds = [(p * (d - inner)).astype(BF16) for p, d in zip(probs, dp)]
    low = [p.astype(BF16) for p in probs]
    dk = [None] * frames
    dv = [None] * frames
    for t in range(frames):
        wide = dot(jnp.concatenate(ds[: t + 1] + low[: t + 1], axis=0), head_expand(t))
        q, do = queries(t).astype(F32), grads(t).astype(F32)
        dq = None
        for f in range(t + 1):
            ds_wide = wide[f * AREA : (f + 1) * AREA]
            p_wide = wide[(t + 1 + f) * AREA : (t + 2 + f) * AREA]
            term = ds_wide * key_rows(f).astype(F32)
            dq = term if dq is None else dq + term
            dk[f] = ds_wide * q if dk[f] is None else dk[f] + ds_wide * q
            dv[f] = p_wide * do if dv[f] is None else dv[f] + p_wide * do
        dqkv_ref[t * AREA : (t + 1) * AREA, 0:512] = (dq * 0.125).astype(BF16)
    for f in range(frames):
        dqkv_ref[f * AREA : (f + 1) * AREA, 512:1024] = (dk[f] * 0.125).astype(BF16)
        dqkv_ref[f * AREA : (f + 1) * AREA, 1024:1536] = dv[f].astype(BF16)
    da = dot_nt(dqkv_ref[...], jnp.concatenate([head_weight(w_ref, j) for j in range(3)], axis=1))
    unit, scale = normalize(x)
    a_ref[...] = (unit * gain + bias).astype(BF16)
    return dx2 + norm_backward(unit, scale, gain, da), row_sums(da * unit), row_sums(da)


def time_backward_kernel(
    place_ref, dx2_ref, x_ref, gain_ref, bias_ref, w_ref, qkv_ref, p_ref, o_ref, dx1_ref, dg_ref, db_ref, *refs
):
    *out_refs, do_ref, dqkv_all, low_all, a_all, o_all, turned_ref, block_ref = refs
    i, count = pl.program_id(0), dqkv_all.shape[0]

    @pl.when(i == 0)
    def _():
        dg_ref[...] = jnp.zeros_like(dg_ref)
        db_ref[...] = jnp.zeros_like(db_ref)

    @pl.when(i < count)
    def _():
        o_all[i] = o_ref[0]
        dx1, dg, db = time_backward_clip(
            dx2_ref[0], x_ref[0], gain_ref[...], bias_ref[...], w_ref, qkv_ref, p_ref,
            dqkv_all.at[i], low_all.at[i], a_all.at[i], do_ref,
        )
        dx1_ref[0] = dx1
        dg_ref[...] += dg
        db_ref[...] += db

    @pl.when(i == count)
    def _():
        attention_products(place_ref, a_all, dqkv_all, low_all, o_all, turned_ref, block_ref, out_refs)


def time_backward(place, dx2, x, gain, bias, w, qkv, p, o, after=()):
    clips, rows, width = x.shape
    sums = [shape((8, width), F32)] * 2 + [shape((4, 4, 64, 512))] * 2
    ins = (place, dx2, x, gain, bias, w, qkv, p, o)
    return run(
        time_backward_kernel, 26, (clips + 1,), ins,
        [SMEM] + clip_specs((dx2, x)) + whole_specs((gain, bias)) + [head_spec(w, 1)] + clip_specs((qkv, p, o)),
        [shape(x.shape, F32)] + sums, [per_clip(x.shape)] + whole_specs(sums),
        [pltpu.VMEM((rows, width), BF16)] + product_scratch(clips, rows, width), after,
    )


def gelu_parts(h):
    e = jnp.exp2(h * h * (-0.5 * math.log2(math.e)) + math.log2(1.0 / math.sqrt(2.0 * math.pi)))
    t = pl.reciprocal(1.0 + (0.3275911 * math.sqrt(0.5)) * jnp.abs(h), approx=True)
    tail = t * (COEFS[0] + t * (COEFS[1] + t * (COEFS[2] + t * (COEFS[3] + t * COEFS[4])))) * e
    cdf = jnp.where(h >= 0, 1.0 - tail, tail)
    return h * cdf, cdf + h * e


def mlp_clip(x, gain, bias, w_ref, c_ref, gb_ref, u_ref, dh_ref, slope_ref, y_ref, send_refs, grad_of):
    tiles = w_ref.shape[1]
    unit, scale = normalize(x)
    c_ref[...] = (unit * gain + bias).astype(BF16)
    for j in range(tiles):
        active, slope = gelu_parts(dot(c_ref[...], hidden_weight(w_ref, j, 0)))
        u_ref[j] = active.astype(BF16)
        slope_ref[j] = slope.astype(BF16)
    y = x + dot(
        jnp.concatenate([u_ref[j] for j in range(tiles)], axis=1),
        jnp.concatenate([hidden_weight(w_ref, j, 1) for j in range(tiles)], axis=0),
    )
    y_ref[...] = y.astype(BF16)
    write_sends(y_ref[...], send_refs)
    dy = grad_of(y)
    for j in range(tiles):
        du = dot_nt(gb_ref[...], hidden_weight(w_ref, j, 1))
        dh_ref[j] = (du * slope_ref[j].astype(F32)).astype(BF16)
    dc = dot_nt(
        jnp.concatenate([dh_ref[j] for j in range(tiles)], axis=1),
        jnp.concatenate([hidden_weight(w_ref, j, 0) for j in range(tiles)], axis=1),
    )
    return dy + norm_backward(unit, scale, gain, dc), row_sums(dc * unit), row_sums(dc)


def mlp_gen_kernel(parts, place_ref, aspect_ref, x_ref, gain_ref, bias_ref, w_ref, grad_ref, *rest):
    part_refs = rest[:parts]
    y_ref, dx_ref, c_ref, gb_ref, u_ref, dh_ref, dg_ref, db_ref, *send_refs, slope_ref = rest[parts:]
    i = pl.program_id(0)

    @pl.when(i == 0)
    def _():
        dg_ref[...] = jnp.zeros_like(dg_ref)
        db_ref[...] = jnp.zeros_like(db_ref)

    if parts:
        join_parts(window_source(aspect_ref[i], place_ref[0]), grad_ref, part_refs, gb_ref)
    else:
        gb_ref[...] = grad_ref[...]
    dx, dg, db = mlp_clip(
        x_ref[0], gain_ref[...], bias_ref[...], w_ref, c_ref.at[0], gb_ref.at[0], u_ref.at[:, 0], dh_ref.at[:, 0], slope_ref,
        y_ref.at[0], send_refs, lambda y: gb_ref[0].astype(F32),
    )
    dx_ref[0] = dx
    dg_ref[...] += dg
    db_ref[...] += db


def tile_block(dims, count):
    return pl.BlockSpec((dims[0], 1) + tuple(dims[2:]), lambda i: (0, jnp.minimum(i, count - 1), 0, 0))


def mlp_gen(direct, place, aspect, x, gain, bias, w, grad, parts=(), after=()):
    total, rows, width = x.shape
    clips, tiles, span = total // 2, w.shape[1], w.shape[3]
    both = [shape(x.shape), shape(x.shape, F32)]
    kept = [shape((clips, rows, width))] * 2
    hidden = [shape((tiles, clips, rows, span))] * 2
    sums = [shape((8, width), F32)] * 2
    sends = send_shapes(kept[0]) if direct else []
    return run(
        partial(mlp_gen_kernel, len(parts)), 20, (clips,), (place, aspect, x, gain, bias, w, grad, *parts),
        [SMEM] * 2 + clip_specs((x,), 0, clips) + whole_specs((gain, bias, w)) + clip_specs((grad, *parts)),
        both + kept + hidden + sums + sends,
        clip_specs(both, 0, clips) + clip_specs(kept) + [tile_block(h.shape, clips) for h in hidden] + whole_specs(sums) + clip_specs(sends),
        [pltpu.VMEM((tiles, rows, span), BF16)], after,
    )


def mlp_disc_kernel(
    sign_ref, count_ref, place_ref, x_ref, gain_ref, bias_ref, w_ref, logit_ref, c_gen, gb_gen, u_gen, dh_gen, dg_gen, db_gen,
    y_ref, dx_ref, out_ref, dg_ref, db_ref, *rest,
):
    send_refs, (slope_ref, c_all, gb_all, u_all, dh_all, turned_ref, block_ref) = rest[:-7], rest[-7:]
    i, (tiles, total, rows, span) = pl.program_id(0), u_all.shape
    count = total // 2

    @pl.when(i == 0)
    def _():
        dg_ref[...] = dg_gen[...]
        db_ref[...] = db_gen[...]

    @pl.when(i < count)
    def _():
        at = count + i
        c_all[i] = c_gen[0]
        gb_all[i] = gb_gen[0]
        u_all[:, i] = u_gen[:, 0]
        dh_all[:, i] = dh_gen[:, 0]

        def grad_of(y):
            sign = sign_ref[i]
            frame = lax.broadcasted_iota(jnp.int32, (rows, 1), 0) // AREA
            live = jnp.where(frame < count_ref[i], -sign, 0.0)
            dy = live * logit_ref[...] * jax.nn.sigmoid(1.0 - sign * logit_ref[...] * y)
            gb_all[at] = dy.astype(BF16)
            return dy

        dx, dg, db = mlp_clip(
            x_ref[0], gain_ref[...], bias_ref[...], w_ref, c_all.at[at], gb_all.at[at], u_all.at[:, at], dh_all.at[:, at],
            slope_ref, y_ref.at[0], send_refs, grad_of,
        )
        dx_ref[0] = dx
        dg_ref[...] += dg
        db_ref[...] += db

    @pl.when(i == count)
    def _():
        turned_ref[0] = c_all[...].reshape(-1, c_all.shape[2]).T
        turned_ref[1] = gb_all[...].reshape(-1, gb_all.shape[2]).T

    @pl.when(i >= count)
    def _():
        at = i - count
        for n, right in enumerate((dh_all, u_all)):
            block_ref[...] = dot(turned_ref[n], right[at].reshape(-1, span))
            for k in range(8):
                out_ref[k, 0, n * 64 : (n + 1) * 64, :] = block_ref[k * 64 : (k + 1) * 64, :].astype(BF16)


def mlp_disc(direct, sign, count, place, x, gain, bias, w, logit, kept, hidden, sums, bases, after=()):
    total, rows, width = x.shape
    clips, tiles, span = total // 2, w.shape[1], w.shape[3]
    outs = [shape(x.shape), shape(x.shape, F32)]
    blocks = shape((8, tiles, 128, span))
    sends = send_shapes(kept[0]) if direct else []
    ins = (sign, count, place, x, gain, bias, w, logit, *kept, *hidden, *sums)
    return run(
        mlp_disc_kernel, 30, (clips + tiles,), ins,
        [SMEM] * 3 + clip_specs((x,), clips, clips) + whole_specs((gain, bias, w, logit)) + clip_specs(kept)
        + [tile_block(h.shape, clips) for h in hidden] + whole_specs(sums),
        outs + [blocks] + [shape(v.shape, F32) for v in sums] + sends,
        clip_specs(outs, clips, clips) + [pl.BlockSpec((8, 1, 128, span), lambda i: (0, jnp.clip(i - clips, 0, tiles - 1), 0, 0))]
        + whole_specs(sums) + clip_specs(sends),
        [
            pltpu.VMEM((tiles, rows, span), BF16),
            pltpu.VMEM((total, rows, width), BF16),
            pltpu.VMEM((total, rows, width), BF16),
            pltpu.VMEM((tiles, total, rows, span), BF16),
            pltpu.VMEM((tiles, total, rows, span), BF16),
            pltpu.VMEM((2, width, total * rows), BF16),
            pltpu.VMEM((width, span), F32),
        ],
        after, bases,
    )


def window_maps(aspect, tokens_frame):
    grid_side = math.isqrt(tokens_frame)
    grid_width = jnp.where(
        aspect == 1, 2 * grid_side, jnp.where(aspect == 2, grid_side // 2, grid_side)
    ).astype(jnp.int32)[:, None]
    across = grid_width // WIN
    places = jnp.arange(tokens_frame, dtype=jnp.int32)[None, :]
    window = places // AREA
    inside = places % AREA
    grid_row = window // across * WIN + inside // WIN
    grid_col = window % across * WIN + inside % WIN
    forward_order = grid_row * grid_width + grid_col
    raster_row = places // grid_width
    raster_col = places % grid_width
    back_order = (
        (raster_row // WIN * across + raster_col // WIN) * AREA + raster_row % WIN * WIN + raster_col % WIN
    )
    return (forward_order, back_order)


def reorder(values, order):
    return jax.vmap(partial(jnp.take, axis=1))(values, order)


def pad_clips(values, split):
    return jnp.pad(values, [(0, -values.shape[0] % split)] + [(0, 0)] * (values.ndim - 1))


def gather_window(x, aspect, split):
    whole_x = pad_clips(lax.all_gather(x, "tensor", axis=2, tiled=True), split)
    aspect = pad_clips(aspect, split)
    t = lax.axis_index("tensor")
    clips = aspect.shape[0] // split
    mine = lax.dynamic_slice_in_dim(whole_x, t % split * clips, clips, 0)
    kinds = lax.dynamic_slice_in_dim(aspect, t % split * clips, clips, 0)
    order, _ = window_maps(kinds, whole_x.shape[2])
    return reorder(mine, lax.dynamic_slice_in_dim(order, t // split * AREA, AREA, 1))


def gather_raster(y, aspect, split, patches):
    every = lax.all_gather(y, "tensor", axis=0)
    count, clips, frames, _, width = every.shape
    every = every.reshape(count // split, split, clips, frames, AREA, width)
    every = jnp.transpose(every, (1, 2, 3, 0, 4, 5)).reshape(split * clips, frames, -1, width)
    _, back = window_maps(aspect, every.shape[2])
    t = lax.axis_index("tensor")
    return reorder(every[: aspect.shape[0]], lax.dynamic_slice_in_dim(back, t * patches, patches, 1))


def attention_piece(d, w_ref, wo_ref):
    rows = w_ref.shape[1] // 8
    part = wo_ref.shape[0] // 8
    qkv = [w_ref[m, pl.ds(pl.multiple_of(d * rows, rows), rows), :] for m in range(3)]
    out = wo_ref[pl.ds(pl.multiple_of(d * part, part), part), :]
    squares = [out[:, c * 128 : (c + 1) * 128] for c in range(out.shape[1] // 128)]
    return jnp.concatenate(qkv + [jnp.concatenate(squares, axis=0)], axis=1)


def pack_weights_kernel(place_ref, sw_ref, swo_ref, tw_ref, two_ref, w_in_ref, w_out_ref, heads_ref, hidden_ref):
    d = place_ref[1]
    heads_ref[0:64, :] = attention_piece(d, sw_ref, swo_ref)
    heads_ref[64:128, :] = attention_piece(d, tw_ref, two_ref)
    rows = pl.ds(pl.multiple_of(d * 64, 64), 64)
    hidden_ref[0:64, :] = w_in_ref[rows, :]
    hidden_ref[64:128, :] = w_out_ref[rows, :]


def pack_weights(place, *weights):
    outs = [shape((128, 512))] * 2
    return run(pack_weights_kernel, 0.01, (1,), (place, *weights), [SMEM] + whole_specs(weights), outs, whole_specs(outs))


def stack_kernel(place_ref, *refs):
    for j in range(4):
        refs[4][place_ref[0] ^ j] = refs[j][...]


def stack_pieces(place, pieces, after=()):
    outs = [shape((4,) + pieces[0].shape)]
    ins = (place, *pieces)
    return run(stack_kernel, 0.01, (1,), ins, [SMEM] + whole_specs(pieces), outs, whole_specs(outs), after=after)[0]


def gather_shard(shard):
    rows = shard.shape[0] // lax.axis_size("dp")
    piece = lax.dynamic_slice_in_dim(shard, lax.axis_index("dp") * rows, rows, 0)
    whole_w = lax.all_gather(piece, ("tensor", "dp"), axis=0, tiled=True)
    return whole_w.reshape((-1,) + shard.shape)


def gather_attention(w, wo):
    width = wo.shape[1]
    heads = gather_shard(w.reshape(-1, w.shape[2])).reshape((-1,) + w.shape)
    heads = jnp.moveaxis(heads, 0, 2).reshape(3, width, 4, -1).transpose(2, 1, 0, 3).reshape(4, width, -1)
    out = gather_shard(wo).reshape(4, width // 4, 4, width // 4).transpose(0, 2, 1, 3).reshape(4, width, -1)
    return jnp.concatenate([heads, out], axis=2)[None]


def gather_hidden(w_in, w_out):
    columns = jnp.moveaxis(gather_shard(w_in), 0, 1).reshape(w_in.shape[0], 4, -1)
    rows = gather_shard(w_out).reshape(4, -1, w_out.shape[1])
    return jnp.concatenate([jnp.moveaxis(columns, 1, 0), rows], axis=1)[None]


def add_kernel(count, *refs):
    operands, outs = refs[:count], refs[count:]
    for i, out in enumerate(outs):
        total = operands[0][i].astype(F32)
        for operand in operands[1:]:
            total = total + operand[i].astype(F32)
        out[...] = total.astype(out.dtype)


def add_blocks(operands, dtype=BF16, after=()):
    outs = [shape(operands[0].shape[1:], dtype)] * operands[0].shape[0]
    return run(
        partial(add_kernel, len(operands)), 0.01, (1,), operands, whole_specs(operands), outs, whole_specs(outs), after=after
    )


def reduce_core(even, odd, after=()):
    return add_blocks([even, swap(odd, "dp", 1)], after=after)


def chips_kernel(*refs):
    ins, out_refs = refs[:8], refs[8:]
    for j, out in enumerate(out_refs):
        at = 0
        for group in (ins[:4], ins[4:]):
            rows = group[0].shape[1]
            out[at : at + rows] = sum(ref[j].astype(F32) for ref in group).astype(BF16)
            at += rows


def chip_parts(near):
    return [near[0]] + [swap(near[i], "dp", 2 * i) for i in (1, 2, 3)]


def reduce_chips(ours, others, after=()):
    outs = [shape((ours[0].shape[1] + others[0].shape[1], ours[0].shape[2]))] * 4
    ins = (*ours, *others)
    return run(chips_kernel, 0.01, (1,), ins, whole_specs(ins), outs, whole_specs(outs), after=after)


def finish_kernel(place_ref, *refs):
    parts, (s_qkv, s_out, t_qkv, t_out, *norms) = refs[:4], refs[4:-1]
    sums_ref = refs[-1]
    total = sum(part[...].astype(F32) for part in parts)
    for block, qkv_ref, out_ref in ((total[0:64], s_qkv, s_out), (total[80:144], t_qkv, t_out)):
        for m in range(3):
            qkv_ref[m] = block[:, m * 128 : (m + 1) * 128]
        out_ref[...] = block[:, 384:512]
    sums_ref[...] = total[64:72]
    d = place_ref[1]
    pair = sums_ref[:, pl.ds(pl.multiple_of(d // 2 * 128, 128), 128)]
    mine = jnp.where(d % 2 == 0, pair[:, 0:64], pair[:, 64:128])
    for n, ref in enumerate(norms):
        ref[...] = mine[n : n + 1]


def finish(place, mine):
    ins = [place, mine[0]] + [swap(mine[j], "tensor", j) for j in (1, 2, 3)]
    outs = [shape((3, 64, 128), F32), shape((64, 128), F32)] * 2 + [shape((1, 64), F32)] * 6
    return run(
        finish_kernel, 0.01, (1,), ins, [SMEM] + whole_specs(ins[1:]), outs, whole_specs(outs), [pltpu.VMEM((8, 512), F32)]
    )


def scatter_grad(grads):
    flat = jnp.concatenate([g.astype(BF16).reshape(g.shape[0], -1) for g in grads], axis=1)
    flat = lax.psum_scatter(flat, "dp", scatter_dimension=0, tiled=True)
    pieces, offset = [], 0
    count = lax.axis_size("tensor")
    for g in grads:
        size = math.prod(g.shape[1:])
        piece = flat[:, offset : offset + size].reshape((flat.shape[0],) + g.shape[1:])
        pieces.append(jnp.moveaxis(piece, 2, 0).reshape(count, flat.shape[0], -1))
        offset += size
    mine = lax.psum_scatter(jnp.concatenate(pieces, axis=2), "tensor", scatter_dimension=0, tiled=True)[0]
    results, offset = [], 0
    for g in grads:
        size = g.shape[1] * g.shape[3]
        results.append(mine[:, offset : offset + size].reshape(-1, g.shape[1], g.shape[3]).astype(F32))
        offset += size
    return results


def in_order(even, odd):
    blocks = jnp.stack([even[:, :, :64], odd[:, :, :64]], axis=1).reshape(8, 4, 64, 4, 128)
    return jnp.transpose(blocks, (0, 2, 3, 1, 4)).reshape(512, 4, 512)


def shards(
    gen_tokens, rec_grad, adv_grad, gen_aspect, gen_frames, disc_tokens, disc_aspect, disc_frames, disc_labels,
    logit_gain, adv_weight, train_step, ln1_gain, ln1_bias, spatial_qkv, spatial_out, ln2_gain, ln2_bias,
    temporal_qkv, temporal_out, ln3_gain, ln3_bias, mlp_in, mlp_out,
):
    tensor = lax.axis_size("tensor")
    dp_at, tensor_at = lax.axis_index("dp"), lax.axis_index("tensor")
    local, frames, patches, width = gen_tokens.shape
    windows = patches * tensor // AREA
    direct = tensor == 4 and windows == 4 and lax.axis_size("dp") == 8
    split = max(tensor // windows, 1)
    clips = -(-local // split)
    place = jnp.stack([tensor_at, dp_at]).astype(jnp.int32)
    vectors = [v.reshape(1, -1) for v in (ln1_gain, ln1_bias, ln2_gain, ln2_bias, ln3_gain, ln3_bias, logit_gain)]
    g1, b1, g2, b2, g3, b3, logit = vectors

    step_value = train_step.astype(F32)
    ramp = adv_weight * step_value / (step_value + HALF)

    def mine(values):
        return lax.dynamic_slice_in_dim(pad_clips(values, split), tensor_at % split * clips, clips, 0)

    count = mine(disc_frames)
    sign = (2 * mine(disc_labels) - 1).astype(F32)
    aspects = (mine(gen_aspect), mine(disc_aspect))

    def flat(x):
        return x.reshape(x.shape[0], -1, width)

    if direct:
        x_gen, x_disc, rec, adv = (flat(v) for v in (gen_tokens, disc_tokens, rec_grad, adv_grad))
        heads, hidden = pack_weights(place, spatial_qkv, spatial_out, temporal_qkv, temporal_out, mlp_in, mlp_out)
        gen_parts = pack(place, gen_aspect, x_gen, (heads,))
        disc_parts = pack(place, disc_aspect, x_disc, gen_parts)
        dy, *dy_parts = pack_grad(place, gen_aspect, gen_frames, ramp, rec, adv, disc_parts)
        heads = [heads] + [swap(heads, "tensor", j) for j in (1, 2, 3)]
        heads = stack_pieces(place, heads, (dy,))
        space_w = time_w = lax.all_gather(heads, "dp", axis=0)
        gen_parts = exchange(gen_parts)
        hidden = [hidden] + [swap(hidden, "tensor", j) for j in (1, 2, 3)]
        hidden = stack_pieces(place, hidden, (heads, *gen_parts))
        mlp_w = lax.all_gather(hidden, "dp", axis=0)
        disc_parts, dy_parts = exchange(disc_parts), exchange(dy_parts)
    else:
        place = jnp.zeros_like(place)
        space_w, time_w = gather_attention(spatial_qkv, spatial_out), gather_attention(temporal_qkv, temporal_out)
        mlp_w = gather_hidden(mlp_in, mlp_out)
        x_gen = flat(gather_window(gen_tokens, gen_aspect, split))
        x_disc = flat(gather_window(disc_tokens, disc_aspect, split))
        live = jnp.arange(frames, dtype=jnp.int32)[None, :] < gen_frames[:, None]
        total = rec_grad.astype(F32) + ramp[0] * adv_grad.astype(F32)
        dy = jnp.where(live[:, :, None, None], total, 0.0).astype(BF16)
        dy = flat(gather_window(dy, gen_aspect, split))
        gen_parts, disc_parts, dy_parts = (), (), ()

    sf = space_forward(place, aspects[0], x_gen, gen_parts, g1, b1, space_w, 2 * clips, (), (hidden,) if direct else ())
    tf = time_forward(sf[0], g2, b2, time_w, clips)
    sf = space_forward(place, aspects[1], x_disc, disc_parts, g1, b1, space_w, 2 * clips, sf, tf[:1])
    x1, s_qkv, s_p, s_o, xw = sf
    x2, t_qkv, t_p, t_o = time_forward(x1, g2, b2, time_w, clips, tf)
    gen = mlp_gen(direct, place, aspects[0], x2, g3, b3, mlp_w, dy, dy_parts)
    y_gen = exchange(gen[8:]) if direct else ()
    y, dx2, ff_blocks, ff_dg, ff_db, *y_sends = mlp_disc(
        direct, sign, count, place, x2, g3, b3, mlp_w, logit, gen[2:4], gen[4:6], gen[6:8], gen[:2]
    )
    y_disc = exchange(y_sends) if direct else ()
    if direct:
        ff_mine = lax.psum_scatter(ff_blocks, "dp", scatter_dimension=0)
    dx1, t_dg, t_db, t_even, t_odd = time_backward(place, dx2, x1, g2, b2, time_w, t_qkv, t_p, t_o, y_gen)
    back = space_backward(direct, dx1, xw, g1, b1, space_w, s_qkv, s_p, (), y_disc)
    kept, (dx0_gen, s_dg, s_db, *gen_sends) = back[:3], back[3:]
    if direct:
        t_near = reduce_core(t_even, t_odd, (dx0_gen,))
        gen_parts = exchange(gen_sends)
        t_parts = chip_parts(t_near)
    back = space_backward(
        direct, dx1, xw, g1, b1, space_w, s_qkv, s_p, kept, (t_near[0],) if direct else ()
    )
    kept, (dx0_disc, d_dg, d_db, *disc_sends) = back[:3], back[3:]
    disc_parts = exchange(disc_sends) if direct else ()
    dqkv, low, a = kept
    zero = jnp.zeros_like(t_dg)
    s_even, s_odd = space_grad(
        place, a, dqkv, low, s_o, (s_dg, d_dg, s_db, d_db, t_dg, zero, t_db, zero, ff_dg, zero, ff_db, zero),
        (dx0_disc, *t_parts) if direct else (),
    )

    part = width // tensor
    if direct:
        ff_share = lax.psum_scatter(ff_mine, "tensor", scatter_dimension=0).astype(F32)
        y_gen = join_raster(place, gen_aspect, y, (y_gen,), 0, 6, (s_even,))
        near = reduce_core(s_even, s_odd, (*gen_parts, *y_gen, *disc_parts[:2]))
        dx_gen = join_raster(place, gen_aspect, dx0_gen, (gen_parts,), 0, JOIN, near[:1])
        y_disc = join_raster(place, disc_aspect, y, (y_disc,), clips, JOIN, near[:1])
        ours = reduce_chips(chip_parts(near), t_parts, (*dx_gen, *y_disc, ff_share))
        dx_disc = join_raster(place, disc_aspect, dx0_disc, (disc_parts,), 0, JOIN, ours[:1])
        s_qkv, s_out, t_qkv, t_out, *small = finish(place, ours)
        shares = (s_qkv, s_out.T, t_qkv, t_out.T)
        small = [n[0] for n in small]
        in_share, out_share = ff_share[:64], ff_share[64:]
        y_gen, y_disc, dx_gen, dx_disc = (v.reshape(gen_tokens.shape) for v in (*y_gen, *y_disc, *dx_gen, *dx_disc))
    else:
        y_gen, y_disc, dx_gen, dx_disc = (
            gather_raster(v.reshape(clips, frames, AREA, width), aspect, split, patches)
            for v, aspect in ((y[:clips], gen_aspect), (y[clips:], disc_aspect), (dx0_gen, gen_aspect), (dx0_disc, disc_aspect))
        )
        ff = jnp.transpose(ff_blocks.reshape(8, 4, 2, 64, 512), (0, 3, 2, 1, 4)).reshape(width, 2, tensor, -1)
        ff_share = scatter_grad([ff])[0]
        in_share, out_share = ff_share[:, 0], ff_share[:, 1]
        shares = []
        for even, odd in ((s_even, s_odd), (t_even, t_odd)):
            block = scatter_grad([in_order(even, odd).reshape(width, 4, tensor, part)])[0]
            shares += [jnp.moveaxis(block[:, :3], 1, 0), block[:, 3].T]
        small = lax.psum(s_even[0, 0, 64:70].astype(F32), ("dp", "tensor"))
        piece = width // lax.axis_size("dp")
        small = lax.dynamic_slice_in_dim(small, dp_at * piece, piece, 1)

    return (
        y_gen, dx_gen, y_disc, dx_disc,
        small[0], small[1], shares[0], shares[1], small[2], small[3], shares[2], shares[3],
        small[4], small[5], in_share, out_share.T,
    )


def solution(mesh):
    tokens = P("dp", None, "tensor", None)
    vector, clip = P(), P("dp")
    qkv, rows, cols = P(None, None, "tensor"), P("tensor", None), P(None, "tensor")
    in_specs = (
        (tokens,) * 3 + (clip,) * 2 + (tokens,) + (clip,) * 3 + (vector,) * 5
        + (qkv, rows, vector, vector, qkv, rows, vector, vector, cols, rows)
    )
    block = (clip, clip, P(None, "dp", "tensor"), P("tensor", "dp"))
    out_specs = (tokens,) * 4 + block * 2 + (clip, clip, P("dp", "tensor"), P("tensor", "dp"))
    return jax.shard_map(shards, mesh=mesh, in_specs=in_specs, out_specs=out_specs, check_vma=False)
```

```python
from functools import partial
import math

import jax
import jax.numpy as jnp
from jax import lax
from jax.experimental import pallas as pl
from jax.experimental.pallas import tpu as pltpu
from jax.sharding import PartitionSpec as P

HEAD_DIM = 64
WIN = 8
AREA = WIN * WIN
HALF = 5000
EPS = 1e-05
F32 = jnp.float32
BF16 = jnp.bfloat16
VMEM_LIMIT = 58 * 1024 * 1024
JOIN = 0.01
COEFS = tuple(math.sqrt(math.pi / 2.0) * a for a in (0.254829592, -0.284496736, 1.421413741, -1.453152027, 1.061405429))

NT = (((1,), (1,)), ((), ()))
TN = (((0,), (0,)), ((), ()))


def dot(lhs, rhs):
    return jnp.dot(lhs, rhs, preferred_element_type=F32)


def dot_nt(lhs, rhs):
    return lax.dot_general(lhs, rhs, NT, preferred_element_type=F32)


def dot_tn(lhs, rhs):
    return lax.dot_general(lhs, rhs, TN, preferred_element_type=F32)


def normalize(value):
    average = jnp.mean(value, axis=-1, keepdims=True)
    centred = value - average
    variance = jnp.mean(centred * centred, axis=-1, keepdims=True)
    scale = lax.rsqrt(variance + EPS)
    return centred * scale, scale


def norm_backward(unit, scale, gain, grad):
    scaled = grad * gain
    inner = scaled - jnp.mean(scaled, axis=-1, keepdims=True)
    return scale * (inner - unit * jnp.mean(scaled * unit, axis=-1, keepdims=True))


def row_sums(values):
    return jnp.sum(values.reshape(-1, 8, values.shape[-1]), axis=0)


HBM = pl.BlockSpec(memory_space=pltpu.HBM)
SMEM = pl.BlockSpec(memory_space=pltpu.SMEM)


def run(kernel, microseconds, grid, ins, in_specs, outs, out_specs, scratch=(), after=(), bases=()):
    ins, after, bases = tuple(ins), tuple(after), tuple(bases)
    count, extra = len(ins), len(after) + len(bases)

    def body(*refs):
        kernel(*refs[:count], *refs[count + extra :])

    return pl.pallas_call(
        body,
        grid=grid,
        in_specs=list(in_specs) + [HBM] * extra,
        out_specs=list(out_specs),
        out_shape=list(outs),
        scratch_shapes=list(scratch),
        input_output_aliases={count + len(after) + i: i for i in range(len(bases))},
        cost_estimate=pl.CostEstimate(flops=int(microseconds * 2.5e9), bytes_accessed=0, transcendentals=0),
        compiler_params=pltpu.CompilerParams(
            dimension_semantics=("arbitrary",) * len(grid), vmem_limit_bytes=VMEM_LIMIT
        ),
    )(*ins, *after, *bases)


def shape(dims, dtype=BF16):
    return jax.ShapeDtypeStruct(tuple(dims), dtype)


def whole(dims):
    zeros = (0,) * len(dims)
    return pl.BlockSpec(tuple(dims), lambda i: zeros)


def per_clip(dims, first=0, count=None):
    zeros = (0,) * (len(dims) - 1)
    count = count or dims[0]
    return pl.BlockSpec((1,) + tuple(dims[1:]), lambda i: (first + jnp.clip(i, 0, count - 1),) + zeros)


def join_rows(w_ref, part):
    return jnp.concatenate(
        [
            jnp.concatenate([part(w_ref, i, j) for j in range(w_ref.shape[1])], axis=1)
            for i in range(w_ref.shape[0])
        ],
        axis=0,
    )


def head_weight(w_ref, m):
    return join_rows(w_ref, lambda ref, i, j: ref[i, j, :, m * 128 : (m + 1) * 128])


def out_weight(w_ref):
    part = w_ref.shape[2] // 4
    return jnp.concatenate(
        [
            jnp.concatenate([w_ref[i, j, c * part : (c + 1) * part, 384:512] for c in range(4)], axis=1)
            for j in range(w_ref.shape[1])
            for i in range(w_ref.shape[0])
        ],
        axis=0,
    )


def hidden_weight(w_ref, j, n):
    part = w_ref.shape[2] // 2
    return jnp.concatenate([w_ref[i, j, n * part : (n + 1) * part, :] for i in range(w_ref.shape[0])], axis=0)


def head_mask(dtype):
    rows = lax.broadcasted_iota(jnp.int32, (256, 256), 0) // HEAD_DIM
    cols = lax.broadcasted_iota(jnp.int32, (256, 256), 1) // HEAD_DIM
    return jnp.where(rows == cols, 1.0, 0.0).astype(dtype)


def spread(values, mask):
    return jnp.concatenate([values] * 4, axis=0) * mask


def pair_product(scores, values, low_lane):
    parts = []
    for c in range(2):
        full = dot_tn(scores[:, c * 128 : (c + 1) * 128], values[:, c * 128 : (c + 1) * 128])
        parts.append(jnp.where(low_lane, full[:64], full[64:]))
    return jnp.concatenate(parts, axis=1)


def one_hot(source, count):
    rows = source.shape[0]
    inside = lax.broadcasted_iota(jnp.int32, (rows, count), 0) % 8
    cols = lax.broadcasted_iota(jnp.int32, (rows, count), 1)
    return jnp.where((source >= 0) & (cols == source * 8 + inside), 1.0, 0.0).astype(BF16)


def chunk_ids():
    return lax.broadcasted_iota(jnp.int32, (AREA, 1), 0) // 8


def send_source(aspect, t):
    c = chunk_ids()
    square = jnp.where(c < 4, 2 * c + 1 - t % 2, -1)
    wide = jnp.where(
        c < 2, 4 * c + (t ^ 1), jnp.where(c < 4, -1, jnp.where(c < 6, 4 * (c - 4) + (t ^ 2), 4 * (c - 6) + (t ^ 3)))
    )
    return jnp.where(aspect == 0, square, jnp.where(aspect == 1, wide, -1))


def window_source(aspect, t):
    c = chunk_ids()
    square = jnp.where(c < 4, 2 * c + t % 2, c + 4)
    wide = jnp.where(c < 2, 4 * c + t, jnp.where(c < 4, c + 10, jnp.where(c < 6, c + 4, c + 8)))
    return jnp.where(aspect == 0, square, jnp.where(aspect == 1, wide, c))


def raster_source(aspect, t):
    c = chunk_ids()
    square = c // 2 + jnp.where(c % 2 == t % 2, 0, 8)
    way = (c % 4) ^ t
    wide = c // 4 + jnp.where(way == 0, 0, jnp.where(way == 1, 8, jnp.where(way == 2, 12, 14)))
    return jnp.where(aspect == 0, square, jnp.where(aspect == 1, wide, c))


def write_sends(values, refs):
    if not refs:
        return
    for f in range(values.shape[0] // AREA):
        base = f * AREA
        refs[0][0, f * 32 : (f + 1) * 32, :] = values[base + 32 : base + 64]
        refs[1][0, f * 16 : (f + 1) * 16, :] = values[base + 16 : base + 32]
        refs[2][0, f * 16 : (f + 1) * 16, :] = values[base + 48 : base + 64]


def pack_rows(values, select, refs):
    for f in range(values.shape[0] // AREA):
        moved = dot(select, values[f * AREA : (f + 1) * AREA]).astype(BF16)
        refs[0][0, f * 32 : (f + 1) * 32, :] = moved[:32]
        refs[1][0, f * 16 : (f + 1) * 16, :] = moved[32:48]
        refs[2][0, f * 16 : (f + 1) * 16, :] = moved[48:]


def join_parts(source, own_ref, part_refs, out_ref):
    select = one_hot(source, 2 * AREA)
    for f in range(out_ref.shape[1] // AREA):
        rows = [own_ref[0, f * AREA : (f + 1) * AREA, :]]
        rows += [ref[0, f * size : (f + 1) * size, :] for ref, size in zip(part_refs, (32, 16, 16))]
        out_ref[0, f * AREA : (f + 1) * AREA, :] = dot(select, jnp.concatenate(rows, axis=0)).astype(BF16)


def pack_kernel(place_ref, aspect_ref, x_ref, *send_refs):
    select = one_hot(send_source(aspect_ref[pl.program_id(0)], place_ref[0]), AREA)
    pack_rows(x_ref[0], select, send_refs)


def pack_grad_kernel(place_ref, aspect_ref, count_ref, ramp_ref, rec_ref, adv_ref, dy_ref, *send_refs):
    clip = pl.program_id(0)
    frame = lax.broadcasted_iota(jnp.int32, (rec_ref.shape[1], 1), 0) // AREA
    total = rec_ref[0].astype(F32) + ramp_ref[0] * adv_ref[0].astype(F32)
    dy_ref[0] = jnp.where(frame < count_ref[clip], total, 0.0).astype(BF16)
    select = one_hot(send_source(aspect_ref[clip], place_ref[0]), AREA)
    pack_rows(dy_ref[0], select, send_refs)


def join_kernel(place_ref, aspect_ref, own_ref, r1_ref, r2_ref, r3_ref, out_ref):
    source = raster_source(aspect_ref[pl.program_id(0)], place_ref[0])
    join_parts(source, own_ref, (r1_ref, r2_ref, r3_ref), out_ref)


def send_shapes(x):
    clips, rows, width = x.shape
    return [shape((clips, rows // part, width)) for part in (2, 4, 4)]


def head_spec(w, n):
    if w.shape[2] != 128:
        return whole(w.shape)
    return pl.BlockSpec(w.shape[:2] + (64, w.shape[3]), lambda i: (0, 0, n, 0))


def clip_specs(arrays, first=0, count=None):
    return [per_clip(a.shape, first, count) for a in arrays]


def whole_specs(arrays):
    return [whole(a.shape) for a in arrays]


def pack(place, aspect, x, after=()):
    outs = send_shapes(x)
    return run(
        pack_kernel, 0.01, x.shape[:1], (place, aspect, x), [SMEM, SMEM, per_clip(x.shape)], outs, clip_specs(outs), after=after
    )


def pack_grad(place, aspect, count, ramp, rec, adv, after=()):
    outs = [shape(rec.shape)] + send_shapes(rec)
    ins = (place, aspect, count, ramp, rec, adv)
    return run(
        pack_grad_kernel, 4, rec.shape[:1], ins, [SMEM] * 4 + clip_specs((rec, adv)), outs, clip_specs(outs), after=after
    )


def join_raster(place, aspect, own, parts, first, microseconds, after=()):
    clips = parts[0][0].shape[0]
    outs = [shape((clips,) + own.shape[1:])]
    ins = (place, aspect, own, *parts[0])
    in_specs = [SMEM] * 2 + clip_specs((own,), first, clips) + clip_specs(parts[0])
    return run(join_kernel, microseconds, (clips,), ins, in_specs, outs, clip_specs(outs), after=after)


def exchange(parts):
    return tuple(swap(part, "tensor", way) for way, part in zip((1, 2, 3), parts))


def swap(x, axis, way):
    return lax.ppermute(x, axis, [(i, i ^ way) for i in range(lax.axis_size(axis))])


def place_products(place_ref, block_ref, out_refs, cols):
    for k in range(8):
        rows = pl.ds(pl.multiple_of((place_ref[1] ^ k) * 64, 64), 64)
        for j in range(4):
            lanes = pl.ds(pl.multiple_of((place_ref[0] ^ j) * 128, 128), 128)
            out_refs[k % 2][k // 2, j, 0:64, cols] = block_ref[rows, lanes].astype(BF16)


def attention_products(place_ref, a_ref, dqkv_ref, low_ref, o_ref, turned_ref, block_ref, out_refs):
    def flat(ref, cols=slice(None)):
        values = ref[:, :, cols]
        return values.reshape(-1, values.shape[-1])

    turned_ref[...] = flat(a_ref).T
    for m in range(3):
        block_ref[...] = dot(turned_ref[...], flat(dqkv_ref, slice(m * 512, (m + 1) * 512)))
        place_products(place_ref, block_ref, out_refs, slice(m * 128, (m + 1) * 128))
    turned_ref[...] = flat(low_ref).T
    block_ref[...] = dot(turned_ref[...], flat(o_ref))
    place_products(place_ref, block_ref, out_refs, slice(384, 512))


def product_scratch(clips, rows, width):
    return [
        pltpu.VMEM((clips, rows, 3 * width), BF16),
        *[pltpu.VMEM((clips, rows, width), BF16)] * 3,
        pltpu.VMEM((width, clips * rows), BF16),
        pltpu.VMEM((width, width), F32),
    ]


def window_blocks(rows):
    return [(w, g) for w in range(rows // AREA) for g in range(2)]


def low_lanes():
    return lax.broadcasted_iota(jnp.int32, (64, 128), 1) < HEAD_DIM


def space_forward_kernel(parts, place_ref, aspect_ref, x_ref, *refs):
    part_refs = refs[:parts]
    gain_ref, bias_ref, w_ref, x1_ref, qkv_ref, p_ref, o_ref, xw_ref, a_ref = refs[parts:]
    rows = x_ref.shape[1]
    if parts:
        join_parts(window_source(aspect_ref[pl.program_id(0)], place_ref[0]), x_ref, part_refs, xw_ref)
    else:
        xw_ref[...] = x_ref[...]
    x = xw_ref[0].astype(F32)
    unit, _ = normalize(x)
    a_ref[...] = (unit * gain_ref[...] + bias_ref[...]).astype(BF16)
    for j in range(3):
        qkv_ref[0, :, j * 512 : (j + 1) * 512] = dot(a_ref[...], head_weight(w_ref, j)).astype(BF16)
    mask, low_lane = head_mask(BF16), low_lanes()

    def part(j, w, g):
        return qkv_ref[0, w * AREA : (w + 1) * AREA, j * 512 + g * 256 : j * 512 + (g + 1) * 256]

    blocks = window_blocks(rows)
    scores = [dot_nt(part(1, w, g), spread(part(0, w, g), mask)) * 0.125 for w, g in blocks]
    for s, (w, g) in zip(scores, blocks):
        e = jnp.exp(s - jnp.max(s, axis=0, keepdims=True))
        p_ref[0, 2 * w + g] = (e * (1.0 / jnp.sum(e, axis=0, keepdims=True))).astype(BF16)
    for w, g in blocks:
        attended = pair_product(p_ref[0, 2 * w + g], part(2, w, g), low_lane)
        o_ref[0, w * AREA : (w + 1) * AREA, g * 256 : (g + 1) * 256] = attended.astype(BF16)
    x1_ref[0] = x + dot(o_ref[0], out_weight(w_ref))


def space_forward(place, aspect, x, parts, gain, bias, w, total, bases=(), after=()):
    clips, rows, width = x.shape
    first = total - clips if bases else 0
    outs = [
        shape((total, rows, width), F32),
        shape((total, rows, 3 * width)),
        shape((total, 2 * rows // AREA, AREA, 256)),
        shape((total, rows, width)),
        shape((total, rows, width)),
    ]
    return run(
        partial(space_forward_kernel, len(parts)), 10, (clips,), (place, aspect, x, *parts, gain, bias, w),
        [SMEM] * 2 + clip_specs((x, *parts)) + whole_specs((gain, bias)) + [head_spec(w, 0)], outs, clip_specs(outs, first, clips),
        [pltpu.VMEM((rows, width), BF16)], after, bases,
    )


def space_backward_clip(dx1, x, gain, bias, w_ref, qkv_ref, p_ref, dqkv_ref, low_ref, a_ref, do_ref):
    low_ref[...] = dx1.astype(BF16)
    do_ref[...] = dot_nt(low_ref[...], out_weight(w_ref)).astype(BF16)
    mask, low_lane = head_mask(BF16), low_lanes()

    def part(j, w, g):
        return qkv_ref[0, w * AREA : (w + 1) * AREA, j * 512 + g * 256 : j * 512 + (g + 1) * 256]

    def grad(w, g):
        return spread(do_ref[w * AREA : (w + 1) * AREA, g * 256 : (g + 1) * 256], mask)

    def put(j, w, g, values):
        dqkv_ref[w * AREA : (w + 1) * AREA, j * 512 + g * 256 : j * 512 + (g + 1) * 256] = values.astype(BF16)

    blocks = window_blocks(low_ref.shape[0])
    grad_probs = [dot_nt(part(2, w, g), grad(w, g)) for w, g in blocks]
    for w, g in blocks:
        put(2, w, g, dot(p_ref[0, 2 * w + g], grad(w, g)))
    grad_scores = []
    for dp, (w, g) in zip(grad_probs, blocks):
        p = p_ref[0, 2 * w + g].astype(F32)
        weighted = p * dp
        grad_scores.append((weighted - p * jnp.sum(weighted, axis=0, keepdims=True)).astype(BF16))
    for ds, (w, g) in zip(grad_scores, blocks):
        put(1, w, g, dot(ds, spread(part(0, w, g), mask)) * 0.125)
    for ds, (w, g) in zip(grad_scores, blocks):
        put(0, w, g, pair_product(ds, part(1, w, g), low_lane) * 0.125)
    da = dot_nt(dqkv_ref[...], jnp.concatenate([head_weight(w_ref, j) for j in range(3)], axis=1))
    unit, scale = normalize(x)
    a_ref[...] = (unit * gain + bias).astype(BF16)
    return dx1 + norm_backward(unit, scale, gain, da), row_sums(da * unit), row_sums(da)


def space_backward_kernel(
    dx1_ref, x_ref, gain_ref, bias_ref, w_ref, qkv_ref, p_ref, dqkv_ref, low_ref, a_ref, dx0_ref, dg_ref, db_ref, *rest
):
    *send_refs, do_ref = rest

    @pl.when(pl.program_id(0) == 0)
    def _():
        dg_ref[...] = jnp.zeros_like(dg_ref)
        db_ref[...] = jnp.zeros_like(db_ref)

    dx0, dg, db = space_backward_clip(
        dx1_ref[0], x_ref[0].astype(F32), gain_ref[...], bias_ref[...], w_ref, qkv_ref, p_ref,
        dqkv_ref.at[0], low_ref.at[0], a_ref.at[0], do_ref,
    )
    dx0_ref[0] = dx0.astype(BF16)
    write_sends(dx0_ref[0], send_refs)
    dg_ref[...] += dg
    db_ref[...] += db


def space_backward(direct, dx1, x, gain, bias, w, qkv, p, bases=(), after=()):
    total, rows, width = x.shape
    clips = total // 2
    first = clips if bases else 0
    kept = [shape((total, rows, 3 * width))] + [shape(x.shape)] * 2
    outs = [shape((clips, rows, width))]
    sums = [shape((8, width), F32)] * 2
    sends = send_shapes(outs[0]) if direct else []
    return run(
        space_backward_kernel, 10, (clips,), (dx1, x, gain, bias, w, qkv, p),
        clip_specs((dx1, x), first, clips) + whole_specs((gain, bias)) + [head_spec(w, 0)] + clip_specs((qkv, p), first, clips),
        kept + outs + sums + sends, clip_specs(kept, first, clips) + clip_specs(outs) + whole_specs(sums) + clip_specs(sends),
        [pltpu.VMEM((rows, width), BF16)], after, bases,
    )


def space_grad_kernel(place_ref, a_ref, dqkv_ref, low_ref, o_ref, *refs):
    norm_refs, (even_ref, odd_ref, turned_ref, block_ref) = refs[:-4], refs[-4:]
    i = pl.program_id(0)

    def place_block(m):
        place_products(place_ref, block_ref, (even_ref, odd_ref), slice(m * 128, (m + 1) * 128))

    @pl.when(i == 0)
    def _():
        turned_ref[...] = a_ref[...].T
        sums = [
            jnp.sum(left[...] + right[...], axis=0, keepdims=True) for left, right in zip(norm_refs[::2], norm_refs[1::2])
        ]
        sums = jnp.concatenate(sums + [jnp.zeros((16 - len(sums), 512), F32)], axis=0).astype(BF16)
        for ref in (even_ref, odd_ref):
            for k in range(4):
                for j in range(4):
                    ref[k, j, 64:80, :] = sums

    for m in range(3):

        @pl.when(i == m)
        def _():
            block_ref[...] = dot(turned_ref[...], dqkv_ref[...])
            place_block(m)

    @pl.when(i == 3)
    def _():
        turned_ref[...] = low_ref[...].T
        block_ref[...] = dot(turned_ref[...], o_ref[...])
        place_block(3)


def space_grad(place, a, dqkv, low, o, norms, after=()):
    a, dqkv, low, o = (v.reshape(-1, v.shape[-1]) for v in (a, dqkv, low, o))
    rows, width = a.shape
    outs = [shape((4, 4, 80, 512))] * 2
    column = pl.BlockSpec((rows, width), lambda i: (0, jnp.minimum(i, 2)))
    return run(
        space_grad_kernel, 6, (4,), (place, a, dqkv, low, o, *norms),
        [SMEM, whole(a.shape), column] + whole_specs((low, o, *norms)), outs, whole_specs(outs),
        [pltpu.VMEM((width, rows), BF16), pltpu.VMEM((width, width), F32)], after,
    )


def head_select(frame):
    rows = lax.broadcasted_iota(jnp.int32, (512, 128), 0) // HEAD_DIM
    cols = lax.broadcasted_iota(jnp.int32, (512, 128), 1) - 8 * frame
    return jnp.where(rows == cols, 1.0, 0.0).astype(BF16)


def head_expand(frame):
    rows = lax.broadcasted_iota(jnp.int32, (128, 512), 0) - 8 * frame
    cols = lax.broadcasted_iota(jnp.int32, (128, 512), 1) // HEAD_DIM
    return jnp.where(rows == cols, 1.0, 0.0).astype(BF16)


def head_sums(products, selector, exact):
    high = products.astype(BF16)
    if not exact:
        return dot(high, selector)
    rest = (products - high.astype(F32)).astype(BF16)
    return dot(high, selector) + dot(rest, selector)


def time_scores(frames, left, right, exact=True):
    totals = [None] * frames
    for t in range(frames):
        lhs = left(t).astype(F32)
        stacked = jnp.concatenate([lhs * right(f).astype(F32) for f in range(t + 1)], axis=0)
        sums = head_sums(stacked, head_select(t), exact)
        for f in range(t + 1):
            part = sums[f * AREA : (f + 1) * AREA]
            totals[f] = part if totals[f] is None else totals[f] + part
    return totals


def time_forward_kernel(x_ref, gain_ref, bias_ref, w_ref, x2_ref, qkv_ref, p_ref, o_ref, a_ref):
    frames = x_ref.shape[1] // AREA
    x = x_ref[0]
    unit, _ = normalize(x)
    a_ref[...] = (unit * gain_ref[...] + bias_ref[...]).astype(BF16)
    for j in range(3):
        qkv_ref[0, :, j * 512 : (j + 1) * 512] = dot(a_ref[...], head_weight(w_ref, j)).astype(BF16)

    def part(j):
        return lambda f: qkv_ref[0, f * AREA : (f + 1) * AREA, j * 512 : (j + 1) * 512]

    scores = time_scores(frames, part(0), part(1))
    lane = lax.broadcasted_iota(jnp.int32, (AREA, 128), 1)
    scores = [jnp.where(lane >= 8 * f, s * 0.125, -1e30) for f, s in enumerate(scores)]
    top = scores[0]
    for s in scores[1:]:
        top = jnp.maximum(top, s)
    exps = [jnp.exp(s - top) for s in scores]
    inverse = 1.0 / sum(exps)
    probs = [e * inverse for e in exps]
    for f in range(frames):
        p_ref[0, f * AREA : (f + 1) * AREA, :] = probs[f]
    low = [p.astype(BF16) for p in probs]
    values = part(2)
    for t in range(frames):
        wide = dot(jnp.concatenate(low[: t + 1], axis=0), head_expand(t))
        total = None
        for f in range(t + 1):
            term = wide[f * AREA : (f + 1) * AREA] * values(f).astype(F32)
            total = term if total is None else total + term
        o_ref[0, t * AREA : (t + 1) * AREA, :] = total.astype(BF16)
    x2_ref[0] = x + dot(o_ref[0], out_weight(w_ref))


def time_forward(x, gain, bias, w, clips, bases=(), after=()):
    total, rows, width = x.shape
    first = total - clips if bases else 0
    outs = [
        shape((total, rows, width), F32),
        shape((total, rows, 3 * width)),
        shape((total, rows, 128), F32),
        shape((total, rows, width)),
    ]
    return run(
        time_forward_kernel, 10, (clips,), (x, gain, bias, w),
        clip_specs((x,), first, clips) + whole_specs((gain, bias)) + [head_spec(w, 1)],
        outs, clip_specs(outs, first, clips), [pltpu.VMEM((rows, width), BF16)], after, bases,
    )


def time_backward_clip(dx2, x, gain, bias, w_ref, qkv_ref, p_ref, dqkv_ref, low_ref, a_ref, do_ref):
    frames = low_ref.shape[0] // AREA
    low_ref[...] = dx2.astype(BF16)
    do_ref[...] = dot_nt(low_ref[...], out_weight(w_ref)).astype(BF16)

    def part(j):
        return lambda f: qkv_ref[0, f * AREA : (f + 1) * AREA, j * 512 : (j + 1) * 512]

    queries, key_rows, values = part(0), part(1), part(2)

    def grads(t):
        return do_ref[t * AREA : (t + 1) * AREA, :]

    dp = time_scores(frames, grads, values, False)
    probs = [p_ref[0, f * AREA : (f + 1) * AREA, :] for f in range(frames)]
    inner = sum(p * d for p, d in zip(probs, dp))
    ds = [(p * (d - inner)).astype(BF16) for p, d in zip(probs, dp)]
    low = [p.astype(BF16) for p in probs]
    dk = [None] * frames
    dv = [None] * frames
    for t in range(frames):
        wide = dot(jnp.concatenate(ds[: t + 1] + low[: t + 1], axis=0), head_expand(t))
        q, do = queries(t).astype(F32), grads(t).astype(F32)
        dq = None
        for f in range(t + 1):
            ds_wide = wide[f * AREA : (f + 1) * AREA]
            p_wide = wide[(t + 1 + f) * AREA : (t + 2 + f) * AREA]
            term = ds_wide * key_rows(f).astype(F32)
            dq = term if dq is None else dq + term
            dk[f] = ds_wide * q if dk[f] is None else dk[f] + ds_wide * q
            dv[f] = p_wide * do if dv[f] is None else dv[f] + p_wide * do
        dqkv_ref[t * AREA : (t + 1) * AREA, 0:512] = (dq * 0.125).astype(BF16)
    for f in range(frames):
        dqkv_ref[f * AREA : (f + 1) * AREA, 512:1024] = (dk[f] * 0.125).astype(BF16)
        dqkv_ref[f * AREA : (f + 1) * AREA, 1024:1536] = dv[f].astype(BF16)
    da = dot_nt(dqkv_ref[...], jnp.concatenate([head_weight(w_ref, j) for j in range(3)], axis=1))
    unit, scale = normalize(x)
    a_ref[...] = (unit * gain + bias).astype(BF16)
    return dx2 + norm_backward(unit, scale, gain, da), row_sums(da * unit), row_sums(da)


def time_backward_kernel(
    place_ref, dx2_ref, x_ref, gain_ref, bias_ref, w_ref, qkv_ref, p_ref, o_ref, dx1_ref, dg_ref, db_ref, *refs
):
    *out_refs, do_ref, dqkv_all, low_all, a_all, o_all, turned_ref, block_ref = refs
    i, count = pl.program_id(0), dqkv_all.shape[0]

    @pl.when(i == 0)
    def _():
        dg_ref[...] = jnp.zeros_like(dg_ref)
        db_ref[...] = jnp.zeros_like(db_ref)

    @pl.when(i < count)
    def _():
        o_all[i] = o_ref[0]
        dx1, dg, db = time_backward_clip(
            dx2_ref[0], x_ref[0], gain_ref[...], bias_ref[...], w_ref, qkv_ref, p_ref,
            dqkv_all.at[i], low_all.at[i], a_all.at[i], do_ref,
        )
        dx1_ref[0] = dx1
        dg_ref[...] += dg
        db_ref[...] += db

    @pl.when(i == count)
    def _():
        attention_products(place_ref, a_all, dqkv_all, low_all, o_all, turned_ref, block_ref, out_refs)


def time_backward(place, dx2, x, gain, bias, w, qkv, p, o, after=()):
    clips, rows, width = x.shape
    sums = [shape((8, width), F32)] * 2 + [shape((4, 4, 64, 512))] * 2
    ins = (place, dx2, x, gain, bias, w, qkv, p, o)
    return run(
        time_backward_kernel, 26, (clips + 1,), ins,
        [SMEM] + clip_specs((dx2, x)) + whole_specs((gain, bias)) + [head_spec(w, 1)] + clip_specs((qkv, p, o)),
        [shape(x.shape, F32)] + sums, [per_clip(x.shape)] + whole_specs(sums),
        [pltpu.VMEM((rows, width), BF16)] + product_scratch(clips, rows, width), after,
    )


def gelu_parts(h):
    e = jnp.exp2(h * h * (-0.5 * math.log2(math.e)) + math.log2(1.0 / math.sqrt(2.0 * math.pi)))
    t = pl.reciprocal(1.0 + (0.3275911 * math.sqrt(0.5)) * jnp.abs(h), approx=True)
    tail = t * (COEFS[0] + t * (COEFS[1] + t * (COEFS[2] + t * (COEFS[3] + t * COEFS[4])))) * e
    cdf = jnp.where(h >= 0, 1.0 - tail, tail)
    return h * cdf, cdf + h * e


def mlp_clip(x, gain, bias, w_ref, c_ref, gb_ref, u_ref, dh_ref, slope_ref, y_ref, send_refs, grad_of, early=False):
    tiles = w_ref.shape[1]
    unit, scale = normalize(x)
    c_ref[...] = (unit * gain + bias).astype(BF16)
    dy = grad_of(None) if early else None
    hidden = [dot(c_ref[...], hidden_weight(w_ref, j, 0)) for j in range(tiles)] if early else None
    for j in range(tiles):
        if early:
            du = dot_nt(gb_ref[...], hidden_weight(w_ref, j, 1))
            active, slope = gelu_parts(hidden[j])
            dh_ref[j] = (du * slope).astype(BF16)
        else:
            active, slope = gelu_parts(dot(c_ref[...], hidden_weight(w_ref, j, 0)))
            slope_ref[j] = slope.astype(BF16)
        u_ref[j] = active.astype(BF16)
    y = x + dot(
        jnp.concatenate([u_ref[j] for j in range(tiles)], axis=1),
        jnp.concatenate([hidden_weight(w_ref, j, 1) for j in range(tiles)], axis=0),
    )
    y_ref[...] = y.astype(BF16)
    write_sends(y_ref[...], send_refs)
    if not early:
        dy = grad_of(y)
        for j in range(tiles):
            du = dot_nt(gb_ref[...], hidden_weight(w_ref, j, 1))
            dh_ref[j] = (du * slope_ref[j].astype(F32)).astype(BF16)
    dc = dot_nt(
        jnp.concatenate([dh_ref[j] for j in range(tiles)], axis=1),
        jnp.concatenate([hidden_weight(w_ref, j, 0) for j in range(tiles)], axis=1),
    )
    return dy + norm_backward(unit, scale, gain, dc), row_sums(dc * unit), row_sums(dc)


def mlp_gen_kernel(parts, place_ref, aspect_ref, x_ref, gain_ref, bias_ref, w_ref, grad_ref, *rest):
    part_refs = rest[:parts]
    y_ref, dx_ref, c_ref, gb_ref, u_ref, dh_ref, dg_ref, db_ref, *send_refs, slope_ref = rest[parts:]
    i = pl.program_id(0)

    @pl.when(i == 0)
    def _():
        dg_ref[...] = jnp.zeros_like(dg_ref)
        db_ref[...] = jnp.zeros_like(db_ref)

    if parts:
        join_parts(window_source(aspect_ref[i], place_ref[0]), grad_ref, part_refs, gb_ref)
    else:
        gb_ref[...] = grad_ref[...]
    dx, dg, db = mlp_clip(
        x_ref[0], gain_ref[...], bias_ref[...], w_ref, c_ref.at[0], gb_ref.at[0], u_ref.at[:, 0], dh_ref.at[:, 0], slope_ref,
        y_ref.at[0], send_refs, lambda y: gb_ref[0].astype(F32), True,
    )
    dx_ref[0] = dx
    dg_ref[...] += dg
    db_ref[...] += db


def tile_block(dims, count):
    return pl.BlockSpec((dims[0], 1) + tuple(dims[2:]), lambda i: (0, jnp.minimum(i, count - 1), 0, 0))


def mlp_gen(direct, place, aspect, x, gain, bias, w, grad, parts=(), after=()):
    total, rows, width = x.shape
    clips, tiles, span = total // 2, w.shape[1], w.shape[3]
    both = [shape(x.shape), shape(x.shape, F32)]
    kept = [shape((clips, rows, width))] * 2
    hidden = [shape((tiles, clips, rows, span))] * 2
    sums = [shape((8, width), F32)] * 2
    sends = send_shapes(kept[0]) if direct else []
    return run(
        partial(mlp_gen_kernel, len(parts)), 20, (clips,), (place, aspect, x, gain, bias, w, grad, *parts),
        [SMEM] * 2 + clip_specs((x,), 0, clips) + whole_specs((gain, bias, w)) + clip_specs((grad, *parts)),
        both + kept + hidden + sums + sends,
        clip_specs(both, 0, clips) + clip_specs(kept) + [tile_block(h.shape, clips) for h in hidden] + whole_specs(sums) + clip_specs(sends),
        [pltpu.VMEM((tiles, rows, span), BF16)], after,
    )


def mlp_disc_kernel(
    sign_ref, count_ref, place_ref, x_ref, gain_ref, bias_ref, w_ref, logit_ref, c_gen, gb_gen, u_gen, dh_gen, dg_gen, db_gen,
    y_ref, dx_ref, out_ref, dg_ref, db_ref, *rest,
):
    send_refs, (slope_ref, c_all, gb_all, u_all, dh_all, turned_ref, block_ref) = rest[:-7], rest[-7:]
    i, (tiles, total, rows, span) = pl.program_id(0), u_all.shape
    count = total // 2

    @pl.when(i == 0)
    def _():
        dg_ref[...] = dg_gen[...]
        db_ref[...] = db_gen[...]

    @pl.when(i < count)
    def _():
        at = count + i
        c_all[i] = c_gen[0]
        gb_all[i] = gb_gen[0]
        u_all[:, i] = u_gen[:, 0]
        dh_all[:, i] = dh_gen[:, 0]

        def grad_of(y):
            sign = sign_ref[i]
            frame = lax.broadcasted_iota(jnp.int32, (rows, 1), 0) // AREA
            live = jnp.where(frame < count_ref[i], -sign, 0.0)
            dy = live * logit_ref[...] * jax.nn.sigmoid(1.0 - sign * logit_ref[...] * y)
            gb_all[at] = dy.astype(BF16)
            return dy

        dx, dg, db = mlp_clip(
            x_ref[0], gain_ref[...], bias_ref[...], w_ref, c_all.at[at], gb_all.at[at], u_all.at[:, at], dh_all.at[:, at],
            slope_ref, y_ref.at[0], send_refs, grad_of,
        )
        dx_ref[0] = dx
        dg_ref[...] += dg
        db_ref[...] += db

    @pl.when(i == count)
    def _():
        turned_ref[0] = c_all[...].reshape(-1, c_all.shape[2]).T
        turned_ref[1] = gb_all[...].reshape(-1, gb_all.shape[2]).T

    @pl.when(i >= count)
    def _():
        at = i - count
        for n, right in enumerate((dh_all, u_all)):
            block_ref[...] = dot(turned_ref[n], right[at].reshape(-1, span))
            for k in range(8):
                out_ref[k, 0, n * 64 : (n + 1) * 64, :] = block_ref[k * 64 : (k + 1) * 64, :].astype(BF16)


def mlp_disc(direct, sign, count, place, x, gain, bias, w, logit, kept, hidden, sums, bases, after=()):
    total, rows, width = x.shape
    clips, tiles, span = total // 2, w.shape[1], w.shape[3]
    outs = [shape(x.shape), shape(x.shape, F32)]
    blocks = shape((8, tiles, 128, span))
    sends = send_shapes(kept[0]) if direct else []
    ins = (sign, count, place, x, gain, bias, w, logit, *kept, *hidden, *sums)
    return run(
        mlp_disc_kernel, 30, (clips + tiles,), ins,
        [SMEM] * 3 + clip_specs((x,), clips, clips) + whole_specs((gain, bias, w, logit)) + clip_specs(kept)
        + [tile_block(h.shape, clips) for h in hidden] + whole_specs(sums),
        outs + [blocks] + [shape(v.shape, F32) for v in sums] + sends,
        clip_specs(outs, clips, clips) + [pl.BlockSpec((8, 1, 128, span), lambda i: (0, jnp.clip(i - clips, 0, tiles - 1), 0, 0))]
        + whole_specs(sums) + clip_specs(sends),
        [
            pltpu.VMEM((tiles, rows, span), BF16),
            pltpu.VMEM((total, rows, width), BF16),
            pltpu.VMEM((total, rows, width), BF16),
            pltpu.VMEM((tiles, total, rows, span), BF16),
            pltpu.VMEM((tiles, total, rows, span), BF16),
            pltpu.VMEM((2, width, total * rows), BF16),
            pltpu.VMEM((width, span), F32),
        ],
        after, bases,
    )


def window_maps(aspect, tokens_frame):
    grid_side = math.isqrt(tokens_frame)
    grid_width = jnp.where(
        aspect == 1, 2 * grid_side, jnp.where(aspect == 2, grid_side // 2, grid_side)
    ).astype(jnp.int32)[:, None]
    across = grid_width // WIN
    places = jnp.arange(tokens_frame, dtype=jnp.int32)[None, :]
    window = places // AREA
    inside = places % AREA
    grid_row = window // across * WIN + inside // WIN
    grid_col = window % across * WIN + inside % WIN
    forward_order = grid_row * grid_width + grid_col
    raster_row = places // grid_width
    raster_col = places % grid_width
    back_order = (
        (raster_row // WIN * across + raster_col // WIN) * AREA + raster_row % WIN * WIN + raster_col % WIN
    )
    return (forward_order, back_order)


def reorder(values, order):
    return jax.vmap(partial(jnp.take, axis=1))(values, order)


def pad_clips(values, split):
    return jnp.pad(values, [(0, -values.shape[0] % split)] + [(0, 0)] * (values.ndim - 1))


def gather_window(x, aspect, split):
    whole_x = pad_clips(lax.all_gather(x, "tensor", axis=2, tiled=True), split)
    aspect = pad_clips(aspect, split)
    t = lax.axis_index("tensor")
    clips = aspect.shape[0] // split
    mine = lax.dynamic_slice_in_dim(whole_x, t % split * clips, clips, 0)
    kinds = lax.dynamic_slice_in_dim(aspect, t % split * clips, clips, 0)
    order, _ = window_maps(kinds, whole_x.shape[2])
    return reorder(mine, lax.dynamic_slice_in_dim(order, t // split * AREA, AREA, 1))


def gather_raster(y, aspect, split, patches):
    every = lax.all_gather(y, "tensor", axis=0)
    count, clips, frames, _, width = every.shape
    every = every.reshape(count // split, split, clips, frames, AREA, width)
    every = jnp.transpose(every, (1, 2, 3, 0, 4, 5)).reshape(split * clips, frames, -1, width)
    _, back = window_maps(aspect, every.shape[2])
    t = lax.axis_index("tensor")
    return reorder(every[: aspect.shape[0]], lax.dynamic_slice_in_dim(back, t * patches, patches, 1))


def attention_piece(d, w_ref, wo_ref):
    rows = w_ref.shape[1] // 8
    part = wo_ref.shape[0] // 8
    qkv = [w_ref[m, pl.ds(pl.multiple_of(d * rows, rows), rows), :] for m in range(3)]
    out = wo_ref[pl.ds(pl.multiple_of(d * part, part), part), :]
    squares = [out[:, c * 128 : (c + 1) * 128] for c in range(out.shape[1] // 128)]
    return jnp.concatenate(qkv + [jnp.concatenate(squares, axis=0)], axis=1)


def pack_weights_kernel(place_ref, sw_ref, swo_ref, tw_ref, two_ref, w_in_ref, w_out_ref, heads_ref, hidden_ref):
    d = place_ref[1]
    heads_ref[0:64, :] = attention_piece(d, sw_ref, swo_ref)
    heads_ref[64:128, :] = attention_piece(d, tw_ref, two_ref)
    rows = pl.ds(pl.multiple_of(d * 64, 64), 64)
    hidden_ref[0:64, :] = w_in_ref[rows, :]
    hidden_ref[64:128, :] = w_out_ref[rows, :]


def pack_weights(place, *weights):
    outs = [shape((128, 512))] * 2
    return run(pack_weights_kernel, 0.01, (1,), (place, *weights), [SMEM] + whole_specs(weights), outs, whole_specs(outs))


def stack_kernel(place_ref, *refs):
    for j in range(4):
        refs[4][place_ref[0] ^ j] = refs[j][...]


def stack_pieces(place, pieces, after=()):
    outs = [shape((4,) + pieces[0].shape)]
    ins = (place, *pieces)
    return run(stack_kernel, 0.01, (1,), ins, [SMEM] + whole_specs(pieces), outs, whole_specs(outs), after=after)[0]


def gather_shard(shard):
    rows = shard.shape[0] // lax.axis_size("dp")
    piece = lax.dynamic_slice_in_dim(shard, lax.axis_index("dp") * rows, rows, 0)
    whole_w = lax.all_gather(piece, ("tensor", "dp"), axis=0, tiled=True)
    return whole_w.reshape((-1,) + shard.shape)


def gather_attention(w, wo):
    width = wo.shape[1]
    heads = gather_shard(w.reshape(-1, w.shape[2])).reshape((-1,) + w.shape)
    heads = jnp.moveaxis(heads, 0, 2).reshape(3, width, 4, -1).transpose(2, 1, 0, 3).reshape(4, width, -1)
    out = gather_shard(wo).reshape(4, width // 4, 4, width // 4).transpose(0, 2, 1, 3).reshape(4, width, -1)
    return jnp.concatenate([heads, out], axis=2)[None]


def gather_hidden(w_in, w_out):
    columns = jnp.moveaxis(gather_shard(w_in), 0, 1).reshape(w_in.shape[0], 4, -1)
    rows = gather_shard(w_out).reshape(4, -1, w_out.shape[1])
    return jnp.concatenate([jnp.moveaxis(columns, 1, 0), rows], axis=1)[None]


def add_kernel(count, *refs):
    operands, outs = refs[:count], refs[count:]
    for i, out in enumerate(outs):
        total = operands[0][i].astype(F32)
        for operand in operands[1:]:
            total = total + operand[i].astype(F32)
        out[...] = total.astype(out.dtype)


def add_blocks(operands, dtype=BF16, after=()):
    outs = [shape(operands[0].shape[1:], dtype)] * operands[0].shape[0]
    return run(
        partial(add_kernel, len(operands)), 0.01, (1,), operands, whole_specs(operands), outs, whole_specs(outs), after=after
    )


def reduce_core(even, odd, after=()):
    return add_blocks([even, swap(odd, "dp", 1)], after=after)


def chips_kernel(*refs):
    ins, out_refs = refs[:8], refs[8:]
    for j, out in enumerate(out_refs):
        at = 0
        for group in (ins[:4], ins[4:]):
            rows = group[0].shape[1]
            out[at : at + rows] = sum(ref[j].astype(F32) for ref in group).astype(BF16)
            at += rows


def chip_parts(near):
    return [near[0]] + [swap(near[i], "dp", 2 * i) for i in (1, 2, 3)]


def reduce_chips(ours, others, after=()):
    outs = [shape((ours[0].shape[1] + others[0].shape[1], ours[0].shape[2]))] * 4
    ins = (*ours, *others)
    return run(chips_kernel, 0.01, (1,), ins, whole_specs(ins), outs, whole_specs(outs), after=after)


def finish_kernel(place_ref, *refs):
    parts, (s_qkv, s_out, t_qkv, t_out, *norms) = refs[:4], refs[4:-1]
    sums_ref = refs[-1]
    total = sum(part[...].astype(F32) for part in parts)
    for block, qkv_ref, out_ref in ((total[0:64], s_qkv, s_out), (total[80:144], t_qkv, t_out)):
        for m in range(3):
            qkv_ref[m] = block[:, m * 128 : (m + 1) * 128]
        out_ref[...] = block[:, 384:512]
    sums_ref[...] = total[64:72]
    d = place_ref[1]
    pair = sums_ref[:, pl.ds(pl.multiple_of(d // 2 * 128, 128), 128)]
    mine = jnp.where(d % 2 == 0, pair[:, 0:64], pair[:, 64:128])
    for n, ref in enumerate(norms):
        ref[...] = mine[n : n + 1]


def finish(place, mine):
    ins = [place, mine[0]] + [swap(mine[j], "tensor", j) for j in (1, 2, 3)]
    outs = [shape((3, 64, 128), F32), shape((64, 128), F32)] * 2 + [shape((1, 64), F32)] * 6
    return run(
        finish_kernel, 0.01, (1,), ins, [SMEM] + whole_specs(ins[1:]), outs, whole_specs(outs), [pltpu.VMEM((8, 512), F32)]
    )


def scatter_grad(grads):
    flat = jnp.concatenate([g.astype(BF16).reshape(g.shape[0], -1) for g in grads], axis=1)
    flat = lax.psum_scatter(flat, "dp", scatter_dimension=0, tiled=True)
    pieces, offset = [], 0
    count = lax.axis_size("tensor")
    for g in grads:
        size = math.prod(g.shape[1:])
        piece = flat[:, offset : offset + size].reshape((flat.shape[0],) + g.shape[1:])
        pieces.append(jnp.moveaxis(piece, 2, 0).reshape(count, flat.shape[0], -1))
        offset += size
    mine = lax.psum_scatter(jnp.concatenate(pieces, axis=2), "tensor", scatter_dimension=0, tiled=True)[0]
    results, offset = [], 0
    for g in grads:
        size = g.shape[1] * g.shape[3]
        results.append(mine[:, offset : offset + size].reshape(-1, g.shape[1], g.shape[3]).astype(F32))
        offset += size
    return results


def in_order(even, odd):
    blocks = jnp.stack([even[:, :, :64], odd[:, :, :64]], axis=1).reshape(8, 4, 64, 4, 128)
    return jnp.transpose(blocks, (0, 2, 3, 1, 4)).reshape(512, 4, 512)


def shards(
    gen_tokens, rec_grad, adv_grad, gen_aspect, gen_frames, disc_tokens, disc_aspect, disc_frames, disc_labels,
    logit_gain, adv_weight, train_step, ln1_gain, ln1_bias, spatial_qkv, spatial_out, ln2_gain, ln2_bias,
    temporal_qkv, temporal_out, ln3_gain, ln3_bias, mlp_in, mlp_out,
):
    tensor = lax.axis_size("tensor")
    dp_at, tensor_at = lax.axis_index("dp"), lax.axis_index("tensor")
    local, frames, patches, width = gen_tokens.shape
    windows = patches * tensor // AREA
    direct = tensor == 4 and windows == 4 and lax.axis_size("dp") == 8
    split = max(tensor // windows, 1)
    clips = -(-local // split)
    place = jnp.stack([tensor_at, dp_at]).astype(jnp.int32)
    vectors = [v.reshape(1, -1) for v in (ln1_gain, ln1_bias, ln2_gain, ln2_bias, ln3_gain, ln3_bias, logit_gain)]
    g1, b1, g2, b2, g3, b3, logit = vectors

    step_value = train_step.astype(F32)
    ramp = adv_weight * step_value / (step_value + HALF)

    def mine(values):
        return lax.dynamic_slice_in_dim(pad_clips(values, split), tensor_at % split * clips, clips, 0)

    count = mine(disc_frames)
    sign = (2 * mine(disc_labels) - 1).astype(F32)
    aspects = (mine(gen_aspect), mine(disc_aspect))

    def flat(x):
        return x.reshape(x.shape[0], -1, width)

    if direct:
        x_gen, x_disc, rec, adv = (flat(v) for v in (gen_tokens, disc_tokens, rec_grad, adv_grad))
        heads, hidden = pack_weights(place, spatial_qkv, spatial_out, temporal_qkv, temporal_out, mlp_in, mlp_out)
        gen_parts = pack(place, gen_aspect, x_gen, (heads,))
        disc_parts = pack(place, disc_aspect, x_disc, gen_parts)
        dy, *dy_parts = pack_grad(place, gen_aspect, gen_frames, ramp, rec, adv, disc_parts)
        heads = [heads] + [swap(heads, "tensor", j) for j in (1, 2, 3)]
        heads = stack_pieces(place, heads, (dy,))
        space_w = time_w = lax.all_gather(heads, "dp", axis=0)
        gen_parts = exchange(gen_parts)
        hidden = [hidden] + [swap(hidden, "tensor", j) for j in (1, 2, 3)]
        hidden = stack_pieces(place, hidden, (heads, *gen_parts))
        mlp_w = lax.all_gather(hidden, "dp", axis=0)
        disc_parts, dy_parts = exchange(disc_parts), exchange(dy_parts)
    else:
        place = jnp.zeros_like(place)
        space_w, time_w = gather_attention(spatial_qkv, spatial_out), gather_attention(temporal_qkv, temporal_out)
        mlp_w = gather_hidden(mlp_in, mlp_out)
        x_gen = flat(gather_window(gen_tokens, gen_aspect, split))
        x_disc = flat(gather_window(disc_tokens, disc_aspect, split))
        live = jnp.arange(frames, dtype=jnp.int32)[None, :] < gen_frames[:, None]
        total = rec_grad.astype(F32) + ramp[0] * adv_grad.astype(F32)
        dy = jnp.where(live[:, :, None, None], total, 0.0).astype(BF16)
        dy = flat(gather_window(dy, gen_aspect, split))
        gen_parts, disc_parts, dy_parts = (), (), ()

    sf = space_forward(place, aspects[0], x_gen, gen_parts, g1, b1, space_w, 2 * clips, (), (hidden,) if direct else ())
    tf = time_forward(sf[0], g2, b2, time_w, clips)
    sf = space_forward(place, aspects[1], x_disc, disc_parts, g1, b1, space_w, 2 * clips, sf, tf[:1])
    x1, s_qkv, s_p, s_o, xw = sf
    x2, t_qkv, t_p, t_o = time_forward(x1, g2, b2, time_w, clips, tf)
    gen = mlp_gen(direct, place, aspects[0], x2, g3, b3, mlp_w, dy, dy_parts)
    y_gen = exchange(gen[8:]) if direct else ()
    y, dx2, ff_blocks, ff_dg, ff_db, *y_sends = mlp_disc(
        direct, sign, count, place, x2, g3, b3, mlp_w, logit, gen[2:4], gen[4:6], gen[6:8], gen[:2]
    )
    y_disc = exchange(y_sends) if direct else ()
    if direct:
        ff_mine = lax.psum_scatter(ff_blocks, "dp", scatter_dimension=0)
    dx1, t_dg, t_db, t_even, t_odd = time_backward(place, dx2, x1, g2, b2, time_w, t_qkv, t_p, t_o, y_gen)
    back = space_backward(direct, dx1, xw, g1, b1, space_w, s_qkv, s_p, (), y_disc)
    kept, (dx0_gen, s_dg, s_db, *gen_sends) = back[:3], back[3:]
    if direct:
        t_near = reduce_core(t_even, t_odd, (dx0_gen,))
        gen_parts = exchange(gen_sends)
        t_parts = chip_parts(t_near)
    back = space_backward(
        direct, dx1, xw, g1, b1, space_w, s_qkv, s_p, kept, (t_near[0],) if direct else ()
    )
    kept, (dx0_disc, d_dg, d_db, *disc_sends) = back[:3], back[3:]
    disc_parts = exchange(disc_sends) if direct else ()
    dqkv, low, a = kept
    zero = jnp.zeros_like(t_dg)
    s_even, s_odd = space_grad(
        place, a, dqkv, low, s_o, (s_dg, d_dg, s_db, d_db, t_dg, zero, t_db, zero, ff_dg, zero, ff_db, zero),
        (dx0_disc, *t_parts) if direct else (),
    )

    part = width // tensor
    if direct:
        ff_share = lax.psum_scatter(ff_mine, "tensor", scatter_dimension=0).astype(F32)
        y_gen = join_raster(place, gen_aspect, y, (y_gen,), 0, 6, (s_even,))
        near = reduce_core(s_even, s_odd, (*gen_parts, *y_gen, *disc_parts[:2]))
        dx_gen = join_raster(place, gen_aspect, dx0_gen, (gen_parts,), 0, JOIN, near[:1])
        y_disc = join_raster(place, disc_aspect, y, (y_disc,), clips, JOIN, near[:1])
        ours = reduce_chips(chip_parts(near), t_parts, (*dx_gen, *y_disc, ff_share))
        dx_disc = join_raster(place, disc_aspect, dx0_disc, (disc_parts,), 0, JOIN, ours[:1])
        s_qkv, s_out, t_qkv, t_out, *small = finish(place, ours)
        shares = (s_qkv, s_out.T, t_qkv, t_out.T)
        small = [n[0] for n in small]
        in_share, out_share = ff_share[:64], ff_share[64:]
        y_gen, y_disc, dx_gen, dx_disc = (v.reshape(gen_tokens.shape) for v in (*y_gen, *y_disc, *dx_gen, *dx_disc))
    else:
        y_gen, y_disc, dx_gen, dx_disc = (
            gather_raster(v.reshape(clips, frames, AREA, width), aspect, split, patches)
            for v, aspect in ((y[:clips], gen_aspect), (y[clips:], disc_aspect), (dx0_gen, gen_aspect), (dx0_disc, disc_aspect))
        )
        ff = jnp.transpose(ff_blocks.reshape(8, 4, 2, 64, 512), (0, 3, 2, 1, 4)).reshape(width, 2, tensor, -1)
        ff_share = scatter_grad([ff])[0]
        in_share, out_share = ff_share[:, 0], ff_share[:, 1]
        shares = []
        for even, odd in ((s_even, s_odd), (t_even, t_odd)):
            block = scatter_grad([in_order(even, odd).reshape(width, 4, tensor, part)])[0]
            shares += [jnp.moveaxis(block[:, :3], 1, 0), block[:, 3].T]
        small = lax.psum(s_even[0, 0, 64:70].astype(F32), ("dp", "tensor"))
        piece = width // lax.axis_size("dp")
        small = lax.dynamic_slice_in_dim(small, dp_at * piece, piece, 1)

    return (
        y_gen, dx_gen, y_disc, dx_disc,
        small[0], small[1], shares[0], shares[1], small[2], small[3], shares[2], shares[3],
        small[4], small[5], in_share, out_share.T,
    )


def solution(mesh):
    tokens = P("dp", None, "tensor", None)
    vector, clip = P(), P("dp")
    qkv, rows, cols = P(None, None, "tensor"), P("tensor", None), P(None, "tensor")
    in_specs = (
        (tokens,) * 3 + (clip,) * 2 + (tokens,) + (clip,) * 3 + (vector,) * 5
        + (qkv, rows, vector, vector, qkv, rows, vector, vector, cols, rows)
    )
    block = (clip, clip, P(None, "dp", "tensor"), P("tensor", "dp"))
    out_specs = (tokens,) * 4 + block * 2 + (clip, clip, P("dp", "tensor"), P("tensor", "dp"))
    return jax.shard_map(shards, mesh=mesh, in_specs=in_specs, out_specs=out_specs, check_vma=False)
```
